32 devices in a mesh: rep: 2 (over core), section: 2 (over y), exp: 8 (over z, x).
Axes of the slice: x: 2, y: 2, z: 4, core: 2. Of those that a mesh axis runs over, the one named last changes fastest.
Arguments:
- row_codes: bfloat16 [2, 1024, 2048], P('section', ('rep', 'exp')), may hold values from -448 to 448
- block_exponents: int32 [2, 1024, 16], P('section', ('rep', 'exp')), may hold values from -10 to -6
- routes: int32 [2, 1024, 8], P('section', ('rep', 'exp')), may hold values from 0 to 15, all different within a row; in each aligned block of 64 rows (0 to 63, 64 to 127, ..., all dimensions but the last counted through in order) at most 48 rows name the same one
- route_weight: float32 [2, 1024, 8], P('section', ('rep', 'exp')), may hold values from 0.02 to 0.3
- out_grad: bfloat16 [2, 1024, 2048], P('section', ('rep', 'exp')), may hold values from -6 to 6
- gate_weight: bfloat16 [2, 16, 384, 2048], P('section', 'exp', 'rep'), may hold values from -0.125 to 0.125
- up_weight: bfloat16 [2, 16, 384, 2048], P('section', 'exp', 'rep'), may hold values from -0.125 to 0.125
- down_weight: bfloat16 [2, 16, 384, 2048], P('section', 'exp', 'rep'), may hold values from -0.3125 to 0.3125
Outputs:
- next_rows: bfloat16 [2, 1024, 2048], P('section', ('rep', 'exp'))
- prev_grads: bfloat16 [2, 1024, 2048], P('section', ('rep', 'exp'))
- gate_weight_grad: bfloat16 [2, 16, 384, 2048], P('section', 'exp', 'rep')
- up_weight_grad: bfloat16 [2, 16, 384, 2048], P('section', 'exp', 'rep')
- down_weight_grad: bfloat16 [2, 16, 384, 2048], P('section', 'exp', 'rep')
The draws below stay inside these ranges and needn't reach their ends.
Inputs may be any that keep to these rules, and one draw needn't show every extreme that they name: `routes`: the 8 experts of a token differ. In the 64 rows of one device of a layer no expert is named by more than 48 rows, a bound that some of them reach.
All inputs are finite; a program needn't handle non-finite values.
Results may differ from the reference program's by a relative error of at most 0.0065.
Values may be sent and summed in bfloat16 or wider, within the bound.
No kernel may reach another device: no remote copies, remote signals or barrier semaphores. Data moves between devices by JAX's collectives and lax.ppermute only.
A program may use at most 128 MiB of HBM per device.

```python
import math
import jax
import jax.numpy as jnp
import numpy as np
from jax import lax

D = 2048
FF = 384
TOPK = 8
TOK_DEV = 64
SECTIONS = 2
EXPERTS = 16
TOKENS = 1024
NB = 16
CAP = 48
N_REP = 2
N_EXP = 8


def set_ends(result, key, least, top_value):
    longest = result.shape.index(max(result.shape))
    spots = []
    for shift in (0, 1):
        where = [jax.random.randint(jax.random.fold_in(key, axis), (), 0, length) for axis, length in enumerate(result.shape)]
        where[longest] = (where[longest] + shift) % result.shape[longest]
        spots.append(tuple(where))
    return result.at[spots[0]].set(least).at[spots[1]].set(top_value)


def level_of(key, extent, shards, smallest, top_value):
    factor_of, own = 1.0, jax.random.fold_in(key, 6)
    for position, blocks in shards:
        steps = jnp.exp(jax.random.uniform(jax.random.fold_in(own, position), (blocks,), jnp.float32, smallest / len(shards), top_value / len(shards)))
        factor_of = factor_of * jnp.repeat(steps, extent[position] // blocks).reshape([-1 if axis == position else 1 for axis in range(len(extent))])
    return factor_of


def routed_block(own_key, own, number, rows, amount, top, most, slope):
    ranking = jax.random.permutation(own_key, amount)
    packed, ordinary = shares(amount, rows * top, most, slope, True), shares(amount, rows * top, most, slope, False)
    places = jnp.arange(amount)

    def named(lengths, offset_by):
        used = int((lengths > 0).sum())
        fixed = max(1, used // 4)
        moved = fixed + (places - fixed + offset_by * (used - fixed)) % max(1, amount - fixed)
        return jnp.zeros((amount,), jnp.int32).at[ranking[jnp.where(places < fixed, places, moved)]].set(jnp.asarray(lengths, jnp.int32))

    lengths = jnp.where(number % 4 == 0, named(packed, number // 4), named(ordinary, number - number // 4 - 1))
    mixed = jax.random.permutation(jax.random.fold_in(own, 3), amount)
    giver, sink = mixed[0:amount // 2 * 2:2], mixed[1:amount // 2 * 2:2]
    room = jnp.minimum(lengths[giver] - 1, most - lengths[sink]) // 2
    room = jnp.where((giver == ranking[0]) | (sink == ranking[0]) | (lengths[sink] == 0), 0, jnp.maximum(room, 0))
    moved = jax.random.randint(jax.random.fold_in(own, 4), (amount // 2,), 0, 1 << 20) % (room + 1)
    lengths = lengths.at[giver].add(-moved).at[sink].add(moved)
    labels = jnp.searchsorted(jnp.cumsum(lengths), jnp.arange(rows * top), side="right").astype(jnp.int32)
    table = labels.reshape(top, rows).T
    table = table[jax.random.permutation(jax.random.fold_in(own, 1), rows)]
    offset_by = jax.random.randint(jax.random.fold_in(own, 2), (rows, 1), 0, top)
    return jnp.take_along_axis(table, (jnp.arange(top)[None, :] + offset_by) % top, axis=1)


def shares(amount, total, most, skew, full):
    portions = [(1 << 20) // math.isqrt(grade ** skew) + 1 for grade in range(1, amount + 1)]
    largest = most if full else min(most, max(-(-total // amount), total * portions[0] // sum(portions)))
    least = 1 if total - largest >= amount - 1 else 0
    given, surplus = [largest] + [least] * (amount - 1), total - largest - least * (amount - 1)
    while surplus > 0:
        movable = [i for i in range(1, amount) if given[i] < largest] or [i for i in range(1, amount) if given[i] < most]
        mass, budget = sum([portions[i] for i in movable]), surplus
        for i in movable:
            more = min(most - given[i], max(1, budget * portions[i] // mass), surplus)
            given[i] = given[i] + more
            surplus = surplus - more
    return np.array(given)


def noise(stream_key, extent, spread, most, cuts=(), kind=jnp.bfloat16):
    array = jax.random.normal(stream_key, extent, jnp.float32) * spread
    if len(cuts) > 0:
        array = level_of(stream_key, extent, cuts, -0.22, 0.18) * array
    return jnp.clip(array, min=-most, max=most).astype(kind)


def setup_inputs(seed: int = 0) -> dict:
    arg_keys = jax.random.split(jax.random.key(seed), 9)
    row_codes = noise(arg_keys[0], (SECTIONS, TOKENS, D), 96.0, 448.0, ((0, 2), (1, 16)))
    block_exponents = set_ends(jax.random.randint(arg_keys[1], (SECTIONS, TOKENS, NB), -10, -5), jax.random.fold_in(arg_keys[1], 1), -10, (-5) - 1).astype(jnp.int32)
    routes_keys = jax.random.split(jax.random.fold_in(arg_keys[2], 1), SECTIONS * TOKENS // TOK_DEV)
    routes_turns = jax.random.permutation(jax.random.fold_in(arg_keys[2], 3), SECTIONS * TOKENS // TOK_DEV)
    routes = jax.vmap(lambda own, number: routed_block(jax.random.fold_in(arg_keys[2], 2), own, number, TOK_DEV, EXPERTS, TOPK, CAP, 2))(routes_keys, routes_turns).reshape((SECTIONS, TOKENS, TOPK))
    route_weight = jnp.clip(jnp.exp(math.log(0.3) - 2.7080503 * jax.random.uniform(arg_keys[3], (SECTIONS, TOKENS, TOPK), jnp.float32) ** level_of(arg_keys[3], (SECTIONS, TOKENS, TOPK), ((0, 2), (1, 16)), -0.2, 0.2)), 0.02, 0.3)
    out_grad = noise(arg_keys[4], (SECTIONS, TOKENS, D), 1.0, 6.0, ((0, 2), (1, 16)))
    gate_weight = noise(arg_keys[5], (SECTIONS, EXPERTS, FF, D), D ** -0.5, 0.125, ((0, 2), (1, 8), (2, 2)))
    up_weight = noise(arg_keys[6], (SECTIONS, EXPERTS, FF, D), D ** -0.5, 0.125, ((0, 2), (1, 8), (2, 2)))
    down_weight = noise(arg_keys[7], (SECTIONS, EXPERTS, FF, D), FF ** -0.5, 0.3125, ((0, 2), (1, 8), (2, 2)))
    return {"row_codes": row_codes, "block_exponents": block_exponents, "routes": routes, "route_weight": route_weight, "out_grad": out_grad, "gate_weight": gate_weight, "up_weight": up_weight, "down_weight": down_weight}


def dequantize(code_rows, exponent_rows):
    row_count = code_rows.shape[0]
    row_width = code_rows.shape[1]
    blocks = code_rows.astype(jnp.float32).reshape(row_count, row_width // 128, 128)
    scales = jnp.exp2(exponent_rows.astype(jnp.float32))[:, :, None]
    return (blocks * scales).reshape(row_count, row_width).astype(jnp.bfloat16)


def expert_pass(expert_rows, gated_grad, gate_rows, up_rows, down_rows):
    gate_act = jnp.dot(expert_rows, gate_rows.T, preferred_element_type=jnp.float32)
    up_act = jnp.dot(expert_rows, up_rows.T, preferred_element_type=jnp.float32)
    sigmoid_gate = jax.nn.sigmoid(gate_act)
    swish = gate_act * sigmoid_gate
    hidden = (swish * up_act).astype(jnp.bfloat16)
    output = jnp.dot(hidden, down_rows, preferred_element_type=jnp.float32).astype(jnp.bfloat16)
    hidden_grad = jnp.dot(gated_grad, down_rows.T, preferred_element_type=jnp.float32)
    gate_grad = (hidden_grad * up_act * sigmoid_gate * (1.0 + gate_act * (1.0 - sigmoid_gate))).astype(jnp.bfloat16)
    up_grad = (hidden_grad * swish).astype(jnp.bfloat16)
    input_grad = (jnp.dot(gate_grad, gate_rows, preferred_element_type=jnp.float32)
                  + jnp.dot(up_grad, up_rows, preferred_element_type=jnp.float32)).astype(jnp.bfloat16)
    gate_total = jnp.dot(gate_grad.T, expert_rows, preferred_element_type=jnp.float32)
    up_total = jnp.dot(up_grad.T, expert_rows, preferred_element_type=jnp.float32)
    down_total = jnp.dot(hidden.T, gated_grad, preferred_element_type=jnp.float32)
    return output, input_grad, gate_total, up_total, down_total


def replica_layer(section_index, first_row, replica_tokens, row_codes, block_exponents, routes,
                  route_weight, out_grad, gate_weight, up_weight, down_weight):
    assigns = replica_tokens * TOPK
    most_rows = N_EXP * CAP
    last_row = first_row + replica_tokens
    inputs = dequantize(row_codes[section_index, first_row:last_row], block_exponents[section_index, first_row:last_row])
    flat_ids = routes[section_index, first_row:last_row].reshape(-1)
    weights_here = route_weight[section_index, first_row:last_row]
    grad_here = out_grad[section_index, first_row:last_row]
    gated_all = (weights_here[:, :, None] * grad_here[:, None, :].astype(jnp.float32)).astype(jnp.bfloat16)
    gated_all = gated_all.reshape(assigns, D)
    zero_value = jnp.zeros((), jnp.bfloat16)

    def one_expert(expert_id):
        positions = jnp.nonzero(flat_ids == expert_id, size=most_rows, fill_value=assigns)[0].astype(jnp.int32)
        present = positions < assigns
        clipped = jnp.minimum(positions, assigns - 1)
        expert_rows = jnp.where(present[:, None], inputs[clipped // TOPK], zero_value)
        gated_grad = jnp.where(present[:, None], gated_all[clipped], zero_value)
        results = expert_pass(expert_rows, gated_grad, gate_weight[section_index, expert_id],
                              up_weight[section_index, expert_id], down_weight[section_index, expert_id])
        return (positions, results[0], results[1], results[2].astype(jnp.bfloat16),
                results[3].astype(jnp.bfloat16), results[4].astype(jnp.bfloat16))

    mapped = lax.map(one_expert, jnp.arange(EXPERTS, dtype=jnp.int32))
    positions = mapped[0].reshape(-1)
    expert_out = jnp.zeros((assigns + 1, D), jnp.float32).at[positions].set(
        mapped[1].reshape(-1, D).astype(jnp.float32))[:assigns]
    expert_back = jnp.zeros((assigns + 1, D), jnp.float32).at[positions].set(
        mapped[2].reshape(-1, D).astype(jnp.float32))[:assigns]
    layer_out = (inputs.astype(jnp.float32)
                 + jnp.sum(weights_here[:, :, None] * expert_out.reshape(replica_tokens, TOPK, D), axis=1)).astype(jnp.bfloat16)
    layer_back = (grad_here.astype(jnp.float32)
                  + jnp.sum(expert_back.reshape(replica_tokens, TOPK, D), axis=1)).astype(jnp.bfloat16)
    return layer_out, layer_back, mapped[3], mapped[4], mapped[5]


def reference(row_codes, block_exponents, routes, route_weight, out_grad, gate_weight, up_weight, down_weight):
    replica_tokens = TOKENS // N_REP
    forward_list = []
    backward_list = []
    gate_list = []
    up_list = []
    down_list = []
    for section_index in range(SECTIONS):
        out_parts = []
        back_parts = []
        gate_sum = jnp.zeros((EXPERTS, FF, D), jnp.float32)
        up_sum = jnp.zeros((EXPERTS, FF, D), jnp.float32)
        down_sum = jnp.zeros((EXPERTS, FF, D), jnp.float32)
        for replica in range(N_REP):
            results = replica_layer(section_index, replica * replica_tokens, replica_tokens, row_codes,
                                    block_exponents, routes, route_weight, out_grad, gate_weight,
                                    up_weight, down_weight)
            out_parts.append(results[0])
            back_parts.append(results[1])
            gate_sum = gate_sum + results[2].astype(jnp.float32)
            up_sum = up_sum + results[3].astype(jnp.float32)
            down_sum = down_sum + results[4].astype(jnp.float32)
        forward_list.append(jnp.concatenate(out_parts, axis=0))
        backward_list.append(jnp.concatenate(back_parts, axis=0))
        gate_list.append(gate_sum.astype(jnp.bfloat16))
        up_list.append(up_sum.astype(jnp.bfloat16))
        down_list.append(down_sum.astype(jnp.bfloat16))
    next_rows = jnp.roll(jnp.stack(forward_list), 1, axis=0)
    prev_grads = jnp.roll(jnp.stack(backward_list), -1, axis=0)
    return (next_rows, prev_grads, jnp.stack(gate_list), jnp.stack(up_list), jnp.stack(down_list))
```

```python
import jax
import jax.numpy as jnp
from jax import lax
from jax.sharding import PartitionSpec as P


def from_behind(value, axis, by):
    peers = lax.axis_size(axis)
    return lax.ppermute(value, axis, [(i, (i + by) % peers) for i in range(peers)])


def dequantize(code_rows, exponent_rows):
    scales = jnp.exp2(exponent_rows.astype(jnp.float32))
    scales = jnp.repeat(scales, code_rows.shape[-1] // exponent_rows.shape[-1], axis=-1)
    return (code_rows.astype(jnp.float32) * scales).astype(jnp.bfloat16)


def dot(a, b, dims):
    return lax.dot_general(a, b, (dims, ((), ())), preferred_element_type=jnp.float32)


def shards(
    row_codes, block_exponents, routes, route_weight, out_grad, gate_weight, up_weight, down_weight
):
    token_count, model_width = row_codes.shape[1:]
    local_experts, half_units = gate_weight.shape[1:3]
    units = half_units * lax.axis_size("rep")
    experts = lax.axis_size("exp") * local_experts
    home_rows = dequantize(row_codes[0], block_exponents[0])
    table = jnp.sum(
        jnp.where(
            routes[0][:, :, None] == jnp.arange(experts, dtype=jnp.int32)[None, None, :],
            route_weight[0][:, :, None],
            0.0,
        ),
        axis=1,
    )
    rows = lax.all_gather(home_rows, "exp", axis=0, tiled=True)
    all_tables = lax.all_gather(table, "exp", axis=0, tiled=True)
    weights = [
        lax.all_gather(w[0], "rep", axis=1, tiled=True).reshape(local_experts * units, model_width)
        for w in (gate_weight, up_weight, down_weight)
    ]
    gate_full, up_full, down_full = weights
    grads = lax.all_gather(out_grad[0], "exp", axis=0, tiled=True)
    mine = lax.dynamic_slice_in_dim(
        all_tables, lax.axis_index("exp") * local_experts, local_experts, axis=1
    )
    scale = jnp.repeat(mine, units, axis=1)
    last, first = ((1,), (1,)), ((0,), (0,))
    gate_act = dot(rows, gate_full, last)
    up_act = dot(rows, up_full, last)
    sigmoid_gate = jax.nn.sigmoid(gate_act)
    swish = gate_act * sigmoid_gate
    hidden = (swish * up_act * scale).astype(jnp.bfloat16)
    output = dot(hidden, down_full, ((1,), (0,))).astype(jnp.bfloat16)
    output_sum = lax.psum_scatter(output, "exp", scatter_dimension=0, tiled=True)
    hidden_grad = dot(grads, down_full, last) * scale
    gate_grad = (
        hidden_grad * up_act * sigmoid_gate * (1.0 + gate_act * (1.0 - sigmoid_gate))
    ).astype(jnp.bfloat16)
    up_grad = (hidden_grad * swish).astype(jnp.bfloat16)
    input_grad = (
        dot(gate_grad, gate_full, ((1,), (0,))) + dot(up_grad, up_full, ((1,), (0,)))
    ).astype(jnp.bfloat16)
    input_sum = lax.psum_scatter(input_grad, "exp", scatter_dimension=0, tiled=True)
    shape = (1, local_experts, units, model_width)
    totals = [
        lax.psum_scatter(
            dot(a, b, first).astype(jnp.bfloat16).reshape(shape),
            "rep",
            scatter_dimension=2,
            tiled=True,
        )
        for a, b in ((gate_grad, rows), (up_grad, rows), (hidden, grads))
    ]
    layer_out = (home_rows.astype(jnp.float32) + output_sum.astype(jnp.float32)).astype(jnp.bfloat16)
    layer_back = (out_grad[0].astype(jnp.float32) + input_sum.astype(jnp.float32)).astype(
        jnp.bfloat16
    )
    next_rows = from_behind(layer_out[None], "section", 1)
    prev_grads = from_behind(layer_back[None], "section", -1)
    return (next_rows, prev_grads, totals[0], totals[1], totals[2])


def solution(mesh):
    tokens = P("section", ("rep", "exp"), None)
    weights = P("section", "exp", "rep", None)
    return jax.shard_map(
        shards,
        mesh=mesh,
        in_specs=(tokens,) * 5 + (weights,) * 3,
        out_specs=(tokens,) * 2 + (weights,) * 3,
        check_vma=False,
    )
```

```python
import functools
import jax
import jax.numpy as jnp
from jax import lax
from jax.experimental import pallas as pl
from jax.experimental.pallas import tpu as pltpu
from jax.sharding import PartitionSpec as P

F32 = jnp.float32
BF16 = jnp.bfloat16
VMEM_BYTES = 40 * 2**20


def ring_order(peers):
    width = 1
    while 8 * width * width <= peers:
        width *= 2
    depth = peers // width
    if width == 1 or depth % 2:
        return list(range(peers))
    order = [z * width for z in range(depth)]
    for back, z in enumerate(reversed(range(depth))):
        columns = list(range(1, width))
        order += [z * width + x for x in (columns if back % 2 == 0 else reversed(columns))]
    return order


def ring_shift(value, by):
    peers = lax.axis_size("exp")
    order = ring_order(peers)
    pairs = []
    for rep in range(lax.axis_size("rep")):
        step = by if rep % 2 == 0 else -by
        for spot in range(peers):
            pairs.append((rep * peers + order[spot], rep * peers + order[(spot + step) % peers]))
    return lax.ppermute(value, ("rep", "exp"), pairs)


def from_behind(value, axis, by):
    peers = lax.axis_size(axis)
    return lax.ppermute(value, axis, [(i, (i + by) % peers) for i in range(peers)])


def dot(a, b, dims):
    return lax.dot_general(a, b, (dims, ((), ())), preferred_element_type=F32)


def whole():
    return pl.BlockSpec(memory_space=pltpu.VMEM)


def turned(value):
    rows, columns = value.shape
    wide = jnp.concatenate([value, jnp.zeros((rows, 128 - columns), F32)], axis=1)
    return wide.T[:columns]


def pack_kernel(experts, codes_ref, exps_ref, routes_ref, weight_ref, grad_ref, out_ref):
    tokens, width = codes_ref.shape
    blocks = exps_ref.shape[0]
    scales = jnp.exp2(exps_ref[...].astype(F32))
    scales = turned(jnp.concatenate([scales, jnp.zeros((128 - blocks, tokens), F32)], axis=0))
    per = width // blocks
    for b in range(blocks):
        cols = slice(b * per, (b + 1) * per)
        out_ref[:, cols] = (codes_ref[:, cols].astype(F32) * scales[:, b : b + 1]).astype(BF16)
    out_ref[:, width : 2 * width] = grad_ref[...]
    expert = lax.broadcasted_iota(jnp.int32, (experts, tokens), 0)
    table = jnp.zeros((experts, tokens), F32)
    for k in range(routes_ref.shape[0]):
        table += jnp.where(routes_ref[k : k + 1, :] == expert, weight_ref[k : k + 1, :], 0.0)
    high = table.astype(BF16).astype(F32)
    middle = (table - high).astype(BF16).astype(F32)
    low = table - high - middle
    extra = out_ref.shape[1] - 2 * width
    parts = [high, middle, low]
    if extra > 3 * experts:
        parts.append(jnp.zeros((extra - 3 * experts, tokens), F32))
    out_ref[:, 2 * width :] = turned(jnp.concatenate(parts, axis=0)).astype(BF16)


def expert_kernel(count, experts, local_experts, width, first_ref, *refs):
    blocks = refs[:count]
    weights = refs[count : count + 6]
    outs = refs[count + 6 : 2 * count + 6]
    gate_out, up_out, hidden_out, buffer, rows, sems = refs[2 * count + 6 :]
    half = weights[0].shape[0]
    units = 2 * half
    copies = []
    for i in range(6):
        kind, side = divmod(i, 2)
        copies.append(
            pltpu.make_async_copy(
                weights[side * 3 + kind], buffer.at[kind, pl.ds(side * half, half)], sems.at[i]
            )
        )
    for copy in copies:
        copy.start()
    tokens = blocks[0].shape[0]
    lanes = blocks[0].shape[1] - 2 * width
    scales = []
    lane = lax.broadcasted_iota(jnp.int32, (tokens, lanes), 1)
    expert_of = lax.rem(lane, experts)
    for i, block in enumerate(blocks):
        rows[0, i * tokens : (i + 1) * tokens, :] = block[:, :width]
        rows[1, i * tokens : (i + 1) * tokens, :] = block[:, width : 2 * width]
        table = block[:, 2 * width :].astype(F32)
        scales.append(
            [
                jnp.sum(
                    jnp.where(expert_of == first_ref[0] + e, table, 0.0), axis=1, keepdims=True
                )
                for e in range(local_experts)
            ]
        )
    scales = [
        jnp.concatenate([s[e] for s in scales], axis=0) for e in range(local_experts)
    ]
    for copy in copies:
        copy.wait()
    tile = 256
    last = ((1,), (1,))
    plain = ((1,), (0,))

    def hidden_tile(j, carry):
        at = pl.ds(pl.multiple_of(j * tile, tile), tile)
        gate = dot(rows[0], buffer[0, at, :], last)
        up = dot(rows[0], buffer[1, at, :], last)
        back = dot(rows[1], buffer[2, at, :], last)
        unit = lax.rem(j * tile + lax.broadcasted_iota(jnp.int32, (1, tile), 1), half)
        scale = jnp.broadcast_to(scales[0], gate.shape)
        for e in range(1, local_experts):
            scale = jnp.where(unit >= e * (half // local_experts), scales[e], scale)
        sig = 1.0 / (1.0 + jnp.exp(-gate))
        swish = gate * sig
        back = back * scale
        hidden_out[:, at] = (swish * up * scale).astype(BF16)
        gate_out[:, at] = (back * up * sig * (1.0 + gate * (1.0 - sig))).astype(BF16)
        up_out[:, at] = (back * swish).astype(BF16)
        return carry

    lax.fori_loop(0, units // tile, hidden_tile, 0)

    def column_tile(n, carry):
        at = pl.ds(pl.multiple_of(n * tile, tile), tile)
        later = pl.ds(pl.multiple_of(width + n * tile, tile), tile)
        output = dot(hidden_out[...], buffer[2, :, at], plain).astype(BF16)
        grad = (
            dot(gate_out[...], buffer[0, :, at], plain) + dot(up_out[...], buffer[1, :, at], plain)
        ).astype(BF16)
        for i, out in enumerate(outs):
            out[:, at] = output[i * tokens : (i + 1) * tokens]
            out[:, later] = grad[i * tokens : (i + 1) * tokens]
        return carry

    lax.fori_loop(0, width // tile, column_tile, 0)


def expert_call(blocks, weights, first, experts, local_experts, width):
    count = len(blocks)
    tokens = blocks[0].shape[0]
    half = weights[0].shape[0]
    rows = count * tokens
    saved = jax.ShapeDtypeStruct((rows, 2 * half), BF16)
    results = pl.pallas_call(
        functools.partial(expert_kernel, count, experts, local_experts, width),
        out_shape=[jax.ShapeDtypeStruct((tokens, 2 * width), BF16)] * count + [saved] * 3,
        in_specs=[pl.BlockSpec(memory_space=pltpu.SMEM)]
        + [whole()] * count
        + [pl.BlockSpec(memory_space=pl.ANY)] * 6,
        out_specs=[whole()] * (count + 3),
        scratch_shapes=[
            pltpu.VMEM((3, 2 * half, width), BF16),
            pltpu.VMEM((2, rows, width), BF16),
            pltpu.SemaphoreType.DMA((6,)),
        ],
        compiler_params=pltpu.CompilerParams(vmem_limit_bytes=VMEM_BYTES),
        cost_estimate=pl.CostEstimate(
            flops=6 * 2 * rows * 2 * half * width,
            bytes_accessed=12 * half * width + 8 * rows * width,
            transcendentals=rows * 2 * half,
        ),
        name="expert_rows",
    )(first, *blocks, *weights)
    return results[:count], results[count:]


def weight_kernel(groups, count, has_received, *refs):
    rows = refs[:count]
    grads = refs[count : 2 * count]
    refs = refs[2 * count :]
    saved = [refs[g * 3 : g * 3 + 3] for g in range(groups)]
    refs = refs[groups * 3 :]
    received = refs[:3] if has_received else None
    outs = refs[-4:-1]
    across = refs[-1]

    @pl.when(pl.program_id(0) == 0)
    def _():
        for kind in range(3):
            start = 0
            for group in saved:
                size = group[kind].shape[0]
                across[kind, :, start : start + size] = group[kind][...].T
                start += size

    right = [
        jnp.concatenate([r[...] for r in rows], axis=0),
        jnp.concatenate([r[...] for r in grads], axis=0),
    ]
    for kind in range(3):
        total = dot(across[kind], right[kind // 2], ((1,), (0,)))
        if has_received:
            total = total + received[kind][...].astype(F32)
        outs[kind][...] = total.astype(BF16)


def weight_call(blocks, saved, side, received, width):
    tokens = blocks[0].shape[0]
    count = len(blocks)
    half = saved[0][0].shape[1] // 2
    tile = 256
    steps = width // tile
    block = lambda offset: pl.BlockSpec((tokens, tile), lambda n: (0, n + offset))
    column = pl.BlockSpec((half, tile), lambda n: (0, n))
    total = tokens * count
    specs = [block(0)] * count + [block(steps)] * count
    args = list(blocks) * 2
    for group in saved:
        specs += [pl.BlockSpec((g.shape[0], half), lambda n: (0, side)) for g in group]
        args += list(group)
    if received is not None:
        specs += [column] * 3
        args += list(received)
    return pl.pallas_call(
        functools.partial(weight_kernel, len(saved), count, received is not None),
        grid=(steps,),
        out_shape=[jax.ShapeDtypeStruct((half, width), BF16)] * 3,
        in_specs=specs,
        out_specs=[column] * 3,
        scratch_shapes=[pltpu.VMEM((3, half, total), BF16)],
        compiler_params=pltpu.CompilerParams(vmem_limit_bytes=VMEM_BYTES),
        cost_estimate=pl.CostEstimate(
            flops=3 * 2 * total * half * width,
            bytes_accessed=4 * total * width + 12 * half * width,
            transcendentals=0,
        ),
        name="weight_grads",
    )(*args)


def add(a, b):
    return (a.astype(F32) + b.astype(F32)).astype(BF16)


def shards(
    row_codes, block_exponents, routes, route_weight, out_grad, gate_weight, up_weight, down_weight
):
    tokens, width = row_codes.shape[1:]
    local_experts, half_units = gate_weight.shape[1:3]
    half = local_experts * half_units
    peers = lax.axis_size("exp")
    experts = peers * local_experts
    lanes = -(-3 * experts // 128) * 128
    own = [w.reshape(half, width) for w in (gate_weight, up_weight, down_weight)]
    other = [from_behind(w, "rep", 1) for w in own]
    weights = own + other
    first = (lax.axis_index("exp") * local_experts).astype(jnp.int32).reshape(1)
    home = pl.pallas_call(
        functools.partial(pack_kernel, experts),
        out_shape=jax.ShapeDtypeStruct((tokens, 2 * width + lanes), BF16),
        in_specs=[whole()] * 5,
        out_specs=whole(),
        name="pack_rows",
    )(row_codes[0], block_exponents[0].T, routes[0].T, route_weight[0].T, out_grad[0])

    ahead, behind = peers // 2, peers // 2 - 1
    near, far = [home], [home]
    arrived = [("home", 0, home)]
    for k in range(1, ahead + 1):
        near.append(ring_shift(near[-1], 1))
        arrived.append(("near", k, near[k]))
        if k <= behind:
            far.append(ring_shift(far[-1], -1))
            arrived.append(("far", k, far[k]))
    groups = [arrived[i : i + 4] for i in range(0, len(arrived) - 1, 4)]
    if len(groups[-1]) > 1 and groups[-1][-1] is arrived[-1]:
        groups[-1] = groups[-1][:-1]
    groups.append(arrived[-1:])
    partial, saved = {}, []
    for group in groups:
        outs, kept = expert_call(
            [g[2] for g in group], weights, first, experts, local_experts, width
        )
        saved.append(kept)
        for (name, k, _), out in zip(group, outs):
            partial[name, k] = out

    blocks = [g[2] for group in groups for g in group]
    given = weight_call(blocks, saved, 1, None, width)
    received = [from_behind(g, "rep", 1) for g in given]

    near_sum, far_sum = partial["near", ahead], partial["far", behind] if behind else None
    for k in range(ahead, 0, -1):
        near_sum = ring_shift(near_sum, -1)
        if k > 1:
            near_sum = add(near_sum, partial["near", k - 1])
        if k <= behind:
            far_sum = ring_shift(far_sum, 1)
            if k > 1:
                far_sum = add(far_sum, partial["far", k - 1])
    total = home[:, : 2 * width].astype(F32) + partial["home", 0].astype(F32)
    total = total + near_sum.astype(F32)
    if behind:
        total = total + far_sum.astype(F32)
    total = total.astype(BF16)
    next_rows = from_behind(total[None, :, :width], "section", 1)
    prev_grads = from_behind(total[None, :, width:], "section", -1)
    totals = weight_call(blocks, saved, 0, received, width)
    shape = (1, local_experts, half_units, width)
    return (next_rows, prev_grads) + tuple(t.reshape(shape) for t in totals)


def solution(mesh):
    tokens = P("section", ("rep", "exp"), None)
    weights = P("section", "exp", "rep", None)
    return jax.shard_map(
        shards,
        mesh=mesh,
        in_specs=(tokens,) * 5 + (weights,) * 3,
        out_specs=(tokens,) * 2 + (weights,) * 3,
        check_vma=False,
    )
```

```python
import functools
import jax
import jax.numpy as jnp
from jax import lax
from jax.experimental import pallas as pl
from jax.experimental.pallas import tpu as pltpu
from jax.sharding import PartitionSpec as P

F32 = jnp.float32
BF16 = jnp.bfloat16
VMEM_BYTES = 60 * 2**20


def ring_order(peers):
    width = 1
    while 8 * width * width <= peers:
        width *= 2
    depth = peers // width
    if width == 1 or depth % 2:
        return list(range(peers))
    order = [z * width for z in range(depth)]
    for back, z in enumerate(reversed(range(depth))):
        columns = list(range(1, width))
        order += [z * width + x for x in (columns if back % 2 == 0 else reversed(columns))]
    return order


def ring_shift(value, by):
    peers = lax.axis_size("exp")
    order = ring_order(peers)
    pairs = []
    for rep in range(lax.axis_size("rep")):
        step = by if rep % 2 == 0 else -by
        for spot in range(peers):
            pairs.append((rep * peers + order[spot], rep * peers + order[(spot + step) % peers]))
    return lax.ppermute(value, ("rep", "exp"), pairs)


def from_behind(value, axis, by):
    peers = lax.axis_size(axis)
    return lax.ppermute(value, axis, [(i, (i + by) % peers) for i in range(peers)])


def dot(a, b, dims):
    return lax.dot_general(a, b, (dims, ((), ())), preferred_element_type=F32)


def whole():
    return pl.BlockSpec(memory_space=pltpu.VMEM)


def turned(value):
    rows, columns = value.shape
    wide = jnp.concatenate([value, jnp.zeros((rows, 128 - columns), F32)], axis=1)
    return wide.T[:columns]


def pack_kernel(experts, codes_ref, exps_ref, routes_ref, weight_ref, grad_ref, out_ref):
    tokens, width = codes_ref.shape
    blocks = exps_ref.shape[0]
    scales = jnp.exp2(exps_ref[...].astype(F32))
    scales = turned(jnp.concatenate([scales, jnp.zeros((128 - blocks, tokens), F32)], axis=0))
    per = width // blocks
    for b in range(blocks):
        cols = slice(b * per, (b + 1) * per)
        out_ref[:, cols] = (codes_ref[:, cols].astype(F32) * scales[:, b : b + 1]).astype(BF16)
    out_ref[:, width : 2 * width] = grad_ref[...]
    expert = lax.broadcasted_iota(jnp.int32, (experts, tokens), 0)
    table = jnp.zeros((experts, tokens), F32)
    for k in range(routes_ref.shape[0]):
        table += jnp.where(routes_ref[k : k + 1, :] == expert, weight_ref[k : k + 1, :], 0.0)
    high = table.astype(BF16).astype(F32)
    middle = (table - high).astype(BF16).astype(F32)
    low = table - high - middle
    extra = out_ref.shape[1] - 2 * width
    parts = [high, middle, low]
    if extra > 3 * experts:
        parts.append(jnp.zeros((extra - 3 * experts, tokens), F32))
    out_ref[:, 2 * width :] = turned(jnp.concatenate(parts, axis=0)).astype(BF16)


def row_copies(blocks, rows, width, sems, offset):
    tokens = blocks[0].shape[0]
    copies = []
    for i, block in enumerate(blocks):
        for part in range(2):
            copies.append(
                pltpu.make_async_copy(
                    block.at[:, pl.ds(part * width, width)],
                    rows.at[part, pl.ds(i * tokens, tokens)],
                    sems.at[offset + 2 * i + part],
                )
            )
    return copies


def expert_kernel(count, experts, local_experts, width, first_ref, *refs):
    blocks = refs[:count]
    weights = refs[count : count + 6]
    outs = refs[count + 6 : 2 * count + 6]
    gate_out, up_out, hidden_out, rows, tables, buffer, gates, slopes, sems = refs[2 * count + 6 :]
    half = weights[0].shape[0]
    units = 2 * half
    copies = []
    for i in range(6):
        kind, side = divmod(i, 2)
        copies.append(
            pltpu.make_async_copy(
                weights[side * 3 + kind], buffer.at[kind, pl.ds(side * half, half)], sems.at[i]
            )
        )
    tokens = blocks[0].shape[0]
    lanes = blocks[0].shape[1] - 2 * width
    loads = row_copies(blocks, rows, width, sems, 6)
    for i, block in enumerate(blocks):
        loads.append(
            pltpu.make_async_copy(
                block.at[:, pl.ds(2 * width, lanes)], tables.at[i], sems.at[6 + 2 * count + i]
            )
        )
    for copy in copies[:2] + loads + copies[2:]:
        copy.start()
    for copy in loads:
        copy.wait()
    parts = []
    expert_of = lax.rem(lax.broadcasted_iota(jnp.int32, (tokens, lanes), 1), experts)
    for i in range(count):
        table = tables[i].astype(F32)
        parts.append(
            [
                jnp.sum(
                    jnp.where(expert_of == first_ref[0] + e, table, 0.0), axis=1, keepdims=True
                )
                for e in range(local_experts)
            ]
        )
    scales = [jnp.concatenate([s[e] for s in parts], axis=0) for e in range(local_experts)]
    tile = 256
    last = ((1,), (1,))
    plain = ((1,), (0,))
    tiles = [slice(j * tile, (j + 1) * tile) for j in range(units // tile)]

    def scale_of(at, shape):
        unit = lax.rem(at.start + lax.broadcasted_iota(jnp.int32, (1, tile), 1), half)
        scale = jnp.broadcast_to(scales[0], shape)
        for e in range(1, local_experts):
            scale = jnp.where(unit >= e * (half // local_experts), scales[e], scale)
        return scale

    copies[0].wait()
    copies[1].wait()
    for at in tiles:
        gates[:, at] = dot(rows[0], buffer[0, at, :], last)
    copies[2].wait()
    copies[3].wait()
    for at in tiles:
        gate = gates[:, at]
        up = dot(rows[0], buffer[1, at, :], last)
        sig = 1.0 / (1.0 + jnp.exp(-gate))
        swish = gate * sig
        scale = scale_of(at, gate.shape)
        hidden_out[:, at] = (swish * up * scale).astype(BF16)
        gates[:, at] = swish * scale
        slopes[:, at] = up * sig * (1.0 + gate * (1.0 - sig)) * scale
    copies[4].wait()
    copies[5].wait()
    for at in tiles:
        back = dot(rows[1], buffer[2, at, :], last)
        gate_out[:, at] = (back * slopes[:, at]).astype(BF16)
        up_out[:, at] = (back * gates[:, at]).astype(BF16)

    def column_tile(n, carry):
        at = pl.ds(pl.multiple_of(n * tile, tile), tile)
        later = pl.ds(pl.multiple_of(width + n * tile, tile), tile)
        output = dot(hidden_out[...], buffer[2, :, at], plain).astype(BF16)
        grad = (
            dot(gate_out[...], buffer[0, :, at], plain) + dot(up_out[...], buffer[1, :, at], plain)
        ).astype(BF16)
        for i, out in enumerate(outs):
            out[:, at] = output[i * tokens : (i + 1) * tokens]
            out[:, later] = grad[i * tokens : (i + 1) * tokens]
        return carry

    lax.fori_loop(0, width // tile, column_tile, 0, unroll=2)


def expert_call(blocks, weights, first, experts, local_experts, width):
    count = len(blocks)
    tokens = blocks[0].shape[0]
    half = weights[0].shape[0]
    rows = count * tokens
    saved = jax.ShapeDtypeStruct((rows, 2 * half), BF16)
    results = pl.pallas_call(
        functools.partial(expert_kernel, count, experts, local_experts, width),
        out_shape=[jax.ShapeDtypeStruct((tokens, 2 * width), BF16)] * count
        + [saved] * 3,
        in_specs=[pl.BlockSpec(memory_space=pltpu.SMEM)]
        + [pl.BlockSpec(memory_space=pl.ANY)] * (count + 6),
        out_specs=[whole()] * (count + 3),
        scratch_shapes=[
            pltpu.VMEM((2, rows, width), BF16),
            pltpu.VMEM((count, tokens, blocks[0].shape[1] - 2 * width), BF16),
            pltpu.VMEM((3, 2 * half, width), BF16),
            pltpu.VMEM((rows, 2 * half), F32),
            pltpu.VMEM((rows, 2 * half), F32),
            pltpu.SemaphoreType.DMA((6 + 3 * count,)),
        ],
        compiler_params=pltpu.CompilerParams(vmem_limit_bytes=VMEM_BYTES),
        cost_estimate=pl.CostEstimate(
            flops=6 * 2 * rows * 2 * half * width,
            bytes_accessed=12 * half * width + 8 * rows * width,
            transcendentals=rows * 2 * half,
        ),
        name="expert_rows",
    )(first, *blocks, *weights)
    return results[:count], results[count:]


def weight_kernel(groups, count, has_received, *refs):
    blocks = refs[:count]
    kept = [refs[count + g * 3 : count + g * 3 + 3] for g in range(groups)]
    refs = refs[count + groups * 3 :]
    received = refs[:3] if has_received else None
    outs = refs[-6:-3]
    across, rows, sems = refs[-3:]
    tile = outs[0].shape[1]
    copies = row_copies(blocks, rows, rows.shape[2], sems, 0)

    @pl.when(pl.program_id(0) == 0)
    def _():
        for copy in copies:
            copy.start()
        for kind in range(3):
            start = 0
            for group in kept:
                size = group[kind].shape[0]
                across[kind, :, start : start + size] = group[kind][...].T
                start += size
        for copy in copies:
            copy.wait()

    at = pl.ds(pl.multiple_of(pl.program_id(0) * tile, tile), tile)
    for kind in range(3):
        total = dot(across[kind], rows[kind // 2, :, at], ((1,), (0,)))
        if has_received:
            total = total + received[kind][...].astype(F32)
        outs[kind][...] = total.astype(BF16)


def weight_call(blocks, kept, side, received, width):
    half = kept[0][0].shape[1] // 2
    tile = 512
    steps = width // tile
    column = pl.BlockSpec((half, tile), lambda n: (0, n))
    total = len(blocks) * blocks[0].shape[0]
    specs = [pl.BlockSpec(memory_space=pl.ANY)] * len(blocks)
    args = list(blocks)
    for group in kept:
        specs += [pl.BlockSpec((g.shape[0], half), lambda n: (0, side)) for g in group]
        args += list(group)
    if received is not None:
        specs += [column] * 3
        args += list(received)
    return pl.pallas_call(
        functools.partial(weight_kernel, len(kept), len(blocks), received is not None),
        grid=(steps,),
        out_shape=[jax.ShapeDtypeStruct((half, width), BF16)] * 3,
        in_specs=specs,
        out_specs=[column] * 3,
        scratch_shapes=[
            pltpu.VMEM((3, half, total), BF16),
            pltpu.VMEM((2, total, width), BF16),
            pltpu.SemaphoreType.DMA((2 * len(blocks),)),
        ],
        compiler_params=pltpu.CompilerParams(vmem_limit_bytes=VMEM_BYTES),
        cost_estimate=pl.CostEstimate(
            flops=3 * 2 * total * half * width,
            bytes_accessed=4 * total * width + 12 * half * width,
            transcendentals=0,
        ),
        name="weight_grads",
    )(*args)


def add(a, b):
    return (a.astype(F32) + b.astype(F32)).astype(BF16)


def shards(
    row_codes, block_exponents, routes, route_weight, out_grad, gate_weight, up_weight, down_weight
):
    tokens, width = row_codes.shape[1:]
    local_experts, half_units = gate_weight.shape[1:3]
    half = local_experts * half_units
    peers = lax.axis_size("exp")
    experts = peers * local_experts
    lanes = -(-3 * experts // 128) * 128
    own = [w.reshape(half, width) for w in (gate_weight, up_weight, down_weight)]
    other = [from_behind(w, "rep", 1) for w in own]
    weights = own + other
    first = (lax.axis_index("exp") * local_experts).astype(jnp.int32).reshape(1)
    home = pl.pallas_call(
        functools.partial(pack_kernel, experts),
        out_shape=jax.ShapeDtypeStruct((tokens, 2 * width + lanes), BF16),
        in_specs=[whole()] * 5,
        out_specs=whole(),
        name="pack_rows",
    )(row_codes[0], block_exponents[0].T, routes[0].T, route_weight[0].T, out_grad[0])

    tie = lax.optimization_barrier
    ahead, behind = peers // 2, peers // 2 - 1
    near, far = [home], [home]
    partial, kept, blocks = {}, [], []

    def expert_rows(names):
        held = [(near if name == "near" else far)[k] for name, k in names]
        outs, saved = expert_call(held, weights, first, experts, local_experts, width)
        for name, out in zip(names, outs):
            partial[name] = out
        kept.append(saved)
        blocks.extend(held)

    waiting = [("near", 0)]
    for k in range(1, ahead + 1):
        near.append(ring_shift(near[k - 1], 1))
        if k <= behind:
            far.append(ring_shift(far[k - 1], -1))
        done = None
        if len(waiting) >= 4:
            expert_rows(waiting[:4])
            done, waiting = kept[-1], waiting[4:]
        if k <= behind:
            near[k], far[k], done = tie((near[k], far[k], done))
            waiting += [("near", k), ("far", k)]
        else:
            expert_rows([name for name in waiting if name[0] == "far"])
            waiting = [name for name in waiting if name[0] == "near"]
            near[k], done = tie((near[k], kept[-1]))
            waiting.append(("near", k))
        if done is not None:
            kept[-1] = done
    far_sum = ring_shift(partial["far", behind], 1)
    expert_rows(waiting)
    far_sum, near_sum = tie((far_sum, partial["near", ahead]))
    given = received = totals = None
    for k in range(ahead, 1, -1):
        near_sum = ring_shift(near_sum, -1)
        left = k - 2
        if left >= 1:
            far_sum = ring_shift(add(far_sum, partial["far", left]), 1)
        if k == ahead:
            given = weight_call(blocks, kept, 1, None, width)
            near_sum, far_sum, given = tie((near_sum, far_sum, given))
            received = [from_behind(g, "rep", 1) for g in given]
        elif k == ahead - 1:
            totals = weight_call(blocks, kept, 0, received, width)
            near_sum, far_sum, totals = tie((near_sum, far_sum, totals))
        if k > 2:
            near_sum = add(near_sum, partial["near", k - 1])
    results = []
    for part, axis_step in ((slice(0, width), 1), (slice(width, 2 * width), -1)):
        arrived = ring_shift(add(near_sum[:, part], partial["near", 1][:, part]), -1)
        total = home[:, part].astype(F32) + partial["near", 0][:, part].astype(F32)
        total = total + far_sum[:, part].astype(F32) + arrived.astype(F32)
        results.append(from_behind(total.astype(BF16)[None], "section", axis_step))
    shape = (1, local_experts, half_units, width)
    return tuple(results) + tuple(t.reshape(shape) for t in totals)


def solution(mesh):
    tokens = P("section", ("rep", "exp"), None)
    weights = P("section", "exp", "rep", None)
    return jax.shard_map(
        shards,
        mesh=mesh,
        in_specs=(tokens,) * 5 + (weights,) * 3,
        out_specs=(tokens,) * 2 + (weights,) * 3,
        check_vma=False,
    )
```

```python
import functools
import jax
import jax.numpy as jnp
from jax import lax
from jax.experimental import pallas as pl
from jax.experimental.pallas import tpu as pltpu
from jax.sharding import PartitionSpec as P

F32 = jnp.float32
BF16 = jnp.bfloat16
VMEM_BYTES = 60 * 2**20


def ring_order(peers):
    width = 1
    while 8 * width * width <= peers:
        width *= 2
    depth = peers // width
    if width == 1 or depth % 2:
        return list(range(peers))
    order = [z * width for z in range(depth)]
    for back, z in enumerate(reversed(range(depth))):
        columns = list(range(1, width))
        order += [z * width + x for x in (columns if back % 2 == 0 else reversed(columns))]
    return order


def ring_shift(value, by):
    peers = lax.axis_size("exp")
    order = ring_order(peers)
    pairs = []
    for rep in range(lax.axis_size("rep")):
        step = by if rep % 2 == 0 else -by
        for spot in range(peers):
            pairs.append((rep * peers + order[spot], rep * peers + order[(spot + step) % peers]))
    return lax.ppermute(value, ("rep", "exp"), pairs)


def from_behind(value, axis, by):
    peers = lax.axis_size(axis)
    return lax.ppermute(value, axis, [(i, (i + by) % peers) for i in range(peers)])


def dot(a, b, dims):
    return lax.dot_general(a, b, (dims, ((), ())), preferred_element_type=F32)


def whole():
    return pl.BlockSpec(memory_space=pltpu.VMEM)


def turned(value):
    rows, columns = value.shape
    wide = jnp.concatenate([value, jnp.zeros((rows, 128 - columns), F32)], axis=1)
    return wide.T[:columns]


def pack_kernel(experts, codes_ref, exps_ref, routes_ref, weight_ref, out_ref):
    tokens, width = codes_ref.shape
    blocks = exps_ref.shape[0]
    scales = jnp.exp2(exps_ref[...].astype(F32))
    scales = turned(jnp.concatenate([scales, jnp.zeros((128 - blocks, tokens), F32)], axis=0))
    per = width // blocks
    for b in range(blocks):
        cols = slice(b * per, (b + 1) * per)
        out_ref[:, cols] = (codes_ref[:, cols].astype(F32) * scales[:, b : b + 1]).astype(BF16)
    expert = lax.broadcasted_iota(jnp.int32, (experts, tokens), 0)
    table = jnp.zeros((experts, tokens), F32)
    for k in range(routes_ref.shape[0]):
        table += jnp.where(routes_ref[k : k + 1, :] == expert, weight_ref[k : k + 1, :], 0.0)
    high = table.astype(BF16).astype(F32)
    middle = (table - high).astype(BF16).astype(F32)
    low = table - high - middle
    extra = out_ref.shape[1] - width
    parts = [high, middle, low]
    if extra > 3 * experts:
        parts.append(jnp.zeros((extra - 3 * experts, tokens), F32))
    out_ref[:, width:] = turned(jnp.concatenate(parts, axis=0)).astype(BF16)


def row_copies(blocks, rows, sems, offset):
    tokens = blocks[0].shape[0]
    return [
        pltpu.make_async_copy(
            block.at[:, pl.ds(0, rows.shape[1])],
            rows.at[pl.ds(i * tokens, tokens)],
            sems.at[offset + i],
        )
        for i, block in enumerate(blocks)
    ]


def weight_copies(weights, buffer, sems):
    half = weights[0].shape[0]
    return [
        pltpu.make_async_copy(
            weights[side * 3 + kind],
            buffer.at[kind, pl.ds(side * half, half)],
            sems.at[2 * kind + side],
        )
        for kind in range(3)
        for side in range(2)
    ]


LAST = ((1,), (1,))
PLAIN = ((1,), (0,))
TILE = 256


def columns_of(width, body):
    def step(n, carry):
        body(pl.ds(pl.multiple_of(n * TILE, TILE), TILE))
        return carry

    lax.fori_loop(0, width // TILE, step, 0, unroll=2)


def forward_kernel(count, experts, local_experts, first_ref, *refs):
    blocks = refs[:count]
    weights = refs[count : count + 6]
    outs = refs[count + 6 : 2 * count + 6]
    hidden_out, swish_out, slope_out, rows, tables, buffer, left, sems = refs[2 * count + 6 :]
    units, width = buffer.shape[1:]
    tokens, lanes = blocks[0].shape[0], tables.shape[1]
    copies = weight_copies(weights, buffer, sems)
    loads = row_copies(blocks, rows, sems, 6)
    for i, block in enumerate(blocks):
        loads.append(
            pltpu.make_async_copy(
                block.at[:, pl.ds(width, lanes)],
                tables.at[pl.ds(i * tokens, tokens)],
                sems.at[6 + count + i],
            )
        )
    for copy in copies[:2] + loads + copies[2:]:
        copy.start()
    for copy in loads + copies[:2]:
        copy.wait()
    gate = dot(buffer[0], rows[...], LAST)
    table = tables[...].astype(F32).T
    expert_of = lax.rem(lax.broadcasted_iota(jnp.int32, table.shape, 0), experts)
    scales = [
        jnp.sum(jnp.where(expert_of == first_ref[0] + e, table, 0.0), axis=0, keepdims=True)
        for e in range(local_experts)
    ]
    half = units // 2
    unit = lax.rem(lax.broadcasted_iota(jnp.int32, (units, 1), 0), half)
    scale = scales[0]
    for e in range(1, local_experts):
        scale = jnp.where(unit >= e * (half // local_experts), scales[e], scale)
    copies[2].wait()
    copies[3].wait()
    up = dot(buffer[1], rows[...], LAST)
    sig = 1.0 / (1.0 + jnp.exp(-gate))
    swish = gate * sig
    weighted = swish * scale
    hidden = (weighted * up).astype(BF16)
    hidden_out[...] = hidden
    swish_out[...] = weighted
    slope_out[...] = up * sig * (1.0 + gate * (1.0 - sig)) * scale
    left[...] = hidden.T
    copies[4].wait()
    copies[5].wait()

    def column(at):
        output = dot(left[...], buffer[2, :, at], PLAIN).astype(BF16)
        for i, out in enumerate(outs):
            out[:, at] = output[i * tokens : (i + 1) * tokens]

    columns_of(width, column)


def backward_kernel(count, *refs):
    blocks = refs[:count]
    swish_ref, slope_ref = refs[count : count + 2]
    weights = refs[count + 2 : count + 8]
    outs = refs[count + 8 : 2 * count + 8]
    gate_out, up_out, rows, buffer, gate_left, up_left, sems = refs[2 * count + 8 :]
    width = buffer.shape[2]
    tokens = blocks[0].shape[0]
    copies = weight_copies(weights, buffer, sems)
    loads = row_copies(blocks, rows, sems, 6)
    for copy in copies[4:] + loads + copies[:4]:
        copy.start()
    for copy in loads + copies[4:]:
        copy.wait()
    back = dot(buffer[2], rows[...], LAST)
    gate_grad = (back * slope_ref[...]).astype(BF16)
    up_grad = (back * swish_ref[...]).astype(BF16)
    gate_out[...] = gate_grad
    up_out[...] = up_grad
    gate_left[...] = gate_grad.T
    up_left[...] = up_grad.T
    for copy in copies[:4]:
        copy.wait()

    def column(at):
        grad = dot(gate_left[...], buffer[0, :, at], PLAIN)
        grad = (grad + dot(up_left[...], buffer[1, :, at], PLAIN)).astype(BF16)
        for i, out in enumerate(outs):
            out[:, at] = grad[i * tokens : (i + 1) * tokens]

    columns_of(width, column)


def forward_call(blocks, weights, first, experts, local_experts, width):
    count, (tokens, wide) = len(blocks), blocks[0].shape
    units, rows = 2 * weights[0].shape[0], count * tokens
    results = pl.pallas_call(
        functools.partial(forward_kernel, count, experts, local_experts),
        out_shape=[jax.ShapeDtypeStruct((tokens, width), BF16)] * count
        + [jax.ShapeDtypeStruct((units, rows), BF16)]
        + [jax.ShapeDtypeStruct((units, rows), F32)] * 2,
        in_specs=[pl.BlockSpec(memory_space=pltpu.SMEM)]
        + [pl.BlockSpec(memory_space=pl.ANY)] * (count + 6),
        out_specs=[whole()] * (count + 3),
        scratch_shapes=[
            pltpu.VMEM((rows, width), BF16),
            pltpu.VMEM((rows, wide - width), BF16),
            pltpu.VMEM((3, units, width), BF16),
            pltpu.VMEM((rows, units), BF16),
            pltpu.SemaphoreType.DMA((6 + 2 * count,)),
        ],
        compiler_params=pltpu.CompilerParams(vmem_limit_bytes=VMEM_BYTES),
        cost_estimate=pl.CostEstimate(
            flops=3 * 2 * rows * units * width,
            bytes_accessed=6 * units * width + 4 * rows * width,
            transcendentals=rows * units,
        ),
        name="expert_forward",
    )(first, *blocks, *weights)
    return results[:count], results[count:]


def backward_call(blocks, saved, weights, width):
    count, tokens = len(blocks), blocks[0].shape[0]
    units, rows = 2 * weights[0].shape[0], count * tokens
    results = pl.pallas_call(
        functools.partial(backward_kernel, count),
        out_shape=[jax.ShapeDtypeStruct((tokens, width), BF16)] * count
        + [jax.ShapeDtypeStruct((units, rows), BF16)] * 2,
        in_specs=[pl.BlockSpec(memory_space=pl.ANY)] * count
        + [whole()] * 2
        + [pl.BlockSpec(memory_space=pl.ANY)] * 6,
        out_specs=[whole()] * (count + 2),
        scratch_shapes=[
            pltpu.VMEM((rows, width), BF16),
            pltpu.VMEM((3, units, width), BF16),
            pltpu.VMEM((rows, units), BF16),
            pltpu.VMEM((rows, units), BF16),
            pltpu.SemaphoreType.DMA((6 + count,)),
        ],
        compiler_params=pltpu.CompilerParams(vmem_limit_bytes=VMEM_BYTES),
        cost_estimate=pl.CostEstimate(
            flops=3 * 2 * rows * units * width,
            bytes_accessed=6 * units * width + 4 * rows * width,
            transcendentals=0,
        ),
        name="expert_backward",
    )(*blocks, *saved, *weights)
    return results[:count], results[count:]


def weight_kernel(groups, count, *refs):
    blocks = [refs[:count], refs[count : 2 * count]]
    kept = [refs[2 * count + g * 3 : 2 * count + g * 3 + 3] for g in range(groups)]
    outs = refs[-9:-3]
    across, rows, sems = refs[-3:]
    half, tile = outs[0].shape
    copies = row_copies(blocks[0], rows.at[0], sems, 0)
    copies += row_copies(blocks[1], rows.at[1], sems, count)

    @pl.when(pl.program_id(0) == 0)
    def _():
        for copy in copies:
            copy.start()
        for kind in range(3):
            start = 0
            for group in kept:
                size = group[kind].shape[1]
                across[kind, :, start : start + size] = group[kind][...]
                start += size
        for copy in copies:
            copy.wait()

    at = pl.ds(pl.multiple_of(pl.program_id(0) * tile, tile), tile)
    for kind in range(3):
        total = dot(across[kind], rows[kind // 2, :, at], PLAIN).astype(BF16)
        outs[kind][...] = total[:half]
        outs[3 + kind][...] = total[half:]


def weight_call(row_blocks, grad_blocks, kept, width):
    count = len(row_blocks)
    units = kept[0][0].shape[0]
    half, tile = units // 2, 2 * TILE
    total = count * row_blocks[0].shape[0]
    results = pl.pallas_call(
        functools.partial(weight_kernel, len(kept), count),
        grid=(width // tile,),
        out_shape=[jax.ShapeDtypeStruct((half, width), BF16)] * 6,
        in_specs=[pl.BlockSpec(memory_space=pl.ANY)] * (2 * count) + [whole()] * (3 * len(kept)),
        out_specs=[pl.BlockSpec((half, tile), lambda n: (0, n))] * 6,
        scratch_shapes=[
            pltpu.VMEM((3, units, total), BF16),
            pltpu.VMEM((2, total, width), BF16),
            pltpu.SemaphoreType.DMA((2 * count,)),
        ],
        compiler_params=pltpu.CompilerParams(vmem_limit_bytes=VMEM_BYTES),
        cost_estimate=pl.CostEstimate(
            flops=3 * 2 * total * units * width,
            bytes_accessed=4 * total * width + 12 * half * width,
            transcendentals=0,
        ),
        name="weight_grads",
    )(*row_blocks, *grad_blocks, *[k for group in kept for k in group])
    return results[:3], results[3:]


def add(a, b):
    return (a.astype(F32) + b.astype(F32)).astype(BF16)


def shards(
    row_codes, block_exponents, routes, route_weight, out_grad, gate_weight, up_weight, down_weight
):
    tokens, width = row_codes.shape[1:]
    local_experts, half_units = gate_weight.shape[1:3]
    half = local_experts * half_units
    peers = lax.axis_size("exp")
    experts = peers * local_experts
    lanes = -(-3 * experts // 128) * 128
    own = [w.reshape(half, width) for w in (gate_weight, up_weight, down_weight)]
    other = [from_behind(w, "rep", 1) for w in own]
    weights = own + other
    first = (lax.axis_index("exp") * local_experts).astype(jnp.int32).reshape(1)
    home = pl.pallas_call(
        functools.partial(pack_kernel, experts),
        out_shape=jax.ShapeDtypeStruct((tokens, width + lanes), BF16),
        in_specs=[whole()] * 4,
        out_specs=whole(),
        name="pack_rows",
    )(row_codes[0], block_exponents[0].T, routes[0].T, route_weight[0].T)

    tie = lax.optimization_barrier
    ahead, behind = peers // 2, peers // 2 - 1
    names = [("near", 0)]
    for k in range(1, ahead + 1):
        names += [("near", k), ("far", k)]
    names = names[: 2 * ahead]
    groups = [names[i : i + 4] for i in range(0, len(names), 4)]
    rows = {("near", 0): home, ("far", 0): home}
    grads = {("near", 0): out_grad[0], ("far", 0): out_grad[0]}
    outputs, back, saved, kept = {}, {}, [], []

    def spread(held, k, work):
        for name, step in (("near", 1), ("far", -1)):
            if (name, k) in names:
                held[name, k] = ring_shift(held[name, k - 1], step)
        done = work()
        here = [name for name in (("near", k), ("far", k)) if name in names]
        tied, done = tie(([held[name] for name in here], done))
        held.update(zip(here, tied))
        return done

    def forward(g):
        outs, keep = forward_call(
            [rows[name] for name in groups[g]], weights, first, experts, local_experts, width
        )
        outputs.update(zip(groups[g], outs))
        saved.append(keep)
        return keep

    def backward(g):
        outs, keep = backward_call(
            [grads[name] for name in groups[g]], saved[g][1:], weights, width
        )
        back.update(zip(groups[g], outs))
        kept.append([keep[0], keep[1], saved[g][0]])
        return keep

    for k in range(1, ahead + 1):
        for held, work, got in ((rows, forward, saved), (grads, backward, kept)):
            ready = k % 2 == 1 and k > 1
            done = spread(held, k, lambda: work(k // 2 - 1) if ready else None)
    forward(len(groups) - 1)
    backward(len(groups) - 1)

    def collect(partial, k, sums):
        near, far = sums
        near = ring_shift(partial["near", ahead] if near is None else near, -1)
        if k > 1:
            far = ring_shift(partial["far", behind] if far is None else far, 1)
        return near, far

    def join(partial, k, sums):
        near, far = sums
        if k > 1:
            near = add(near, partial["near", k - 1])
        if k > 2:
            far = add(far, partial["far", k - 2])
        return near, far

    out_sums = back_sums = (None, None)
    own = other_half = received = totals = None
    for k in range(ahead, 0, -1):
        out_sums = collect(outputs, k, out_sums)
        back_sums = collect(back, k, back_sums)
        if k == ahead:
            own, other_half = weight_call(
                [rows[name] for group in groups for name in group],
                [grads[name] for group in groups for name in group],
                kept,
                width,
            )
            back_sums, own, other_half = tie((back_sums, own, other_half))
            received = [from_behind(g, "rep", 1) for g in other_half]
        elif k == ahead - 1:
            totals = [add(a, b) for a, b in zip(own, received)]
            back_sums, totals = tie((back_sums, totals))
        out_sums = join(outputs, k, out_sums)
        back_sums = join(back, k, back_sums)
    results = []
    for base, partial, sums, step in (
        (home[:, :width], outputs, out_sums, 1),
        (out_grad[0], back, back_sums, -1),
    ):
        total = base.astype(F32) + partial["near", 0].astype(F32)
        total = total + sums[0].astype(F32) + sums[1].astype(F32)
        results.append(from_behind(total.astype(BF16)[None], "section", step))
    shape = (1, local_experts, half_units, width)
    return tuple(results) + tuple(t.reshape(shape) for t in totals)


def solution(mesh):
    tokens = P("section", ("rep", "exp"), None)
    weights = P("section", "exp", "rep", None)
    return jax.shard_map(
        shards,
        mesh=mesh,
        in_specs=(tokens,) * 5 + (weights,) * 3,
        out_specs=(tokens,) * 2 + (weights,) * 3,
        check_vma=False,
    )
```

```python
import functools
import jax
import jax.numpy as jnp
from jax import lax
from jax.experimental import pallas as pl
from jax.experimental.pallas import tpu as pltpu
from jax.sharding import PartitionSpec as P

F32 = jnp.float32
BF16 = jnp.bfloat16


def vmem(peers):
    return (30 if peers <= 8 else 60) * 2**20


def ring_order(peers):
    width = 1
    while 8 * width * width <= peers:
        width *= 2
    depth = peers // width
    if width == 1 or depth % 2:
        return list(range(peers))
    order = [z * width for z in range(depth)]
    for back, z in enumerate(reversed(range(depth))):
        columns = list(range(1, width))
        order += [z * width + x for x in (columns if back % 2 == 0 else reversed(columns))]
    return order


def ring_shift(value, by):
    peers = lax.axis_size("exp")
    order = ring_order(peers)
    pairs = []
    for rep in range(lax.axis_size("rep")):
        step = by if rep % 2 == 0 else -by
        for spot in range(peers):
            pairs.append((rep * peers + order[spot], rep * peers + order[(spot + step) % peers]))
    return lax.ppermute(value, ("rep", "exp"), pairs)


def from_behind(value, axis, by):
    peers = lax.axis_size(axis)
    return lax.ppermute(value, axis, [(i, (i + by) % peers) for i in range(peers)])


def dot(a, b, dims):
    return lax.dot_general(a, b, (dims, ((), ())), preferred_element_type=F32)


def whole():
    return pl.BlockSpec(memory_space=pltpu.VMEM)


def turned(value):
    rows, columns = value.shape
    wide = jnp.concatenate([value, jnp.zeros((rows, 128 - columns), F32)], axis=1)
    return wide.T[:columns]


def pack_kernel(experts, codes_ref, exps_ref, routes_ref, weight_ref, grad_ref, out_ref):
    tokens, width = codes_ref.shape
    blocks = exps_ref.shape[0]
    scales = jnp.exp2(exps_ref[...].astype(F32))
    scales = turned(jnp.concatenate([scales, jnp.zeros((128 - blocks, tokens), F32)], axis=0))
    per = width // blocks
    for b in range(blocks):
        cols = slice(b * per, (b + 1) * per)
        out_ref[:, cols] = (codes_ref[:, cols].astype(F32) * scales[:, b : b + 1]).astype(BF16)
    expert = lax.broadcasted_iota(jnp.int32, (experts, tokens), 0)
    table = jnp.zeros((experts, tokens), F32)
    for k in range(routes_ref.shape[0]):
        table += jnp.where(routes_ref[k : k + 1, :] == expert, weight_ref[k : k + 1, :], 0.0)
    high = table.astype(BF16).astype(F32)
    middle = (table - high).astype(BF16).astype(F32)
    low = table - high - middle
    out_ref[:, width : 2 * width] = grad_ref[...]
    extra = out_ref.shape[1] - 2 * width
    parts = [high, middle, low]
    if extra > 3 * experts:
        parts.append(jnp.zeros((extra - 3 * experts, tokens), F32))
    out_ref[:, 2 * width :] = turned(jnp.concatenate(parts, axis=0)).astype(BF16)


LAST = ((1,), (1,))
PLAIN = ((1,), (0,))
TILE = 256


def columns_of(width, body):
    def step(n, carry):
        body(n * TILE)
        return carry

    lax.fori_loop(0, width // TILE, step, 0, unroll=2)


def span(start):
    return pl.ds(pl.multiple_of(start, TILE), TILE)


def load_kernel(*refs):
    count = len(refs) // 2
    copies = [
        pltpu.make_async_copy(refs[i], refs[count + i], refs[-1].at[i]) for i in range(count)
    ]
    for copy in copies:
        copy.start()
    for copy in copies:
        copy.wait()


def load_call(weights):
    return pl.pallas_call(
        load_kernel,
        out_shape=[jax.ShapeDtypeStruct(w.shape, w.dtype) for w in weights],
        in_specs=[pl.BlockSpec(memory_space=pl.ANY)] * len(weights),
        out_specs=[whole()] * len(weights),
        scratch_shapes=[pltpu.SemaphoreType.DMA((len(weights),))],
        cost_estimate=pl.CostEstimate(flops=0, bytes_accessed=10**7, transcendentals=0),
        name="load_weights",
    )(*weights)


def expert_kernel(count, experts, local_experts, first_ref, *refs):
    blocks = refs[:count]
    weights = refs[count : count + 6]
    outs = refs[count + 6 : 2 * count + 6]
    saved = refs[2 * count + 6 : 2 * count + 9]
    rows, left = refs[2 * count + 9 :]
    half, width = weights[0].shape
    tokens = blocks[0].shape[0]
    tables = []
    for i, block in enumerate(blocks):
        rows[0, i * tokens : (i + 1) * tokens] = block[:, :width]
        rows[1, i * tokens : (i + 1) * tokens] = block[:, width : 2 * width]
        tables.append(block[:, 2 * width :].astype(F32))
    table = jnp.concatenate(tables, axis=0).T
    expert_of = lax.rem(lax.broadcasted_iota(jnp.int32, table.shape, 0), experts)
    scales = [
        jnp.sum(jnp.where(expert_of == first_ref[0] + e, table, 0.0), axis=0, keepdims=True)
        for e in range(local_experts)
    ]
    unit = lax.broadcasted_iota(jnp.int32, (half, 1), 0)
    scale = scales[0]
    for e in range(1, local_experts):
        scale = jnp.where(unit >= e * (half // local_experts), scales[e], scale)
    for side in range(2):
        at = slice(side * half, (side + 1) * half)
        gate = dot(weights[3 * side][...], rows[0], LAST)
        up = dot(weights[3 * side + 1][...], rows[0], LAST)
        back = dot(weights[3 * side + 2][...], rows[1], LAST) * scale
        sig = 1.0 / (1.0 + jnp.exp(-gate))
        swish = gate * sig
        results = (
            back * up * sig * (1.0 + gate * (1.0 - sig)),
            back * swish,
            swish * up * scale,
        )
        for kind, result in enumerate(results):
            result = result.astype(BF16)
            saved[kind][at, :] = result
            left[kind, :, at] = result.T

    def column(start):
        at, later = span(start), span(width + start)
        right = [
            jnp.concatenate([weights[kind][:, at], weights[3 + kind][:, at]], axis=0)
            for kind in range(3)
        ]
        output = dot(left[2], right[2], PLAIN).astype(BF16)
        grad = (dot(left[0], right[0], PLAIN) + dot(left[1], right[1], PLAIN)).astype(BF16)
        for i, out in enumerate(outs):
            out[:, at] = output[i * tokens : (i + 1) * tokens]
            out[:, later] = grad[i * tokens : (i + 1) * tokens]

    columns_of(width, column)


def expert_call(blocks, weights, first, experts, local_experts):
    count, tokens = len(blocks), blocks[0].shape[0]
    half, width = weights[0].shape
    units, rows = 2 * half, count * tokens
    results = pl.pallas_call(
        functools.partial(expert_kernel, count, experts, local_experts),
        out_shape=[jax.ShapeDtypeStruct((tokens, 2 * width), BF16)] * count
        + [jax.ShapeDtypeStruct((units, rows), BF16)] * 3,
        in_specs=[pl.BlockSpec(memory_space=pltpu.SMEM)] + [whole()] * (count + 6),
        out_specs=[whole()] * (count + 3),
        scratch_shapes=[
            pltpu.VMEM((2, rows, width), BF16),
            pltpu.VMEM((3, rows, units), BF16),
        ],
        compiler_params=pltpu.CompilerParams(vmem_limit_bytes=vmem(experts // local_experts)),
        cost_estimate=pl.CostEstimate(
            flops=6 * 2 * rows * units * width,
            bytes_accessed=6 * units * width + 8 * rows * width,
            transcendentals=rows * units,
        ),
        name="expert_rows",
    )(first, *blocks, *weights)
    return results[:count], results[count:]


def weight_kernel(groups, count, *refs):
    blocks = refs[:count]
    kept = [refs[count + g * 3 : count + g * 3 + 3] for g in range(groups)]
    outs, across = refs[-7:-1], refs[-1]
    half, width = outs[0].shape
    for kind in range(3):
        start = 0
        for group in kept:
            size = group[kind].shape[1]
            across[kind, :, start : start + size] = group[kind][...]
            start += size

    def column(start):
        at, later = span(start), span(width + start)
        right = [
            jnp.concatenate([b[:, at] for b in blocks], axis=0),
            jnp.concatenate([b[:, later] for b in blocks], axis=0),
        ]
        for kind in range(3):
            total = dot(across[kind], right[kind // 2], PLAIN).astype(BF16)
            outs[kind][:, at] = total[:half]
            outs[3 + kind][:, at] = total[half:]

    columns_of(width, column)


def weight_call(blocks, kept, width, peers):
    count = len(blocks)
    units = kept[0][0].shape[0]
    half, total = units // 2, count * blocks[0].shape[0]
    results = pl.pallas_call(
        functools.partial(weight_kernel, len(kept), count),
        out_shape=[jax.ShapeDtypeStruct((half, width), BF16)] * 6,
        in_specs=[whole()] * (count + 3 * len(kept)),
        out_specs=[whole()] * 6,
        scratch_shapes=[pltpu.VMEM((3, units, total), BF16)],
        compiler_params=pltpu.CompilerParams(vmem_limit_bytes=vmem(peers)),
        cost_estimate=pl.CostEstimate(
            flops=3 * 2 * total * units * width,
            bytes_accessed=4 * total * width + 12 * half * width,
            transcendentals=0,
        ),
        name="weight_grads",
    )(*blocks, *[k for group in kept for k in group])
    return results[:3], results[3:]


def add(a, b):
    return (a.astype(F32) + b.astype(F32)).astype(BF16)


def shards(
    row_codes, block_exponents, routes, route_weight, out_grad, gate_weight, up_weight, down_weight
):
    tokens, width = row_codes.shape[1:]
    local_experts, half_units = gate_weight.shape[1:3]
    half = local_experts * half_units
    peers = lax.axis_size("exp")
    experts = peers * local_experts
    lanes = -(-3 * experts // 128) * 128
    shards_of = [w.reshape(half, width) for w in (gate_weight, up_weight, down_weight)]
    other = [from_behind(w, "rep", 1) for w in shards_of]
    own = load_call(shards_of)
    weights = list(own) + other
    first = (lax.axis_index("exp") * local_experts).astype(jnp.int32).reshape(1)
    home = pl.pallas_call(
        functools.partial(pack_kernel, experts),
        out_shape=jax.ShapeDtypeStruct((tokens, 2 * width + lanes), BF16),
        in_specs=[whole()] * 5,
        out_specs=whole(),
        name="pack_rows",
    )(row_codes[0], block_exponents[0].T, routes[0].T, route_weight[0].T, out_grad[0])

    tie = lax.optimization_barrier
    ahead, behind = peers // 2, peers // 2 - 1
    names = [("near", 0)]
    for k in range(1, ahead + 1):
        names += [("near", k), ("far", k)]
    names = names[: 2 * ahead]
    groups = [names[i : i + 4] for i in range(0, len(names) - 4, 4)]
    groups.append([name for name in names[-4:] if name[0] == "far"])
    groups.append([name for name in names[-4:] if name[0] == "near"])
    held = {("near", 0): home, ("far", 0): tie((home, own))[0]}
    partial, kept = {}, []

    def work(group):
        outs, saved = expert_call(
            [held[name] for name in group], weights, first, experts, local_experts
        )
        partial.update(zip(group, outs))
        kept.append(saved)

    for k in range(1, ahead + 1):
        held["near", k] = ring_shift(held["near", k - 1], 1)
        if k <= behind:
            held["far", k] = ring_shift(held["far", k - 1], -1)
        if k % 2 == 1 and k > 1:
            work(groups[(k - 3) // 2])
            held["near", k], kept[-1] = tie((held["near", k], kept[-1]))
    work(groups[-2])
    far_sum = ring_shift(partial["far", behind], 1)
    held["near", ahead], kept[-1] = tie((held["near", ahead], kept[-1]))
    work(groups[-1])
    far_sum, near_sum = tie((far_sum, partial["near", ahead]))
    own_total = received = totals = None
    blocks = [held[name] for group in groups for name in group]
    for k in range(ahead, 1, -1):
        near_sum = ring_shift(near_sum, -1)
        left = k - 2
        if left >= 1:
            far_sum = ring_shift(add(far_sum, partial["far", left]), 1)
        if k == ahead:
            own_total, other_total = weight_call(blocks, kept, width, peers)
            near_sum, far_sum, own_total, other_total = tie(
                (near_sum, far_sum, own_total, other_total)
            )
            received = [from_behind(g, "rep", 1) for g in other_total]
        elif k == ahead - 1:
            totals = [add(a, b) for a, b in zip(own_total, received)]
            near_sum, far_sum, totals = tie((near_sum, far_sum, totals))
        if k > 2:
            near_sum = add(near_sum, partial["near", k - 1])
    results = []
    for part, step in ((slice(0, width), 1), (slice(width, 2 * width), -1)):
        arrived = ring_shift(add(near_sum[:, part], partial["near", 1][:, part]), -1)
        total = home[:, part].astype(F32) + partial["near", 0][:, part].astype(F32)
        total = total + far_sum[:, part].astype(F32) + arrived.astype(F32)
        results.append(from_behind(total.astype(BF16)[None], "section", step))
    shape = (1, local_experts, half_units, width)
    return tuple(results) + tuple(t.reshape(shape) for t in totals)


def solution(mesh):
    tokens = P("section", ("rep", "exp"), None)
    weights = P("section", "exp", "rep", None)
    return jax.shard_map(
        shards,
        mesh=mesh,
        in_specs=(tokens,) * 5 + (weights,) * 3,
        out_specs=(tokens,) * 2 + (weights,) * 3,
        check_vma=False,
    )
```

```python
import functools
import jax
import jax.numpy as jnp
from jax import lax
from jax.experimental import pallas as pl
from jax.experimental.pallas import tpu as pltpu
from jax.sharding import PartitionSpec as P

F32 = jnp.float32
BF16 = jnp.bfloat16


def vmem(peers):
    return (24 if peers <= 8 else 60) * 2**20


def ring_order(peers):
    width = 1
    while 8 * width * width <= peers:
        width *= 2
    depth = peers // width
    if width == 1 or depth % 2:
        return list(range(peers))
    order = [z * width for z in range(depth)]
    for back, z in enumerate(reversed(range(depth))):
        columns = list(range(1, width))
        order += [z * width + x for x in (columns if back % 2 == 0 else reversed(columns))]
    return order


def ring_shift(value, by, sections=0):
    peers, layers = lax.axis_size("exp"), lax.axis_size("section")
    order = ring_order(peers)
    pairs = []
    for rep in range(lax.axis_size("rep")):
        step = by if rep % 2 == 0 else -by
        for layer in range(layers):
            source = (rep * layers + layer) * peers
            target = (rep * layers + (layer + sections) % layers) * peers
            for spot in range(peers):
                pairs.append((source + order[spot], target + order[(spot + step) % peers]))
    return lax.ppermute(value, ("rep", "section", "exp"), pairs)


def from_behind(value, axis, by):
    peers = lax.axis_size(axis)
    return lax.ppermute(value, axis, [(i, (i + by) % peers) for i in range(peers)])


def dot(a, b, dims):
    return lax.dot_general(a, b, (dims, ((), ())), preferred_element_type=F32)


def whole():
    return pl.BlockSpec(memory_space=pltpu.VMEM)


def turned(value):
    rows, columns = value.shape
    wide = jnp.concatenate([value, jnp.zeros((rows, 128 - columns), F32)], axis=1)
    return wide.T[:columns]


def pack_kernel(experts, codes_ref, exps_ref, routes_ref, weight_ref, grad_ref, out_ref):
    tokens, width = codes_ref.shape
    blocks = exps_ref.shape[0]
    scales = jnp.exp2(exps_ref[...].astype(F32))
    scales = turned(jnp.concatenate([scales, jnp.zeros((128 - blocks, tokens), F32)], axis=0))
    per = width // blocks
    for b in range(blocks):
        cols = slice(b * per, (b + 1) * per)
        out_ref[:, cols] = (codes_ref[:, cols].astype(F32) * scales[:, b : b + 1]).astype(BF16)
    expert = lax.broadcasted_iota(jnp.int32, (experts, tokens), 0)
    table = jnp.zeros((experts, tokens), F32)
    for k in range(routes_ref.shape[0]):
        table += jnp.where(routes_ref[k : k + 1, :] == expert, weight_ref[k : k + 1, :], 0.0)
    high = table.astype(BF16).astype(F32)
    middle = (table - high).astype(BF16).astype(F32)
    low = table - high - middle
    out_ref[:, width : 2 * width] = grad_ref[...]
    extra = out_ref.shape[1] - 2 * width
    parts = [high, middle, low]
    if extra > 3 * experts:
        parts.append(jnp.zeros((extra - 3 * experts, tokens), F32))
    out_ref[:, 2 * width :] = turned(jnp.concatenate(parts, axis=0)).astype(BF16)


LAST = ((1,), (1,))
PLAIN = ((1,), (0,))
TILE = 256


def columns_of(width, body):
    def step(n, carry):
        body(n * TILE)
        return carry

    lax.fori_loop(0, width // TILE, step, 0, unroll=2)


def span(start):
    return pl.ds(pl.multiple_of(start, TILE), TILE)


def load_kernel(*refs):
    count = len(refs) // 2
    copies = [
        pltpu.make_async_copy(refs[i], refs[count + i], refs[-1].at[i]) for i in range(count)
    ]
    for copy in copies:
        copy.start()
    for copy in copies:
        copy.wait()


def load_call(weights):
    return pl.pallas_call(
        load_kernel,
        out_shape=[jax.ShapeDtypeStruct(w.shape, w.dtype) for w in weights],
        in_specs=[pl.BlockSpec(memory_space=pl.ANY)] * len(weights),
        out_specs=[whole()] * len(weights),
        scratch_shapes=[pltpu.SemaphoreType.DMA((len(weights),))],
        compiler_params=pltpu.CompilerParams(vmem_limit_bytes=8 * 2**20),
        cost_estimate=pl.CostEstimate(
            flops=0, bytes_accessed=sum(4 * w.size for w in weights), transcendentals=0
        ),
        name="load_weights",
    )(*weights)


def expert_kernel(count, experts, local_experts, first_ref, *refs):
    blocks = refs[:count]
    weights = refs[count : count + 6]
    outs = refs[count + 6 : 2 * count + 6]
    saved = refs[2 * count + 6 : 2 * count + 9]
    rows, left = refs[2 * count + 9 :]
    half, width = weights[0].shape
    tokens = blocks[0].shape[0]
    tables = []
    for i, block in enumerate(blocks):
        rows[0, i * tokens : (i + 1) * tokens] = block[:, :width]
        rows[1, i * tokens : (i + 1) * tokens] = block[:, width : 2 * width]
        tables.append(block[:, 2 * width :].astype(F32))
    table = jnp.concatenate(tables, axis=0).T
    expert_of = lax.rem(lax.broadcasted_iota(jnp.int32, table.shape, 0), experts)
    scales = [
        jnp.sum(jnp.where(expert_of == first_ref[0] + e, table, 0.0), axis=0, keepdims=True)
        for e in range(local_experts)
    ]
    unit = lax.broadcasted_iota(jnp.int32, (half, 1), 0)
    scale = scales[0]
    for e in range(1, local_experts):
        scale = jnp.where(unit >= e * (half // local_experts), scales[e], scale)
    for side in range(2):
        at = slice(side * half, (side + 1) * half)
        gate = dot(weights[3 * side][...], rows[0], LAST)
        up = dot(weights[3 * side + 1][...], rows[0], LAST)
        back = dot(weights[3 * side + 2][...], rows[1], LAST) * scale
        sig = 1.0 / (1.0 + jnp.exp(-gate))
        swish = gate * sig
        results = (
            back * up * sig * (1.0 + gate * (1.0 - sig)),
            back * swish,
            swish * up * scale,
        )
        for kind, result in enumerate(results):
            result = result.astype(BF16)
            saved[kind][at, :] = result
            left[kind, :, at] = result.T

    def column(start):
        at, later = span(start), span(width + start)
        right = [
            jnp.concatenate([weights[kind][:, at], weights[3 + kind][:, at]], axis=0)
            for kind in range(3)
        ]
        output = dot(left[2], right[2], PLAIN).astype(BF16)
        grad = (dot(left[0], right[0], PLAIN) + dot(left[1], right[1], PLAIN)).astype(BF16)
        for i, out in enumerate(outs):
            out[:, at] = output[i * tokens : (i + 1) * tokens]
            out[:, later] = grad[i * tokens : (i + 1) * tokens]

    columns_of(width, column)


def expert_call(blocks, weights, first, experts, local_experts):
    count, tokens = len(blocks), blocks[0].shape[0]
    half, width = weights[0].shape
    units, rows = 2 * half, count * tokens
    results = pl.pallas_call(
        functools.partial(expert_kernel, count, experts, local_experts),
        out_shape=[jax.ShapeDtypeStruct((tokens, 2 * width), BF16)] * count
        + [jax.ShapeDtypeStruct((units, rows), BF16)] * 3,
        in_specs=[pl.BlockSpec(memory_space=pltpu.SMEM)] + [whole()] * (count + 6),
        out_specs=[whole()] * (count + 3),
        scratch_shapes=[
            pltpu.VMEM((2, rows, width), BF16),
            pltpu.VMEM((3, rows, units), BF16),
        ],
        compiler_params=pltpu.CompilerParams(vmem_limit_bytes=vmem(experts // local_experts)),
        cost_estimate=pl.CostEstimate(
            flops=6 * 2 * rows * units * width,
            bytes_accessed=6 * units * width + 8 * rows * width,
            transcendentals=rows * units,
        ),
        name="expert_rows",
    )(first, *blocks, *weights)
    return results[:count], results[count:]


def weight_kernel(groups, count, *refs):
    blocks = refs[:count]
    kept = [refs[count + g * 3 : count + g * 3 + 3] for g in range(groups)]
    outs, across = refs[-7:-1], refs[-1]
    half, width = outs[0].shape
    for kind in range(3):
        start = 0
        for group in kept:
            size = group[kind].shape[1]
            across[kind, :, start : start + size] = group[kind][...]
            start += size

    def column(start):
        at, later = span(start), span(width + start)
        right = [
            jnp.concatenate([b[:, at] for b in blocks], axis=0),
            jnp.concatenate([b[:, later] for b in blocks], axis=0),
        ]
        for kind in range(3):
            total = dot(across[kind], right[kind // 2], PLAIN).astype(BF16)
            outs[kind][:, at] = total[:half]
            outs[3 + kind][:, at] = total[half:]

    columns_of(width, column)


def weight_call(blocks, kept, width, peers):
    count = len(blocks)
    units = kept[0][0].shape[0]
    half, total = units // 2, count * blocks[0].shape[0]
    results = pl.pallas_call(
        functools.partial(weight_kernel, len(kept), count),
        out_shape=[jax.ShapeDtypeStruct((half, width), BF16)] * 6,
        in_specs=[whole()] * (count + 3 * len(kept)),
        out_specs=[whole()] * 6,
        scratch_shapes=[pltpu.VMEM((3, units, total), BF16)],
        compiler_params=pltpu.CompilerParams(vmem_limit_bytes=vmem(peers)),
        cost_estimate=pl.CostEstimate(
            flops=3 * 2 * total * units * width,
            bytes_accessed=4 * total * width + 12 * half * width,
            transcendentals=0,
        ),
        name="weight_grads",
    )(*blocks, *[k for group in kept for k in group])
    return results[:3], results[3:]


def add(a, b):
    return (a.astype(F32) + b.astype(F32)).astype(BF16)


def shards(
    row_codes, block_exponents, routes, route_weight, out_grad, gate_weight, up_weight, down_weight
):
    tokens, width = row_codes.shape[1:]
    local_experts, half_units = gate_weight.shape[1:3]
    half = local_experts * half_units
    peers = lax.axis_size("exp")
    experts = peers * local_experts
    lanes = -(-3 * experts // 128) * 128
    shards_of = [w.reshape(half, width) for w in (gate_weight, up_weight, down_weight)]
    other = [from_behind(w, "rep", 1) for w in shards_of]
    own = load_call(shards_of[:1]) + load_call(shards_of[1:])
    weights = list(own) + other
    first = (lax.axis_index("exp") * local_experts).astype(jnp.int32).reshape(1)
    home = pl.pallas_call(
        functools.partial(pack_kernel, experts),
        out_shape=jax.ShapeDtypeStruct((tokens, 2 * width + lanes), BF16),
        in_specs=[whole()] * 5,
        out_specs=whole(),
        compiler_params=pltpu.CompilerParams(vmem_limit_bytes=8 * 2**20),
        name="pack_rows",
    )(row_codes[0], block_exponents[0].T, routes[0].T, route_weight[0].T, out_grad[0])

    tie = lax.optimization_barrier
    ahead, behind = peers // 2, peers // 2 - 1
    names = [("near", 0)]
    for k in range(1, ahead + 1):
        names += [("near", k), ("far", k)]
    names = names[: 2 * ahead]
    groups = [names[i : i + 4] for i in range(0, len(names) - 4, 4)]
    groups.append([name for name in names[-4:] if name[0] == "far"])
    groups.append([name for name in names[-4:] if name[0] == "near"])
    held = {("near", 0): home, ("far", 0): tie((home, own[0]))[0]}
    partial, kept = {}, []

    def work(group):
        outs, saved = expert_call(
            [held[name] for name in group], weights, first, experts, local_experts
        )
        partial.update(zip(group, outs))
        kept.append(saved)

    for k in range(1, ahead + 1):
        held["near", k] = ring_shift(held["near", k - 1], 1)
        if k <= behind:
            held["far", k] = ring_shift(held["far", k - 1], -1)
        if k == 1:
            held["near", 1], own = tie((held["near", 1], own))
            weights[:3] = own
        if k % 2 == 1 and k > 1:
            work(groups[(k - 3) // 2])
            held["near", k], kept[-1] = tie((held["near", k], kept[-1]))
    work(groups[-2])
    far_sum = ring_shift(partial["far", behind], 1)
    held["near", ahead], kept[-1] = tie((held["near", ahead], kept[-1]))
    work(groups[-1])
    both = (slice(0, width), slice(width, 2 * width))
    near_sum = partial["near", ahead]
    own_total = other_total = None
    blocks = [held[name] for group in groups for name in group]
    steps = (1, -1)
    finals = []
    for part, step in zip(both, steps):
        kept_here = add(home[:, part], partial["near", 0][:, part])
        finals.append([from_behind(kept_here, "section", step)])
    for k in range(ahead, 1, -1):
        near_sum = ring_shift(near_sum, -1)
        left = k - 2
        if left > 1:
            far_done = far_sum
            far_sum = ring_shift(add(far_sum, partial["far", left]), 1)
            near_sum, _ = tie((near_sum, far_done))
        if k == 3:
            own_total, other_total = weight_call(blocks, kept, width, peers)
            here = [final[0] for final in finals]
            near_sum, own_total, other_total, _ = tie((near_sum, own_total, other_total, here))
            near_sum = add(near_sum, partial["near", 2])
            for final, part, step in zip(finals, both, steps):
                last = add(far_sum[:, part], partial["far", 1][:, part])
                final.append(ring_shift(last, 1, step))
        elif k == 2:
            here = [final[1] for final in finals]
            near_sum, other_total, _ = tie((near_sum, other_total, here))
        else:
            near_sum = add(near_sum, partial["near", k - 1])
    for final, part, step in zip(finals, both, steps):
        final.append(ring_shift(add(near_sum[:, part], partial["near", 1][:, part]), -1, step))
    received = [from_behind(g, "rep", 1) for g in other_total]
    totals = [add(a, b) for a, b in zip(own_total, received)]
    results = []
    for final in finals:
        if results:
            final, _ = tie((final, results[0]))
        results.append(sum(f.astype(F32) for f in final).astype(BF16)[None])
    shape = (1, local_experts, half_units, width)
    return tuple(results) + tuple(t.reshape(shape) for t in totals)


def solution(mesh):
    tokens = P("section", ("rep", "exp"), None)
    weights = P("section", "exp", "rep", None)
    return jax.shard_map(
        shards,
        mesh=mesh,
        in_specs=(tokens,) * 5 + (weights,) * 3,
        out_specs=(tokens,) * 2 + (weights,) * 3,
        check_vma=False,
    )
```

```python
import functools
import jax
import jax.numpy as jnp
from jax import lax
from jax.experimental import pallas as pl
from jax.experimental.pallas import tpu as pltpu
from jax.sharding import PartitionSpec as P

F32 = jnp.float32
BF16 = jnp.bfloat16


def vmem(peers):
    return (24 if peers <= 8 else 60) * 2**20


def ring_order(peers):
    width = 1
    while 8 * width * width <= peers:
        width *= 2
    depth = peers // width
    if width == 1 or depth % 2:
        return list(range(peers))
    order = [z * width for z in range(depth)]
    for back, z in enumerate(reversed(range(depth))):
        columns = list(range(1, width))
        order += [z * width + x for x in (columns if back % 2 == 0 else reversed(columns))]
    return order


def ring_shift(value, by, sections=0):
    peers, layers = lax.axis_size("exp"), lax.axis_size("section")
    order = ring_order(peers)
    pairs = []
    for rep in range(lax.axis_size("rep")):
        step = by if rep % 2 == 0 else -by
        for layer in range(layers):
            source = (rep * layers + layer) * peers
            target = (rep * layers + (layer + sections) % layers) * peers
            for spot in range(peers):
                pairs.append((source + order[spot], target + order[(spot + step) % peers]))
    return lax.ppermute(value, ("rep", "section", "exp"), pairs)


def from_behind(value, axis, by):
    peers = lax.axis_size(axis)
    return lax.ppermute(value, axis, [(i, (i + by) % peers) for i in range(peers)])


def dot(a, b, dims):
    return lax.dot_general(a, b, (dims, ((), ())), preferred_element_type=F32)


def whole():
    return pl.BlockSpec(memory_space=pltpu.VMEM)


def turned(value):
    rows, columns = value.shape
    wide = jnp.concatenate([value, jnp.zeros((rows, 128 - columns), F32)], axis=1)
    return wide.T[:columns]


def pack_kernel(experts, codes_ref, exps_ref, routes_ref, weight_ref, grad_ref, out_ref):
    tokens, width = codes_ref.shape
    blocks = exps_ref.shape[0]
    scales = jnp.exp2(exps_ref[...].astype(F32))
    scales = turned(jnp.concatenate([scales, jnp.zeros((128 - blocks, tokens), F32)], axis=0))
    per = width // blocks
    for b in range(blocks):
        cols = slice(b * per, (b + 1) * per)
        out_ref[:, cols] = (codes_ref[:, cols].astype(F32) * scales[:, b : b + 1]).astype(BF16)
    expert = lax.broadcasted_iota(jnp.int32, (experts, tokens), 0)
    table = jnp.zeros((experts, tokens), F32)
    for k in range(routes_ref.shape[0]):
        table += jnp.where(routes_ref[k : k + 1, :] == expert, weight_ref[k : k + 1, :], 0.0)
    high = table.astype(BF16).astype(F32)
    middle = (table - high).astype(BF16).astype(F32)
    low = table - high - middle
    out_ref[:, width : 2 * width] = grad_ref[...]
    extra = out_ref.shape[1] - 2 * width
    parts = [high, middle, low]
    if extra > 3 * experts:
        parts.append(jnp.zeros((extra - 3 * experts, tokens), F32))
    out_ref[:, 2 * width :] = turned(jnp.concatenate(parts, axis=0)).astype(BF16)


LAST = ((1,), (1,))
PLAIN = ((1,), (0,))
TILE = 256


def columns_of(width, body):
    def step(n, carry):
        body(n * TILE)
        return carry

    lax.fori_loop(0, width // TILE, step, 0, unroll=2)


def span(start):
    return pl.ds(pl.multiple_of(start, TILE), TILE)


def load_kernel(*refs):
    count = len(refs) // 2
    copies = [
        pltpu.make_async_copy(refs[i], refs[count + i], refs[-1].at[i]) for i in range(count)
    ]
    for copy in copies:
        copy.start()
    for copy in copies:
        copy.wait()


def load_call(weights):
    return pl.pallas_call(
        load_kernel,
        out_shape=[jax.ShapeDtypeStruct(w.shape, w.dtype) for w in weights],
        in_specs=[pl.BlockSpec(memory_space=pl.ANY)] * len(weights),
        out_specs=[whole()] * len(weights),
        scratch_shapes=[pltpu.SemaphoreType.DMA((len(weights),))],
        compiler_params=pltpu.CompilerParams(vmem_limit_bytes=8 * 2**20),
        cost_estimate=pl.CostEstimate(
            flops=0, bytes_accessed=sum(4 * w.size for w in weights), transcendentals=0
        ),
        name="load_weights",
    )(*weights)


def expert_kernel(count, experts, local_experts, *refs):
    blocks = refs[:count]
    weights = refs[count : count + 6]
    outs = refs[count + 6 : 2 * count + 6]
    saved = refs[2 * count + 6 : 2 * count + 9]
    rows, left = refs[2 * count + 9 :]
    half, width = weights[0].shape
    tokens = blocks[0].shape[0]
    tables = []
    for i, block in enumerate(blocks):
        rows[0, i * tokens : (i + 1) * tokens] = block[:, :width]
        rows[1, i * tokens : (i + 1) * tokens] = block[:, width : 2 * width]
        tables.append(block[:, 2 * width :].astype(F32))
    table = jnp.concatenate(tables, axis=0).T
    expert_of = lax.rem(lax.broadcasted_iota(jnp.int32, table.shape, 0), experts)
    first = lax.axis_index("exp") * local_experts
    scales = [
        jnp.sum(jnp.where(expert_of == first + e, table, 0.0), axis=0, keepdims=True)
        for e in range(local_experts)
    ]
    unit = lax.broadcasted_iota(jnp.int32, (half, 1), 0)
    scale = scales[0]
    for e in range(1, local_experts):
        scale = jnp.where(unit >= e * (half // local_experts), scales[e], scale)
    for side in range(2):
        at = slice(side * half, (side + 1) * half)
        gate = dot(weights[3 * side][...], rows[0], LAST)
        up = dot(weights[3 * side + 1][...], rows[0], LAST)
        back = dot(weights[3 * side + 2][...], rows[1], LAST) * scale
        sig = 1.0 / (1.0 + jnp.exp(-gate))
        swish = gate * sig
        results = (
            back * up * sig * (1.0 + gate * (1.0 - sig)),
            back * swish,
            swish * up * scale,
        )
        for kind, result in enumerate(results):
            result = result.astype(BF16)
            saved[kind][at, :] = result
            left[kind, :, at] = result.T

    def column(start):
        at, later = span(start), span(width + start)
        right = [
            jnp.concatenate([weights[kind][:, at], weights[3 + kind][:, at]], axis=0)
            for kind in range(3)
        ]
        output = dot(left[2], right[2], PLAIN).astype(BF16)
        grad = (dot(left[0], right[0], PLAIN) + dot(left[1], right[1], PLAIN)).astype(BF16)
        for i, out in enumerate(outs):
            out[:, at] = output[i * tokens : (i + 1) * tokens]
            out[:, later] = grad[i * tokens : (i + 1) * tokens]

    columns_of(width, column)


def expert_call(blocks, weights, experts, local_experts):
    count, tokens = len(blocks), blocks[0].shape[0]
    half, width = weights[0].shape
    units, rows = 2 * half, count * tokens
    results = pl.pallas_call(
        functools.partial(expert_kernel, count, experts, local_experts),
        out_shape=[jax.ShapeDtypeStruct((tokens, 2 * width), BF16)] * count
        + [jax.ShapeDtypeStruct((units, rows), BF16)] * 3,
        in_specs=[whole()] * (count + 6),
        out_specs=[whole()] * (count + 3),
        scratch_shapes=[
            pltpu.VMEM((2, rows, width), BF16),
            pltpu.VMEM((3, rows, units), BF16),
        ],
        compiler_params=pltpu.CompilerParams(vmem_limit_bytes=vmem(experts // local_experts)),
        cost_estimate=pl.CostEstimate(
            flops=6 * 2 * rows * units * width,
            bytes_accessed=6 * units * width + 8 * rows * width,
            transcendentals=rows * units,
        ),
        name="expert_rows",
    )(*blocks, *weights)
    return results[:count], results[count:]


def weight_kernel(groups, count, *refs):
    blocks = refs[:count]
    kept = [refs[count + g * 3 : count + g * 3 + 3] for g in range(groups)]
    outs, across = refs[-7:-1], refs[-1]
    half, width = outs[0].shape
    for kind in range(3):
        start = 0
        for group in kept:
            size = group[kind].shape[1]
            across[kind, :, start : start + size] = group[kind][...]
            start += size

    def column(start):
        at, later = span(start), span(width + start)
        right = [
            jnp.concatenate([b[:, at] for b in blocks], axis=0),
            jnp.concatenate([b[:, later] for b in blocks], axis=0),
        ]
        for kind in range(3):
            total = dot(across[kind], right[kind // 2], PLAIN).astype(BF16)
            outs[kind][:, at] = total[:half]
            outs[3 + kind][:, at] = total[half:]

    columns_of(width, column)


def weight_call(blocks, kept, width, peers):
    count = len(blocks)
    units = kept[0][0].shape[0]
    half, total = units // 2, count * blocks[0].shape[0]
    results = pl.pallas_call(
        functools.partial(weight_kernel, len(kept), count),
        out_shape=[jax.ShapeDtypeStruct((half, width), BF16)] * 6,
        in_specs=[whole()] * (count + 3 * len(kept)),
        out_specs=[whole()] * 6,
        scratch_shapes=[pltpu.VMEM((3, units, total), BF16)],
        compiler_params=pltpu.CompilerParams(vmem_limit_bytes=vmem(peers)),
        cost_estimate=pl.CostEstimate(
            flops=3 * 2 * total * units * width,
            bytes_accessed=4 * total * width + 12 * half * width,
            transcendentals=0,
        ),
        name="weight_grads",
    )(*blocks, *[k for group in kept for k in group])
    return results[:3], results[3:]


def add(a, b):
    return (a.astype(F32) + b.astype(F32)).astype(BF16)


def shards(
    row_codes, block_exponents, routes, route_weight, out_grad, gate_weight, up_weight, down_weight
):
    tokens, width = row_codes.shape[1:]
    local_experts, half_units = gate_weight.shape[1:3]
    half = local_experts * half_units
    peers = lax.axis_size("exp")
    experts = peers * local_experts
    lanes = -(-3 * experts // 128) * 128
    shards_of = [w.reshape(half, width) for w in (gate_weight, up_weight, down_weight)]
    other = [from_behind(w, "rep", 1) for w in shards_of]
    home = pl.pallas_call(
        functools.partial(pack_kernel, experts),
        out_shape=jax.ShapeDtypeStruct((tokens, 2 * width + lanes), BF16),
        in_specs=[whole()] * 5,
        out_specs=whole(),
        compiler_params=pltpu.CompilerParams(vmem_limit_bytes=60 * 2**20),
        name="pack_rows",
    )(row_codes[0], block_exponents[0].T, routes[0].T, route_weight[0].T, out_grad[0])

    tie = lax.optimization_barrier
    shards_of = tie((home, shards_of))[1]
    own = load_call(shards_of[:1]) + load_call(shards_of[1:])
    weights = list(own) + other
    ahead, behind = peers // 2, peers // 2 - 1
    names = [("near", 0)]
    for k in range(1, ahead + 1):
        names += [("near", k), ("far", k)]
    names = names[: 2 * ahead]
    groups = [names[i : i + 4] for i in range(0, len(names) - 4, 4)]
    groups.append([name for name in names[-4:] if name[0] == "far"])
    groups.append([name for name in names[-4:] if name[0] == "near"])
    held = {("near", 0): home, ("far", 0): tie((home, own[0]))[0]}
    partial, kept = {}, []

    def work(group):
        outs, saved = expert_call(
            [held[name] for name in group], weights, experts, local_experts
        )
        partial.update(zip(group, outs))
        kept.append(saved)

    for k in range(1, ahead + 1):
        held["near", k] = ring_shift(held["near", k - 1], 1)
        if k <= behind:
            held["far", k] = ring_shift(held["far", k - 1], -1)
        if k == 1:
            held["near", 1], own = tie((held["near", 1], own))
            weights[:3] = own
        if k % 2 == 1 and k > 1:
            work(groups[(k - 3) // 2])
            held["near", k], kept[-1] = tie((held["near", k], kept[-1]))
    work(groups[-2])
    far_sum = ring_shift(partial["far", behind], 1)
    held["near", ahead], kept[-1] = tie((held["near", ahead], kept[-1]))
    work(groups[-1])
    both = (slice(0, width), slice(width, 2 * width))
    near_sum = partial["near", ahead]
    own_total = received = None
    blocks = [held[name] for group in groups for name in group]
    steps = (1, -1)
    finals = []
    for part, step in zip(both, steps):
        kept_here = add(home[:, part], partial["near", 0][:, part])
        finals.append([from_behind(kept_here, "section", step)])
    for k in range(ahead, 1, -1):
        near_sum = ring_shift(near_sum, -1)
        left = k - 2
        if left > 1:
            far_done = far_sum
            far_sum = ring_shift(add(far_sum, partial["far", left]), 1)
            near_sum, _ = tie((near_sum, far_done))
        if k == 3:
            own_total, other_total = weight_call(blocks, kept, width, peers)
            here = [final[0] for final in finals]
            near_sum, own_total, other_total, _ = tie((near_sum, own_total, other_total, here))
            near_sum = add(near_sum, partial["near", 2])
            lasts = [add(far_sum[:, part], partial["far", 1][:, part]) for part in both]
            near_sum, lasts = tie((near_sum, lasts))
            for final, last, step in zip(finals, lasts, steps):
                final.append(ring_shift(last, 1, step))
        elif k == 2:
            here = [final[1] for final in finals]
            near_sum, other_total, _ = tie((near_sum, other_total, here))
            received = [from_behind(g, "rep", 1) for g in other_total]
        elif k > 2:
            near_sum = add(near_sum, partial["near", k - 1])
    lasts = [add(near_sum[:, part], partial["near", 1][:, part]) for part in both]
    for final, last, step in zip(finals, lasts, steps):
        final.append(ring_shift(last, -1, step))
    totals = [add(a, b) for a, b in zip(own_total, received)]
    finals, totals = tie((finals, totals))
    results = [sum(f.astype(F32) for f in final).astype(BF16)[None] for final in finals]
    shape = (1, local_experts, half_units, width)
    return tuple(results) + tuple(t.reshape(shape) for t in totals)


def solution(mesh):
    tokens = P("section", ("rep", "exp"), None)
    weights = P("section", "exp", "rep", None)
    return jax.shard_map(
        shards,
        mesh=mesh,
        in_specs=(tokens,) * 5 + (weights,) * 3,
        out_specs=(tokens,) * 2 + (weights,) * 3,
        check_vma=False,
    )
```

```python
import functools
import jax
import jax.numpy as jnp
from jax import lax
from jax.experimental import pallas as pl
from jax.experimental.pallas import tpu as pltpu
from jax.sharding import PartitionSpec as P

F32 = jnp.float32
BF16 = jnp.bfloat16


def vmem(peers):
    return (24 if peers <= 8 else 60) * 2**20


def ring_order(peers):
    width = 1
    while 8 * width * width <= peers:
        width *= 2
    depth = peers // width
    if width == 1 or depth % 2:
        return list(range(peers))
    order = [z * width for z in range(depth)]
    for back, z in enumerate(reversed(range(depth))):
        columns = list(range(1, width))
        order += [z * width + x for x in (columns if back % 2 == 0 else reversed(columns))]
    return order


def ring_shift(value, by, sections=0):
    peers, layers = lax.axis_size("exp"), lax.axis_size("section")
    order = ring_order(peers)
    pairs = []
    for rep in range(lax.axis_size("rep")):
        step = by if rep % 2 == 0 else -by
        for layer in range(layers):
            source = (rep * layers + layer) * peers
            target = (rep * layers + (layer + sections) % layers) * peers
            for spot in range(peers):
                pairs.append((source + order[spot], target + order[(spot + step) % peers]))
    return lax.ppermute(value, ("rep", "section", "exp"), pairs)


def from_behind(value, axis, by):
    peers = lax.axis_size(axis)
    return lax.ppermute(value, axis, [(i, (i + by) % peers) for i in range(peers)])


def dot(a, b, dims):
    return lax.dot_general(a, b, (dims, ((), ())), preferred_element_type=F32)


def whole():
    return pl.BlockSpec(memory_space=pltpu.VMEM)


def turned(value):
    rows, columns = value.shape
    wide = jnp.concatenate([value, jnp.zeros((rows, 128 - columns), F32)], axis=1)
    return wide.T[:columns]


def pack_kernel(experts, codes_ref, exps_ref, routes_ref, weight_ref, grad_ref, out_ref):
    tokens, width = codes_ref.shape
    blocks = exps_ref.shape[0]
    scales = jnp.exp2(exps_ref[...].astype(F32))
    scales = turned(jnp.concatenate([scales, jnp.zeros((128 - blocks, tokens), F32)], axis=0))
    per = width // blocks
    for b in range(blocks):
        cols = slice(b * per, (b + 1) * per)
        out_ref[:, cols] = (codes_ref[:, cols].astype(F32) * scales[:, b : b + 1]).astype(BF16)
    expert = lax.broadcasted_iota(jnp.int32, (experts, tokens), 0)
    table = jnp.zeros((experts, tokens), F32)
    for k in range(routes_ref.shape[0]):
        table += jnp.where(routes_ref[k : k + 1, :] == expert, weight_ref[k : k + 1, :], 0.0)
    high = table.astype(BF16).astype(F32)
    middle = (table - high).astype(BF16).astype(F32)
    low = table - high - middle
    out_ref[:, width : 2 * width] = grad_ref[...]
    extra = out_ref.shape[1] - 2 * width
    parts = [high, middle, low]
    if extra > 3 * experts:
        parts.append(jnp.zeros((extra - 3 * experts, tokens), F32))
    out_ref[:, 2 * width :] = turned(jnp.concatenate(parts, axis=0)).astype(BF16)


LAST = ((1,), (1,))
PLAIN = ((1,), (0,))
TILE = 256


def columns_of(width, body):
    def step(n, carry):
        body(n * TILE)
        return carry

    lax.fori_loop(0, width // TILE, step, 0, unroll=2)


def span(start):
    return pl.ds(pl.multiple_of(start, TILE), TILE)


def load_kernel(*refs):
    count = len(refs) // 2
    copies = [
        pltpu.make_async_copy(refs[i], refs[count + i], refs[-1].at[i]) for i in range(count)
    ]
    for copy in copies:
        copy.start()
    for copy in copies:
        copy.wait()


def load_call(weights):
    return pl.pallas_call(
        load_kernel,
        out_shape=[jax.ShapeDtypeStruct(w.shape, w.dtype) for w in weights],
        in_specs=[pl.BlockSpec(memory_space=pl.ANY)] * len(weights),
        out_specs=[whole()] * len(weights),
        scratch_shapes=[pltpu.SemaphoreType.DMA((len(weights),))],
        compiler_params=pltpu.CompilerParams(vmem_limit_bytes=8 * 2**20),
        cost_estimate=pl.CostEstimate(
            flops=0, bytes_accessed=sum(4 * w.size for w in weights), transcendentals=0
        ),
        name="load_weights",
    )(*weights)


def expert_kernel(count, experts, local_experts, *refs):
    blocks = refs[:count]
    weights = refs[count : count + 6]
    outs = refs[count + 6 : 2 * count + 6]
    saved = refs[2 * count + 6 : 2 * count + 9]
    rows, left = refs[2 * count + 9 :]
    half, width = weights[0].shape
    tokens = blocks[0].shape[0]
    tables = []
    for i, block in enumerate(blocks):
        rows[0, i * tokens : (i + 1) * tokens] = block[:, :width]
        rows[1, i * tokens : (i + 1) * tokens] = block[:, width : 2 * width]
        tables.append(block[:, 2 * width :].astype(F32))
    table = jnp.concatenate(tables, axis=0).T
    expert_of = lax.rem(lax.broadcasted_iota(jnp.int32, table.shape, 0), experts)
    first = lax.axis_index("exp") * local_experts
    scales = [
        jnp.sum(jnp.where(expert_of == first + e, table, 0.0), axis=0, keepdims=True)
        for e in range(local_experts)
    ]
    unit = lax.broadcasted_iota(jnp.int32, (half, 1), 0)
    scale = scales[0]
    for e in range(1, local_experts):
        scale = jnp.where(unit >= e * (half // local_experts), scales[e], scale)
    for side in range(2):
        at = slice(side * half, (side + 1) * half)
        gate = dot(weights[3 * side][...], rows[0], LAST)
        up = dot(weights[3 * side + 1][...], rows[0], LAST)
        back = dot(weights[3 * side + 2][...], rows[1], LAST) * scale
        sig = 1.0 / (1.0 + jnp.exp(-gate))
        swish = gate * sig
        results = (
            back * up * sig * (1.0 + gate * (1.0 - sig)),
            back * swish,
            swish * up * scale,
        )
        for kind, result in enumerate(results):
            result = result.astype(BF16)
            saved[kind][at, :] = result
            left[kind, :, at] = result.T

    def column(start):
        at, later = span(start), span(width + start)
        right = [
            jnp.concatenate([weights[kind][:, at], weights[3 + kind][:, at]], axis=0)
            for kind in range(3)
        ]
        output = dot(left[2], right[2], PLAIN).astype(BF16)
        grad = (dot(left[0], right[0], PLAIN) + dot(left[1], right[1], PLAIN)).astype(BF16)
        for i, out in enumerate(outs):
            out[:, at] = output[i * tokens : (i + 1) * tokens]
            out[:, later] = grad[i * tokens : (i + 1) * tokens]

    columns_of(width, column)


def expert_call(blocks, weights, experts, local_experts):
    count, tokens = len(blocks), blocks[0].shape[0]
    half, width = weights[0].shape
    units, rows = 2 * half, count * tokens
    results = pl.pallas_call(
        functools.partial(expert_kernel, count, experts, local_experts),
        out_shape=[jax.ShapeDtypeStruct((tokens, 2 * width), BF16)] * count
        + [jax.ShapeDtypeStruct((units, rows), BF16)] * 3,
        in_specs=[whole()] * (count + 6),
        out_specs=[whole()] * (count + 3),
        scratch_shapes=[
            pltpu.VMEM((2, rows, width), BF16),
            pltpu.VMEM((3, rows, units), BF16),
        ],
        compiler_params=pltpu.CompilerParams(vmem_limit_bytes=vmem(experts // local_experts)),
        cost_estimate=pl.CostEstimate(
            flops=6 * 2 * rows * units * width,
            bytes_accessed=6 * units * width + 8 * rows * width,
            transcendentals=rows * units,
        ),
        name="expert_rows",
    )(*blocks, *weights)
    return results[:count], results[count:]


def weight_kernel(groups, count, *refs):
    blocks = refs[:count]
    kept = [refs[count + g * 3 : count + g * 3 + 3] for g in range(groups)]
    outs, across = refs[-7:-1], refs[-1]
    half, width = outs[0].shape
    for kind in range(3):
        start = 0
        for group in kept:
            size = group[kind].shape[1]
            across[kind, :, start : start + size] = group[kind][...]
            start += size

    def column(start):
        at, later = span(start), span(width + start)
        right = [
            jnp.concatenate([b[:, at] for b in blocks], axis=0),
            jnp.concatenate([b[:, later] for b in blocks], axis=0),
        ]
        for kind in range(3):
            total = dot(across[kind], right[kind // 2], PLAIN).astype(BF16)
            outs[kind][:, at] = total[:half]
            outs[3 + kind][:, at] = total[half:]

    columns_of(width, column)


def weight_call(blocks, kept, width, peers):
    count = len(blocks)
    units = kept[0][0].shape[0]
    half, total = units // 2, count * blocks[0].shape[0]
    results = pl.pallas_call(
        functools.partial(weight_kernel, len(kept), count),
        out_shape=[jax.ShapeDtypeStruct((half, width), BF16)] * 6,
        in_specs=[whole()] * (count + 3 * len(kept)),
        out_specs=[whole()] * 6,
        scratch_shapes=[pltpu.VMEM((3, units, total), BF16)],
        compiler_params=pltpu.CompilerParams(vmem_limit_bytes=vmem(peers)),
        cost_estimate=pl.CostEstimate(
            flops=3 * 2 * total * units * width,
            bytes_accessed=4 * total * width + 12 * half * width,
            transcendentals=0,
        ),
        name="weight_grads",
    )(*blocks, *[k for group in kept for k in group])
    return results[:3], results[3:]


def add(a, b):
    return (a.astype(F32) + b.astype(F32)).astype(BF16)


def shards(
    row_codes, block_exponents, routes, route_weight, out_grad, gate_weight, up_weight, down_weight
):
    tokens, width = row_codes.shape[1:]
    local_experts, half_units = gate_weight.shape[1:3]
    half = local_experts * half_units
    peers = lax.axis_size("exp")
    experts = peers * local_experts
    lanes = -(-3 * experts // 128) * 128
    shards_of = [w.reshape(half, width) for w in (gate_weight, up_weight, down_weight)]
    other = [from_behind(w, "rep", 1) for w in shards_of]
    home = pl.pallas_call(
        functools.partial(pack_kernel, experts),
        out_shape=jax.ShapeDtypeStruct((tokens, 2 * width + lanes), BF16),
        in_specs=[whole()] * 5,
        out_specs=whole(),
        compiler_params=pltpu.CompilerParams(vmem_limit_bytes=60 * 2**20),
        name="pack_rows",
    )(row_codes[0], block_exponents[0].T, routes[0].T, route_weight[0].T, out_grad[0])

    tie = lax.optimization_barrier
    shards_of = tie((home, shards_of))[1]
    own = load_call(shards_of[:1]) + load_call(shards_of[1:])
    weights = list(own) + other
    ahead, behind = peers // 2, peers // 2 - 1
    names = [("near", 0)]
    for k in range(1, ahead + 1):
        names += [("near", k), ("far", k)]
    names = names[: 2 * ahead]
    groups = [names[i : i + 4] for i in range(0, len(names) - 4, 4)]
    groups.append([name for name in names[-4:] if name[0] == "far"])
    groups.append([name for name in names[-4:] if name[0] == "near"])
    held = {("near", 0): home, ("far", 0): tie((home, own))[0]}
    partial, kept = {}, []

    def work(group):
        outs, saved = expert_call(
            [held[name] for name in group], weights, experts, local_experts
        )
        partial.update(zip(group, outs))
        kept.append(saved)

    for k in range(1, ahead + 1):
        held["near", k] = ring_shift(held["near", k - 1], 1)
        if k <= behind:
            held["far", k] = ring_shift(held["far", k - 1], -1)
        if k == 1:
            held["near", 1], own = tie((held["near", 1], own))
            weights[:3] = own
        if k % 2 == 1 and k > 1:
            work(groups[(k - 3) // 2])
            held["near", k], kept[-1] = tie((held["near", k], kept[-1]))
    work(groups[-2])
    far_sum = ring_shift(partial["far", behind], 1)
    held["near", ahead], kept[-1] = tie((held["near", ahead], kept[-1]))
    work(groups[-1])
    both = (slice(0, width), slice(width, 2 * width))
    near_sum = partial["near", ahead]
    own_total = received = None
    blocks = [held[name] for group in groups for name in group]
    steps = (1, -1)
    finals = []
    here, near_sum = tie((partial["near", 0], near_sum))
    for part, step in zip(both, steps):
        kept_here = add(home[:, part], here[:, part])
        finals.append([from_behind(kept_here, "section", step)])
    for k in range(ahead, 1, -1):
        near_sum = ring_shift(near_sum, -1)
        left = k - 2
        if left > 1:
            far_done = far_sum
            far_sum = ring_shift(add(far_sum, partial["far", left]), 1)
            near_sum, _ = tie((near_sum, far_done))
        if k == 3:
            own_total, other_total = weight_call(blocks, kept, width, peers)
            here = [final[0] for final in finals]
            near_sum, own_total, other_total, _ = tie((near_sum, own_total, other_total, here))
            lasts = [add(far_sum[:, part], partial["far", 1][:, part]) for part in both]
            for final, last, step in zip(finals, lasts, steps):
                final.append(ring_shift(last, 1, step))
            near_sum, _ = tie((near_sum, lasts))
            near_sum = add(near_sum, partial["near", 2])
        elif k == 2:
            here = [final[1] for final in finals]
            near_sum, other_total, _ = tie((near_sum, other_total, here))
            received = [from_behind(g, "rep", 1) for g in other_total]
        elif k > 2:
            near_sum = add(near_sum, partial["near", k - 1])
    lasts = [add(near_sum[:, part], partial["near", 1][:, part]) for part in both]
    for final, last, step in zip(finals, lasts, steps):
        final.append(ring_shift(last, -1, step))
    totals = [add(a, b) for a, b in zip(own_total, received)]
    finals, totals = tie((finals, totals))
    results = [sum(f.astype(F32) for f in final).astype(BF16)[None] for final in finals]
    shape = (1, local_experts, half_units, width)
    return tuple(results) + tuple(t.reshape(shape) for t in totals)


def solution(mesh):
    tokens = P("section", ("rep", "exp"), None)
    weights = P("section", "exp", "rep", None)
    return jax.shard_map(
        shards,
        mesh=mesh,
        in_specs=(tokens,) * 5 + (weights,) * 3,
        out_specs=(tokens,) * 2 + (weights,) * 3,
        check_vma=False,
    )
```

```python
import functools
import jax
import jax.numpy as jnp
from jax import lax
from jax.experimental import pallas as pl
from jax.experimental.pallas import tpu as pltpu
from jax.sharding import PartitionSpec as P

F32 = jnp.float32
BF16 = jnp.bfloat16


def vmem(peers):
    return (24 if peers <= 8 else 60) * 2**20


def ring_order(peers):
    width = 1
    while 8 * width * width <= peers:
        width *= 2
    depth = peers // width
    if width == 1 or depth % 2:
        return list(range(peers))
    order = [z * width for z in range(depth)]
    for back, z in enumerate(reversed(range(depth))):
        columns = list(range(1, width))
        order += [z * width + x for x in (columns if back % 2 == 0 else reversed(columns))]
    return order


def ring_shift(value, by, sections=0):
    peers, layers = lax.axis_size("exp"), lax.axis_size("section")
    order = ring_order(peers)
    pairs = []
    for rep in range(lax.axis_size("rep")):
        step = by if rep % 2 == 0 else -by
        for layer in range(layers):
            source = (rep * layers + layer) * peers
            target = (rep * layers + (layer + sections) % layers) * peers
            for spot in range(peers):
                pairs.append((source + order[spot], target + order[(spot + step) % peers]))
    return lax.ppermute(value, ("rep", "section", "exp"), pairs)


def from_behind(value, axis, by):
    peers = lax.axis_size(axis)
    return lax.ppermute(value, axis, [(i, (i + by) % peers) for i in range(peers)])


def dot(a, b, dims):
    return lax.dot_general(a, b, (dims, ((), ())), preferred_element_type=F32)


def whole():
    return pl.BlockSpec(memory_space=pltpu.VMEM)


def turned(value):
    rows, columns = value.shape
    wide = jnp.concatenate([value, jnp.zeros((rows, 128 - columns), F32)], axis=1)
    return wide.T[:columns]


def pack_kernel(experts, codes_ref, exps_ref, routes_ref, weight_ref, grad_ref, out_ref):
    tokens, width = codes_ref.shape
    blocks = exps_ref.shape[0]
    scales = jnp.exp2(exps_ref[...].astype(F32))
    scales = turned(jnp.concatenate([scales, jnp.zeros((128 - blocks, tokens), F32)], axis=0))
    per = width // blocks
    for b in range(blocks):
        cols = slice(b * per, (b + 1) * per)
        out_ref[:, cols] = (codes_ref[:, cols].astype(F32) * scales[:, b : b + 1]).astype(BF16)
    expert = lax.broadcasted_iota(jnp.int32, (experts, tokens), 0)
    table = jnp.zeros((experts, tokens), F32)
    for k in range(routes_ref.shape[0]):
        table += jnp.where(routes_ref[k : k + 1, :] == expert, weight_ref[k : k + 1, :], 0.0)
    high = table.astype(BF16).astype(F32)
    middle = (table - high).astype(BF16).astype(F32)
    low = table - high - middle
    out_ref[:, width : 2 * width] = grad_ref[...]
    extra = out_ref.shape[1] - 2 * width
    parts = [high, middle, low]
    if extra > 3 * experts:
        parts.append(jnp.zeros((extra - 3 * experts, tokens), F32))
    out_ref[:, 2 * width :] = turned(jnp.concatenate(parts, axis=0)).astype(BF16)


LAST = ((1,), (1,))
PLAIN = ((1,), (0,))
TILE = 256


def columns_of(width, body):
    def step(n, carry):
        body(n * TILE)
        return carry

    lax.fori_loop(0, width // TILE, step, 0, unroll=2)


def span(start):
    return pl.ds(pl.multiple_of(start, TILE), TILE)


def load_kernel(*refs):
    count = len(refs) // 2
    copies = [
        pltpu.make_async_copy(refs[i], refs[count + i], refs[-1].at[i]) for i in range(count)
    ]
    for copy in copies:
        copy.start()
    for copy in copies:
        copy.wait()


def load_call(weights):
    return pl.pallas_call(
        load_kernel,
        out_shape=[jax.ShapeDtypeStruct(w.shape, w.dtype) for w in weights],
        in_specs=[pl.BlockSpec(memory_space=pl.ANY)] * len(weights),
        out_specs=[whole()] * len(weights),
        scratch_shapes=[pltpu.SemaphoreType.DMA((len(weights),))],
        compiler_params=pltpu.CompilerParams(vmem_limit_bytes=8 * 2**20),
        cost_estimate=pl.CostEstimate(
            flops=0, bytes_accessed=sum(4 * w.size for w in weights), transcendentals=0
        ),
        name="load_weights",
    )(*weights)


def expert_kernel(count, experts, local_experts, *refs):
    blocks = refs[:count]
    weights = refs[count : count + 6]
    outs = refs[count + 6 : 2 * count + 6]
    saved = refs[2 * count + 6 : 2 * count + 9]
    rows, left = refs[2 * count + 9 :]
    half, width = weights[0].shape
    tokens = blocks[0].shape[0]
    tables = []
    for i, block in enumerate(blocks):
        rows[0, i * tokens : (i + 1) * tokens] = block[:, :width]
        rows[1, i * tokens : (i + 1) * tokens] = block[:, width : 2 * width]
        tables.append(block[:, 2 * width :].astype(F32))
    table = jnp.concatenate(tables, axis=0).T
    expert_of = lax.rem(lax.broadcasted_iota(jnp.int32, table.shape, 0), experts)
    first = lax.axis_index("exp") * local_experts
    scales = [
        jnp.sum(jnp.where(expert_of == first + e, table, 0.0), axis=0, keepdims=True)
        for e in range(local_experts)
    ]
    unit = lax.broadcasted_iota(jnp.int32, (half, 1), 0)
    scale = scales[0]
    for e in range(1, local_experts):
        scale = jnp.where(unit >= e * (half // local_experts), scales[e], scale)
    for side in range(2):
        at = slice(side * half, (side + 1) * half)
        gate = dot(weights[3 * side][...], rows[0], LAST)
        up = dot(weights[3 * side + 1][...], rows[0], LAST)
        back = dot(weights[3 * side + 2][...], rows[1], LAST) * scale
        sig = 1.0 / (1.0 + jnp.exp(-gate))
        swish = gate * sig
        results = (
            back * up * sig * (1.0 + gate * (1.0 - sig)),
            back * swish,
            swish * up * scale,
        )
        for kind, result in enumerate(results):
            result = result.astype(BF16)
            saved[kind][at, :] = result
            left[kind, :, at] = result.T

    def column(start):
        at, later = span(start), span(width + start)
        right = [
            jnp.concatenate([weights[kind][:, at], weights[3 + kind][:, at]], axis=0)
            for kind in range(3)
        ]
        output = dot(left[2], right[2], PLAIN).astype(BF16)
        grad = (dot(left[0], right[0], PLAIN) + dot(left[1], right[1], PLAIN)).astype(BF16)
        for i, out in enumerate(outs):
            out[:, at] = output[i * tokens : (i + 1) * tokens]
            out[:, later] = grad[i * tokens : (i + 1) * tokens]

    columns_of(width, column)


def expert_call(blocks, weights, experts, local_experts):
    count, tokens = len(blocks), blocks[0].shape[0]
    half, width = weights[0].shape
    units, rows = 2 * half, count * tokens
    results = pl.pallas_call(
        functools.partial(expert_kernel, count, experts, local_experts),
        out_shape=[jax.ShapeDtypeStruct((tokens, 2 * width), BF16)] * count
        + [jax.ShapeDtypeStruct((units, rows), BF16)] * 3,
        in_specs=[whole()] * (count + 6),
        out_specs=[whole()] * (count + 3),
        scratch_shapes=[
            pltpu.VMEM((2, rows, width), BF16),
            pltpu.VMEM((3, rows, units), BF16),
        ],
        compiler_params=pltpu.CompilerParams(vmem_limit_bytes=vmem(experts // local_experts)),
        cost_estimate=pl.CostEstimate(
            flops=6 * 2 * rows * units * width,
            bytes_accessed=6 * units * width + 8 * rows * width,
            transcendentals=rows * units,
        ),
        name="expert_rows",
    )(*blocks, *weights)
    return results[:count], results[count:]


def weight_kernel(groups, count, *refs):
    blocks = refs[:count]
    kept = [refs[count + g * 3 : count + g * 3 + 3] for g in range(groups)]
    outs, across = refs[-7:-1], refs[-1]
    half, width = outs[0].shape
    for kind in range(3):
        start = 0
        for group in kept:
            size = group[kind].shape[1]
            across[kind, :, start : start + size] = group[kind][...]
            start += size

    def column(start):
        at, later = span(start), span(width + start)
        right = [
            jnp.concatenate([b[:, at] for b in blocks], axis=0),
            jnp.concatenate([b[:, later] for b in blocks], axis=0),
        ]
        for kind in range(3):
            total = dot(across[kind], right[kind // 2], PLAIN).astype(BF16)
            outs[kind][:, at] = total[:half]
            outs[3 + kind][:, at] = total[half:]

    columns_of(width, column)


def weight_call(blocks, kept, width, peers):
    count = len(blocks)
    units = kept[0][0].shape[0]
    half, total = units // 2, count * blocks[0].shape[0]
    results = pl.pallas_call(
        functools.partial(weight_kernel, len(kept), count),
        out_shape=[jax.ShapeDtypeStruct((half, width), BF16)] * 6,
        in_specs=[whole()] * (count + 3 * len(kept)),
        out_specs=[whole()] * 6,
        scratch_shapes=[pltpu.VMEM((3, units, total), BF16)],
        compiler_params=pltpu.CompilerParams(vmem_limit_bytes=vmem(peers)),
        cost_estimate=pl.CostEstimate(
            flops=3 * 2 * total * units * width,
            bytes_accessed=4 * total * width + 12 * half * width,
            transcendentals=0,
        ),
        name="weight_grads",
    )(*blocks, *[k for group in kept for k in group])
    return results[:3], results[3:]


def add(a, b):
    return (a.astype(F32) + b.astype(F32)).astype(BF16)


def shards(
    row_codes, block_exponents, routes, route_weight, out_grad, gate_weight, up_weight, down_weight
):
    tokens, width = row_codes.shape[1:]
    local_experts, half_units = gate_weight.shape[1:3]
    half = local_experts * half_units
    peers = lax.axis_size("exp")
    experts = peers * local_experts
    lanes = -(-3 * experts // 128) * 128
    shards_of = [w.reshape(half, width) for w in (gate_weight, up_weight, down_weight)]
    other = [from_behind(w, "rep", 1) for w in shards_of]
    home = pl.pallas_call(
        functools.partial(pack_kernel, experts),
        out_shape=jax.ShapeDtypeStruct((tokens, 2 * width + lanes), BF16),
        in_specs=[whole()] * 5,
        out_specs=whole(),
        compiler_params=pltpu.CompilerParams(vmem_limit_bytes=60 * 2**20),
        name="pack_rows",
    )(row_codes[0], block_exponents[0].T, routes[0].T, route_weight[0].T, out_grad[0])

    tie = lax.optimization_barrier
    shards_of = tie((home, shards_of))[1]
    own = load_call(shards_of[:1]) + load_call(shards_of[1:])
    weights = list(own) + other
    ahead, behind = peers // 2, peers // 2 - 1
    names = [("near", 0)]
    for k in range(1, ahead + 1):
        names += [("near", k), ("far", k)]
    names = names[: 2 * ahead]
    groups = [names[i : i + 4] for i in range(0, len(names) - 4, 4)]
    groups.append([name for name in names[-4:] if name[0] == "far"])
    groups.append([name for name in names[-4:] if name[0] == "near"])
    held = {("near", 0): home, ("far", 0): tie((home, own))[0]}
    partial, kept = {}, []

    def work(group):
        outs, saved = expert_call(
            [held[name] for name in group], weights, experts, local_experts
        )
        partial.update(zip(group, outs))
        kept.append(saved)

    for k in range(1, ahead + 1):
        held["near", k] = ring_shift(held["near", k - 1], 1)
        if k <= behind:
            held["far", k] = ring_shift(held["far", k - 1], -1)
        if k == 1:
            held["near", 1], own = tie((held["near", 1], own))
            weights[:3] = own
        if k % 2 == 1 and k > 1:
            work(groups[(k - 3) // 2])
            held["near", k], kept[-1] = tie((held["near", k], kept[-1]))
    work(groups[-2])
    far_sum = ring_shift(partial["far", behind], 1)
    held["near", ahead], kept[-1] = tie((held["near", ahead], kept[-1]))
    work(groups[-1])
    both = (slice(0, width), slice(width, 2 * width))
    near_sum = partial["near", ahead]
    own_total = received = None
    blocks = [held[name] for group in groups for name in group]
    steps = (1, -1)
    finals = []
    here, near_sum = tie((partial["near", 0], near_sum))
    for part, step in zip(both, steps):
        kept_here = add(home[:, part], here[:, part])
        finals.append([from_behind(kept_here, "section", step)])
    for k in range(ahead, 1, -1):
        near_sum = ring_shift(near_sum, -1)
        left = k - 2
        if left > 1:
            far_done = far_sum
            far_sum = ring_shift(add(far_sum, partial["far", left]), 1)
            near_sum, _ = tie((near_sum, far_done))
        if k == 3:
            lasts = [add(far_sum[:, part], partial["far", 1][:, part]) for part in both]
            for final, last, step in zip(finals, lasts, steps):
                final.append(ring_shift(last, 1, step))
            kept[-1], _ = tie((kept[-1], lasts))
            own_total, other_total = weight_call(blocks, kept, width, peers)
            here = [final[0] for final in finals] + finals[0][1:]
            near_sum, own_total, other_total, _ = tie((near_sum, own_total, other_total, here))
            near_sum = add(near_sum, partial["near", 2])
            near_sum, other_total = tie((near_sum, other_total))
            received = [from_behind(g, "rep", 1) for g in other_total]
        elif k == 2:
            here = [final[1] for final in finals]
            near_sum, _ = tie((near_sum, here))
        elif k > 2:
            near_sum = add(near_sum, partial["near", k - 1])
    lasts = [add(near_sum[:, part], partial["near", 1][:, part]) for part in both]
    for final, last, step in zip(finals, lasts, steps):
        final.append(ring_shift(last, -1, step))
    totals = [add(a, b) for a, b in zip(own_total, received)]
    finals, totals = tie((finals, totals))
    results = [sum(f.astype(F32) for f in final).astype(BF16)[None] for final in finals]
    shape = (1, local_experts, half_units, width)
    return tuple(results) + tuple(t.reshape(shape) for t in totals)


def solution(mesh):
    tokens = P("section", ("rep", "exp"), None)
    weights = P("section", "exp", "rep", None)
    return jax.shard_map(
        shards,
        mesh=mesh,
        in_specs=(tokens,) * 5 + (weights,) * 3,
        out_specs=(tokens,) * 2 + (weights,) * 3,
        check_vma=False,
    )
```

```python
import functools
import jax
import jax.numpy as jnp
from jax import lax
from jax.experimental import pallas as pl
from jax.experimental.pallas import tpu as pltpu
from jax.sharding import PartitionSpec as P

F32 = jnp.float32
BF16 = jnp.bfloat16


def vmem(peers):
    return (24 if peers <= 8 else 60) * 2**20


def ring_order(peers):
    width = 1
    while 8 * width * width <= peers:
        width *= 2
    depth = peers // width
    if width == 1 or depth % 2:
        return list(range(peers))
    order = [z * width for z in range(depth)]
    for back, z in enumerate(reversed(range(depth))):
        columns = list(range(1, width))
        order += [z * width + x for x in (columns if back % 2 == 0 else reversed(columns))]
    return order


def ring_shift(value, by, sections=0):
    peers, layers = lax.axis_size("exp"), lax.axis_size("section")
    order = ring_order(peers)
    pairs = []
    for rep in range(lax.axis_size("rep")):
        step = by if rep % 2 == 0 else -by
        for layer in range(layers):
            source = (rep * layers + layer) * peers
            target = (rep * layers + (layer + sections) % layers) * peers
            for spot in range(peers):
                pairs.append((source + order[spot], target + order[(spot + step) % peers]))
    return lax.ppermute(value, ("rep", "section", "exp"), pairs)


def from_behind(value, axis, by):
    peers = lax.axis_size(axis)
    return lax.ppermute(value, axis, [(i, (i + by) % peers) for i in range(peers)])


def dot(a, b, dims):
    return lax.dot_general(a, b, (dims, ((), ())), preferred_element_type=F32)


def whole():
    return pl.BlockSpec(memory_space=pltpu.VMEM)


def turned(value):
    rows, columns = value.shape
    wide = jnp.concatenate([value, jnp.zeros((rows, 128 - columns), F32)], axis=1)
    return wide.T[:columns]


def pack_kernel(experts, codes_ref, exps_ref, routes_ref, weight_ref, grad_ref, out_ref):
    tokens, width = codes_ref.shape
    blocks = exps_ref.shape[0]
    scales = jnp.exp2(exps_ref[...].astype(F32))
    scales = turned(jnp.concatenate([scales, jnp.zeros((128 - blocks, tokens), F32)], axis=0))
    per = width // blocks
    for b in range(blocks):
        cols = slice(b * per, (b + 1) * per)
        out_ref[:, cols] = (codes_ref[:, cols].astype(F32) * scales[:, b : b + 1]).astype(BF16)
    expert = lax.broadcasted_iota(jnp.int32, (experts, tokens), 0)
    table = jnp.zeros((experts, tokens), F32)
    for k in range(routes_ref.shape[0]):
        table += jnp.where(routes_ref[k : k + 1, :] == expert, weight_ref[k : k + 1, :], 0.0)
    high = table.astype(BF16).astype(F32)
    middle = (table - high).astype(BF16).astype(F32)
    low = table - high - middle
    out_ref[:, width : 2 * width] = grad_ref[...]
    extra = out_ref.shape[1] - 2 * width
    parts = [high, middle, low]
    if extra > 3 * experts:
        parts.append(jnp.zeros((extra - 3 * experts, tokens), F32))
    out_ref[:, 2 * width :] = turned(jnp.concatenate(parts, axis=0)).astype(BF16)


LAST = ((1,), (1,))
PLAIN = ((1,), (0,))
TILE = 256


def columns_of(width, body):
    def step(n, carry):
        body(n * TILE)
        return carry

    lax.fori_loop(0, width // TILE, step, 0, unroll=2)


def span(start):
    return pl.ds(pl.multiple_of(start, TILE), TILE)


def load_kernel(*refs):
    count = len(refs) // 2
    copies = [
        pltpu.make_async_copy(refs[i], refs[count + i], refs[-1].at[i]) for i in range(count)
    ]
    for copy in copies:
        copy.start()
    for copy in copies:
        copy.wait()


def load_call(weights):
    return pl.pallas_call(
        load_kernel,
        out_shape=[jax.ShapeDtypeStruct(w.shape, w.dtype) for w in weights],
        in_specs=[pl.BlockSpec(memory_space=pl.ANY)] * len(weights),
        out_specs=[whole()] * len(weights),
        scratch_shapes=[pltpu.SemaphoreType.DMA((len(weights),))],
        compiler_params=pltpu.CompilerParams(vmem_limit_bytes=8 * 2**20),
        cost_estimate=pl.CostEstimate(
            flops=0, bytes_accessed=sum(4 * w.size for w in weights), transcendentals=0
        ),
        name="load_weights",
    )(*weights)


def expert_kernel(count, experts, local_experts, *refs):
    blocks = refs[:count]
    weights = refs[count : count + 6]
    outs = refs[count + 6 : 2 * count + 6]
    saved = refs[2 * count + 6 : 2 * count + 9]
    rows, left = refs[2 * count + 9 :]
    half, width = weights[0].shape
    tokens = blocks[0].shape[0]
    tables = []
    for i, block in enumerate(blocks):
        rows[0, i * tokens : (i + 1) * tokens] = block[:, :width]
        rows[1, i * tokens : (i + 1) * tokens] = block[:, width : 2 * width]
        tables.append(block[:, 2 * width :].astype(F32))
    table = jnp.concatenate(tables, axis=0).T
    expert_of = lax.rem(lax.broadcasted_iota(jnp.int32, table.shape, 0), experts)
    first = lax.axis_index("exp") * local_experts
    scales = [
        jnp.sum(jnp.where(expert_of == first + e, table, 0.0), axis=0, keepdims=True)
        for e in range(local_experts)
    ]
    unit = lax.broadcasted_iota(jnp.int32, (half, 1), 0)
    scale = scales[0]
    for e in range(1, local_experts):
        scale = jnp.where(unit >= e * (half // local_experts), scales[e], scale)
    for side in range(2):
        at = slice(side * half, (side + 1) * half)
        gate = dot(weights[3 * side][...], rows[0], LAST)
        up = dot(weights[3 * side + 1][...], rows[0], LAST)
        back = dot(weights[3 * side + 2][...], rows[1], LAST) * scale
        sig = 1.0 / (1.0 + jnp.exp(-gate))
        swish = gate * sig
        results = (
            back * up * sig * (1.0 + gate * (1.0 - sig)),
            back * swish,
            swish * up * scale,
        )
        for kind, result in enumerate(results):
            result = result.astype(BF16)
            saved[kind][at, :] = result
            left[kind, :, at] = result.T

    def column(start):
        at, later = span(start), span(width + start)
        right = [
            jnp.concatenate([weights[kind][:, at], weights[3 + kind][:, at]], axis=0)
            for kind in range(3)
        ]
        output = dot(left[2], right[2], PLAIN).astype(BF16)
        grad = (dot(left[0], right[0], PLAIN) + dot(left[1], right[1], PLAIN)).astype(BF16)
        for i, out in enumerate(outs):
            out[:, at] = output[i * tokens : (i + 1) * tokens]
            out[:, later] = grad[i * tokens : (i + 1) * tokens]

    columns_of(width, column)


def expert_call(blocks, weights, experts, local_experts):
    count, tokens = len(blocks), blocks[0].shape[0]
    half, width = weights[0].shape
    units, rows = 2 * half, count * tokens
    results = pl.pallas_call(
        functools.partial(expert_kernel, count, experts, local_experts),
        out_shape=[jax.ShapeDtypeStruct((tokens, 2 * width), BF16)] * count
        + [jax.ShapeDtypeStruct((units, rows), BF16)] * 3,
        in_specs=[whole()] * (count + 6),
        out_specs=[whole()] * (count + 3),
        scratch_shapes=[
            pltpu.VMEM((2, rows, width), BF16),
            pltpu.VMEM((3, rows, units), BF16),
        ],
        compiler_params=pltpu.CompilerParams(vmem_limit_bytes=vmem(experts // local_experts)),
        cost_estimate=pl.CostEstimate(
            flops=6 * 2 * rows * units * width,
            bytes_accessed=6 * units * width + 8 * rows * width,
            transcendentals=rows * units,
        ),
        name="expert_rows",
    )(*blocks, *weights)
    return results[:count], results[count:]


def weight_kernel(groups, count, *refs):
    blocks = refs[:count]
    kept = [refs[count + g * 3 : count + g * 3 + 3] for g in range(groups)]
    outs, across = refs[-7:-1], refs[-1]
    half, width = outs[0].shape
    for kind in range(3):
        start = 0
        for group in kept:
            size = group[kind].shape[1]
            across[kind, :, start : start + size] = group[kind][...]
            start += size

    def column(start):
        at, later = span(start), span(width + start)
        right = [
            jnp.concatenate([b[:, at] for b in blocks], axis=0),
            jnp.concatenate([b[:, later] for b in blocks], axis=0),
        ]
        for kind in range(3):
            total = dot(across[kind], right[kind // 2], PLAIN).astype(BF16)
            outs[kind][:, at] = total[:half]
            outs[3 + kind][:, at] = total[half:]

    columns_of(width, column)


def weight_call(blocks, kept, width, peers):
    count = len(blocks)
    units = kept[0][0].shape[0]
    half, total = units // 2, count * blocks[0].shape[0]
    results = pl.pallas_call(
        functools.partial(weight_kernel, len(kept), count),
        out_shape=[jax.ShapeDtypeStruct((half, width), BF16)] * 6,
        in_specs=[whole()] * (count + 3 * len(kept)),
        out_specs=[whole()] * 6,
        scratch_shapes=[pltpu.VMEM((3, units, total), BF16)],
        compiler_params=pltpu.CompilerParams(vmem_limit_bytes=vmem(peers)),
        cost_estimate=pl.CostEstimate(
            flops=3 * 2 * total * units * width,
            bytes_accessed=4 * total * width + 12 * half * width,
            transcendentals=0,
        ),
        name="weight_grads",
    )(*blocks, *[k for group in kept for k in group])
    return results[:3], results[3:]


def add(a, b):
    return (a.astype(F32) + b.astype(F32)).astype(BF16)


def shards(
    row_codes, block_exponents, routes, route_weight, out_grad, gate_weight, up_weight, down_weight
):
    tokens, width = row_codes.shape[1:]
    local_experts, half_units = gate_weight.shape[1:3]
    half = local_experts * half_units
    peers = lax.axis_size("exp")
    experts = peers * local_experts
    lanes = -(-3 * experts // 128) * 128
    shards_of = [w.reshape(half, width) for w in (gate_weight, up_weight, down_weight)]
    other = [from_behind(w, "rep", 1) for w in shards_of]
    home = pl.pallas_call(
        functools.partial(pack_kernel, experts),
        out_shape=jax.ShapeDtypeStruct((tokens, 2 * width + lanes), BF16),
        in_specs=[whole()] * 5,
        out_specs=whole(),
        compiler_params=pltpu.CompilerParams(vmem_limit_bytes=60 * 2**20),
        name="pack_rows",
    )(row_codes[0], block_exponents[0].T, routes[0].T, route_weight[0].T, out_grad[0])

    tie = lax.optimization_barrier
    shards_of = tie((home, shards_of))[1]
    own = load_call(shards_of[:1]) + load_call(shards_of[1:])
    weights = list(own) + other
    ahead, behind = peers // 2, peers // 2 - 1
    names = [("near", 0)]
    for k in range(1, ahead + 1):
        names += [("near", k), ("far", k)]
    names = names[: 2 * ahead]
    groups = [names[i : i + 4] for i in range(0, len(names) - 4, 4)]
    groups += [names[-4:-2], names[-2:]]
    held = {("near", 0): home, ("far", 0): tie((home, own))[0]}
    partial, kept = {}, []

    def work(group):
        outs, saved = expert_call(
            [held[name] for name in group], weights, experts, local_experts
        )
        partial.update(zip(group, outs))
        kept.append(saved)

    for k in range(1, ahead + 1):
        held["near", k] = ring_shift(held["near", k - 1], 1)
        if k == 1:
            held["near", 1], own = tie((held["near", 1], own))
            weights[:3] = own
        if k % 2 == 1 and k > 1:
            work(groups[(k - 3) // 2])
            held["far", k - 1], kept[-1] = tie((held["far", k - 1], kept[-1]))
        if k <= behind:
            held["far", k] = ring_shift(held["far", k - 1], -1)
    work(groups[-2])
    arrived = [held[name] for name in groups[-1]]
    arrived, kept[-1] = tie((arrived, kept[-1]))
    held.update(zip(groups[-1], arrived))
    work(groups[-1])
    far_sum = ring_shift(partial["far", behind], 1)
    both = (slice(0, width), slice(width, 2 * width))
    near_sum = partial["near", ahead]
    own_total = received = None
    blocks = [held[name] for group in groups for name in group]
    steps = (1, -1)
    finals = []
    here, near_sum = tie((partial["near", 0], near_sum))
    for part, step in zip(both, steps):
        kept_here = add(home[:, part], here[:, part])
        finals.append([from_behind(kept_here, "section", step)])
    for k in range(ahead, 1, -1):
        near_sum = ring_shift(near_sum, -1)
        left = k - 2
        if left > 1:
            far_done = far_sum
            far_sum = ring_shift(add(far_sum, partial["far", left]), 1)
            near_sum, _ = tie((near_sum, far_done))
        if k == 3:
            own_total, other_total = weight_call(blocks, kept, width, peers)
            here = [final[0] for final in finals]
            near_sum, own_total, other_total, _ = tie((near_sum, own_total, other_total, here))
            lasts = [add(far_sum[:, part], partial["far", 1][:, part]) for part in both]
            for final, last, step in zip(finals, lasts, steps):
                final.append(ring_shift(last, 1, step))
            near_sum, _ = tie((near_sum, lasts))
            near_sum = add(near_sum, partial["near", 2])
        elif k == 2:
            here = [final[1] for final in finals]
            near_sum, other_total, _ = tie((near_sum, other_total, here))
            received = [from_behind(g, "rep", 1) for g in other_total]
        elif k > 2:
            near_sum = add(near_sum, partial["near", k - 1])
    lasts = [add(near_sum[:, part], partial["near", 1][:, part]) for part in both]
    for final, last, step in zip(finals, lasts, steps):
        final.append(ring_shift(last, -1, step))
    totals = [add(a, b) for a, b in zip(own_total, received)]
    finals, totals = tie((finals, totals))
    results = [sum(f.astype(F32) for f in final).astype(BF16)[None] for final in finals]
    shape = (1, local_experts, half_units, width)
    return tuple(results) + tuple(t.reshape(shape) for t in totals)


def solution(mesh):
    tokens = P("section", ("rep", "exp"), None)
    weights = P("section", "exp", "rep", None)
    return jax.shard_map(
        shards,
        mesh=mesh,
        in_specs=(tokens,) * 5 + (weights,) * 3,
        out_specs=(tokens,) * 2 + (weights,) * 3,
        check_vma=False,
    )
```

```python
import functools
import jax
import jax.numpy as jnp
from jax import lax
from jax.experimental import pallas as pl
from jax.experimental.pallas import tpu as pltpu
from jax.sharding import PartitionSpec as P

F32 = jnp.float32
BF16 = jnp.bfloat16


def vmem(peers):
    return (24 if peers <= 8 else 60) * 2**20


def ring_order(peers):
    width = 1
    while 8 * width * width <= peers:
        width *= 2
    depth = peers // width
    if width == 1 or depth % 2:
        return list(range(peers))
    order = [z * width for z in range(depth)]
    for back, z in enumerate(reversed(range(depth))):
        columns = list(range(1, width))
        order += [z * width + x for x in (columns if back % 2 == 0 else reversed(columns))]
    return order


def ring_shift(value, by, sections=0):
    peers, layers = lax.axis_size("exp"), lax.axis_size("section")
    order = ring_order(peers)
    pairs = []
    for rep in range(lax.axis_size("rep")):
        step = by if rep % 2 == 0 else -by
        for layer in range(layers):
            source = (rep * layers + layer) * peers
            target = (rep * layers + (layer + sections) % layers) * peers
            for spot in range(peers):
                pairs.append((source + order[spot], target + order[(spot + step) % peers]))
    return lax.ppermute(value, ("rep", "section", "exp"), pairs)


def from_behind(value, axis, by):
    peers = lax.axis_size(axis)
    return lax.ppermute(value, axis, [(i, (i + by) % peers) for i in range(peers)])


def dot(a, b, dims):
    return lax.dot_general(a, b, (dims, ((), ())), preferred_element_type=F32)


def whole():
    return pl.BlockSpec(memory_space=pltpu.VMEM)


def turned(value):
    rows, columns = value.shape
    wide = jnp.concatenate([value, jnp.zeros((rows, 128 - columns), F32)], axis=1)
    return wide.T[:columns]


def pack_kernel(experts, codes_ref, exps_ref, routes_ref, weight_ref, grad_ref, out_ref):
    tokens, width = codes_ref.shape
    blocks = exps_ref.shape[0]
    scales = jnp.exp2(exps_ref[...].astype(F32))
    scales = turned(jnp.concatenate([scales, jnp.zeros((128 - blocks, tokens), F32)], axis=0))
    per = width // blocks
    for b in range(blocks):
        cols = slice(b * per, (b + 1) * per)
        out_ref[:, cols] = (codes_ref[:, cols].astype(F32) * scales[:, b : b + 1]).astype(BF16)
    expert = lax.broadcasted_iota(jnp.int32, (experts, tokens), 0)
    table = jnp.zeros((experts, tokens), F32)
    for k in range(routes_ref.shape[0]):
        table += jnp.where(routes_ref[k : k + 1, :] == expert, weight_ref[k : k + 1, :], 0.0)
    high = table.astype(BF16).astype(F32)
    middle = (table - high).astype(BF16).astype(F32)
    low = table - high - middle
    out_ref[:, width : 2 * width] = grad_ref[...]
    extra = out_ref.shape[1] - 2 * width
    parts = [high, middle, low]
    if extra > 3 * experts:
        parts.append(jnp.zeros((extra - 3 * experts, tokens), F32))
    out_ref[:, 2 * width :] = turned(jnp.concatenate(parts, axis=0)).astype(BF16)


LAST = ((1,), (1,))
PLAIN = ((1,), (0,))
TILE = 256


def columns_of(width, body):
    def step(n, carry):
        body(n * TILE)
        return carry

    lax.fori_loop(0, width // TILE, step, 0, unroll=2)


def span(start):
    return pl.ds(pl.multiple_of(start, TILE), TILE)


def load_kernel(*refs):
    count = len(refs) // 2
    copies = [
        pltpu.make_async_copy(refs[i], refs[count + i], refs[-1].at[i]) for i in range(count)
    ]
    for copy in copies:
        copy.start()
    for copy in copies:
        copy.wait()


def load_call(weights):
    return pl.pallas_call(
        load_kernel,
        out_shape=[jax.ShapeDtypeStruct(w.shape, w.dtype) for w in weights],
        in_specs=[pl.BlockSpec(memory_space=pl.ANY)] * len(weights),
        out_specs=[whole()] * len(weights),
        scratch_shapes=[pltpu.SemaphoreType.DMA((len(weights),))],
        compiler_params=pltpu.CompilerParams(vmem_limit_bytes=8 * 2**20),
        cost_estimate=pl.CostEstimate(
            flops=0, bytes_accessed=sum(4 * w.size for w in weights), transcendentals=0
        ),
        name="load_weights",
    )(*weights)


def expert_kernel(count, experts, local_experts, *refs):
    blocks = refs[:count]
    weights = refs[count : count + 6]
    outs = refs[count + 6 : 2 * count + 6]
    saved = refs[2 * count + 6 : 2 * count + 9]
    rows, left = refs[2 * count + 9 :]
    half, width = weights[0].shape
    tokens = blocks[0].shape[0]
    tables = []
    for i, block in enumerate(blocks):
        rows[0, i * tokens : (i + 1) * tokens] = block[:, :width]
        rows[1, i * tokens : (i + 1) * tokens] = block[:, width : 2 * width]
        tables.append(block[:, 2 * width :].astype(F32))
    table = jnp.concatenate(tables, axis=0).T
    expert_of = lax.rem(lax.broadcasted_iota(jnp.int32, table.shape, 0), experts)
    first = lax.axis_index("exp") * local_experts
    scales = [
        jnp.sum(jnp.where(expert_of == first + e, table, 0.0), axis=0, keepdims=True)
        for e in range(local_experts)
    ]
    unit = lax.broadcasted_iota(jnp.int32, (half, 1), 0)
    scale = scales[0]
    for e in range(1, local_experts):
        scale = jnp.where(unit >= e * (half // local_experts), scales[e], scale)
    for side in range(2):
        at = slice(side * half, (side + 1) * half)
        gate = dot(weights[3 * side][...], rows[0], LAST)
        up = dot(weights[3 * side + 1][...], rows[0], LAST)
        back = dot(weights[3 * side + 2][...], rows[1], LAST) * scale
        sig = 1.0 / (1.0 + jnp.exp(-gate))
        swish = gate * sig
        results = (
            back * up * sig * (1.0 + gate * (1.0 - sig)),
            back * swish,
            swish * up * scale,
        )
        for kind, result in enumerate(results):
            result = result.astype(BF16)
            saved[kind][at, :] = result
            left[kind, :, at] = result.T

    def column(start):
        at, later = span(start), span(width + start)
        right = [
            jnp.concatenate([weights[kind][:, at], weights[3 + kind][:, at]], axis=0)
            for kind in range(3)
        ]
        output = dot(left[2], right[2], PLAIN).astype(BF16)
        grad = (dot(left[0], right[0], PLAIN) + dot(left[1], right[1], PLAIN)).astype(BF16)
        for i, out in enumerate(outs):
            out[:, at] = output[i * tokens : (i + 1) * tokens]
            out[:, later] = grad[i * tokens : (i + 1) * tokens]

    columns_of(width, column)


def expert_call(blocks, weights, experts, local_experts):
    count, tokens = len(blocks), blocks[0].shape[0]
    half, width = weights[0].shape
    units, rows = 2 * half, count * tokens
    results = pl.pallas_call(
        functools.partial(expert_kernel, count, experts, local_experts),
        out_shape=[jax.ShapeDtypeStruct((tokens, 2 * width), BF16)] * count
        + [jax.ShapeDtypeStruct((units, rows), BF16)] * 3,
        in_specs=[whole()] * (count + 6),
        out_specs=[whole()] * (count + 3),
        scratch_shapes=[
            pltpu.VMEM((2, rows, width), BF16),
            pltpu.VMEM((3, rows, units), BF16),
        ],
        compiler_params=pltpu.CompilerParams(vmem_limit_bytes=vmem(experts // local_experts)),
        cost_estimate=pl.CostEstimate(
            flops=6 * 2 * rows * units * width,
            bytes_accessed=6 * units * width + 8 * rows * width,
            transcendentals=rows * units,
        ),
        name="expert_rows",
    )(*blocks, *weights)
    return results[:count], results[count:]


def weight_kernel(groups, count, *refs):
    blocks = refs[:count]
    kept = [refs[count + g * 3 : count + g * 3 + 3] for g in range(groups)]
    outs, across = refs[-7:-1], refs[-1]
    half, width = outs[0].shape
    for kind in range(3):
        start = 0
        for group in kept:
            size = group[kind].shape[1]
            across[kind, :, start : start + size] = group[kind][...]
            start += size

    def column(start):
        at, later = span(start), span(width + start)
        right = [
            jnp.concatenate([b[:, at] for b in blocks], axis=0),
            jnp.concatenate([b[:, later] for b in blocks], axis=0),
        ]
        for kind in range(3):
            total = dot(across[kind], right[kind // 2], PLAIN).astype(BF16)
            outs[kind][:, at] = total[:half]
            outs[3 + kind][:, at] = total[half:]

    columns_of(width, column)


def weight_call(blocks, kept, width, peers):
    count = len(blocks)
    units = kept[0][0].shape[0]
    half, total = units // 2, count * blocks[0].shape[0]
    results = pl.pallas_call(
        functools.partial(weight_kernel, len(kept), count),
        out_shape=[jax.ShapeDtypeStruct((half, width), BF16)] * 6,
        in_specs=[whole()] * (count + 3 * len(kept)),
        out_specs=[whole()] * 6,
        scratch_shapes=[pltpu.VMEM((3, units, total), BF16)],
        compiler_params=pltpu.CompilerParams(vmem_limit_bytes=vmem(peers)),
        cost_estimate=pl.CostEstimate(
            flops=3 * 2 * total * units * width,
            bytes_accessed=4 * total * width + 12 * half * width,
            transcendentals=0,
        ),
        name="weight_grads",
    )(*blocks, *[k for group in kept for k in group])
    return results[:3], results[3:]


def add(a, b):
    return (a.astype(F32) + b.astype(F32)).astype(BF16)


def shards(
    row_codes, block_exponents, routes, route_weight, out_grad, gate_weight, up_weight, down_weight
):
    tokens, width = row_codes.shape[1:]
    local_experts, half_units = gate_weight.shape[1:3]
    half = local_experts * half_units
    peers = lax.axis_size("exp")
    experts = peers * local_experts
    lanes = -(-3 * experts // 128) * 128
    shards_of = [w.reshape(half, width) for w in (gate_weight, up_weight, down_weight)]
    other = [from_behind(w, "rep", 1) for w in shards_of]
    home = pl.pallas_call(
        functools.partial(pack_kernel, experts),
        out_shape=jax.ShapeDtypeStruct((tokens, 2 * width + lanes), BF16),
        in_specs=[whole()] * 5,
        out_specs=whole(),
        compiler_params=pltpu.CompilerParams(vmem_limit_bytes=60 * 2**20),
        name="pack_rows",
    )(row_codes[0], block_exponents[0].T, routes[0].T, route_weight[0].T, out_grad[0])

    tie = lax.optimization_barrier
    shards_of = tie((home, shards_of))[1]
    own = load_call(shards_of[:1]) + load_call(shards_of[1:])
    weights = list(own) + other
    ahead, behind = peers // 2, peers // 2 - 1
    names = [("near", 0)]
    for k in range(1, ahead + 1):
        names += [("near", k), ("far", k)]
    names = names[: 2 * ahead]
    groups = [names[i : i + 4] for i in range(0, len(names) - 4, 4)]
    groups += [[name for name in names[-4:] if name[0] == way] for way in ("far", "near")]
    held = {("near", 0): home, ("far", 0): tie((home, own))[0]}
    partial, kept = {}, []

    def work(group):
        outs, saved = expert_call(
            [held[name] for name in group], weights, experts, local_experts
        )
        partial.update(zip(group, outs))
        kept.append(saved)

    for k in range(1, ahead + 1):
        held["near", k] = ring_shift(held["near", k - 1], 1)
        if k == 1:
            held["near", 1], own = tie((held["near", 1], own))
            weights[:3] = own
        if k % 2 == 1 and k > 1:
            work(groups[(k - 3) // 2])
            held["far", k - 1], kept[-1] = tie((held["far", k - 1], kept[-1]))
        if k <= behind:
            held["far", k] = ring_shift(held["far", k - 1], -1)
    work(groups[-2])
    far_sum = ring_shift(partial["far", behind], 1)
    held["near", ahead], kept[-1] = tie((held["near", ahead], kept[-1]))
    work(groups[-1])
    both = (slice(0, width), slice(width, 2 * width))
    near_sum = partial["near", ahead]
    own_total = received = None
    blocks = [held[name] for group in groups for name in group]
    steps = (1, -1)
    finals = []
    here, far_sum = tie((partial["near", 0], far_sum))
    for part, step in zip(both, steps):
        kept_here = add(home[:, part], here[:, part])
        finals.append([from_behind(kept_here, "section", step)])
    for k in range(ahead, 1, -1):
        near_sum = ring_shift(near_sum, -1)
        left = k - 2
        if left > 1:
            far_done = far_sum
            far_next = add(far_sum, partial["far", left])
            far_sum = ring_shift(far_next, 1)
            near_sum, _ = tie((near_sum, far_done))
        if k == 4:
            kept[-1], _ = tie((kept[-1], far_next))
            own_total, other_total = weight_call(blocks, kept, width, peers)
            near_sum, own_total, other_total = tie((near_sum, own_total, other_total))
        if k == 3:
            lasts = [add(far_sum[:, part], partial["far", 1][:, part]) for part in both]
            for final, last, step in zip(finals, lasts, steps):
                final.append(ring_shift(last, 1, step))
            here = [final[0] for final in finals] + finals[0][1:]
            near_sum, _ = tie((near_sum, here))
            near_sum = add(near_sum, partial["near", 2])
            near_sum, other_total = tie((near_sum, other_total))
            received = [from_behind(g, "rep", 1) for g in other_total]
        elif k == 2:
            here = [final[1] for final in finals]
            near_sum, _ = tie((near_sum, here))
        elif k > 2:
            near_sum = add(near_sum, partial["near", k - 1])
    lasts = [add(near_sum[:, part], partial["near", 1][:, part]) for part in both]
    for final, last, step in zip(finals, lasts, steps):
        final.append(ring_shift(last, -1, step))
    totals = [add(a, b) for a, b in zip(own_total, received)]
    finals, totals = tie((finals, totals))
    results = [sum(f.astype(F32) for f in final).astype(BF16)[None] for final in finals]
    shape = (1, local_experts, half_units, width)
    return tuple(results) + tuple(t.reshape(shape) for t in totals)


def solution(mesh):
    tokens = P("section", ("rep", "exp"), None)
    weights = P("section", "exp", "rep", None)
    return jax.shard_map(
        shards,
        mesh=mesh,
        in_specs=(tokens,) * 5 + (weights,) * 3,
        out_specs=(tokens,) * 2 + (weights,) * 3,
        check_vma=False,
    )
```

```python
import functools
import jax
import jax.numpy as jnp
from jax import lax
from jax.experimental import pallas as pl
from jax.experimental.pallas import tpu as pltpu
from jax.sharding import PartitionSpec as P

F32 = jnp.float32
BF16 = jnp.bfloat16


def vmem(peers):
    return (24 if peers <= 8 else 60) * 2**20


def ring_order(peers):
    width = 1
    while 8 * width * width <= peers:
        width *= 2
    depth = peers // width
    if width == 1 or depth % 2:
        return list(range(peers))
    order = [z * width for z in range(depth)]
    for back, z in enumerate(reversed(range(depth))):
        columns = list(range(1, width))
        order += [z * width + x for x in (columns if back % 2 == 0 else reversed(columns))]
    return order


def ring_shift(value, by, sections=0):
    peers, layers = lax.axis_size("exp"), lax.axis_size("section")
    order = ring_order(peers)
    pairs = []
    for rep in range(lax.axis_size("rep")):
        step = by if rep % 2 == 0 else -by
        for layer in range(layers):
            source = (rep * layers + layer) * peers
            target = (rep * layers + (layer + sections) % layers) * peers
            for spot in range(peers):
                pairs.append((source + order[spot], target + order[(spot + step) % peers]))
    return lax.ppermute(value, ("rep", "section", "exp"), pairs)


def from_behind(value, axis, by):
    peers = lax.axis_size(axis)
    return lax.ppermute(value, axis, [(i, (i + by) % peers) for i in range(peers)])


def dot(a, b, dims):
    return lax.dot_general(a, b, (dims, ((), ())), preferred_element_type=F32)


def whole():
    return pl.BlockSpec(memory_space=pltpu.VMEM)


def turned(value):
    rows, columns = value.shape
    wide = jnp.concatenate([value, jnp.zeros((rows, 128 - columns), F32)], axis=1)
    return wide.T[:columns]


def pack_kernel(experts, codes_ref, exps_ref, routes_ref, weight_ref, grad_ref, out_ref):
    tokens, width = codes_ref.shape
    blocks = exps_ref.shape[0]
    scales = jnp.exp2(exps_ref[...].astype(F32))
    scales = turned(jnp.concatenate([scales, jnp.zeros((128 - blocks, tokens), F32)], axis=0))
    per = width // blocks
    for b in range(blocks):
        cols = slice(b * per, (b + 1) * per)
        out_ref[:, cols] = (codes_ref[:, cols].astype(F32) * scales[:, b : b + 1]).astype(BF16)
    expert = lax.broadcasted_iota(jnp.int32, (experts, tokens), 0)
    table = jnp.zeros((experts, tokens), F32)
    for k in range(routes_ref.shape[0]):
        table += jnp.where(routes_ref[k : k + 1, :] == expert, weight_ref[k : k + 1, :], 0.0)
    high = table.astype(BF16).astype(F32)
    middle = (table - high).astype(BF16).astype(F32)
    low = table - high - middle
    out_ref[:, width : 2 * width] = grad_ref[...]
    extra = out_ref.shape[1] - 2 * width
    parts = [high, middle, low]
    if extra > 3 * experts:
        parts.append(jnp.zeros((extra - 3 * experts, tokens), F32))
    out_ref[:, 2 * width :] = turned(jnp.concatenate(parts, axis=0)).astype(BF16)


PLAIN = ((1,), (0,))
TILE = 256


def columns_of(width, body):
    def step(n, carry):
        body(n * TILE)
        return carry

    lax.fori_loop(0, width // TILE, step, 0, unroll=2)


def span(start):
    return pl.ds(pl.multiple_of(start, TILE), TILE)


def load_kernel(*refs):
    count = len(refs) // 2
    copies = [
        pltpu.make_async_copy(refs[i], refs[count + i], refs[-1].at[i]) for i in range(count)
    ]
    for copy in copies:
        copy.start()
    for copy in copies:
        copy.wait()


def load_call(weights):
    return pl.pallas_call(
        load_kernel,
        out_shape=[jax.ShapeDtypeStruct(w.shape, w.dtype) for w in weights],
        in_specs=[pl.BlockSpec(memory_space=pl.ANY)] * len(weights),
        out_specs=[whole()] * len(weights),
        scratch_shapes=[pltpu.SemaphoreType.DMA((len(weights),))],
        compiler_params=pltpu.CompilerParams(vmem_limit_bytes=8 * 2**20),
        cost_estimate=pl.CostEstimate(
            flops=0, bytes_accessed=sum(4 * w.size for w in weights), transcendentals=0
        ),
        name="load_weights",
    )(*weights)


def expert_kernel(count, experts, local_experts, *refs):
    blocks = refs[:count]
    weights = refs[count : count + 6]
    outs = refs[count + 6 : 2 * count + 6]
    saved = refs[2 * count + 6 : 2 * count + 9]
    rows, left = refs[2 * count + 9 :]
    half, width = weights[0].shape
    tokens = blocks[0].shape[0]
    tables = []
    for start in range(0, 2 * width, TILE):
        part, at = divmod(start, width)
        piece = jnp.concatenate([block[:, start : start + TILE] for block in blocks], axis=0)
        rows[part, at : at + TILE] = piece.T
    for block in blocks:
        tables.append(block[:, 2 * width :].astype(F32))
    table = jnp.concatenate(tables, axis=0).T
    expert_of = lax.rem(lax.broadcasted_iota(jnp.int32, table.shape, 0), experts)
    first = lax.axis_index("exp") * local_experts
    scales = [
        jnp.sum(jnp.where(expert_of == first + e, table, 0.0), axis=0, keepdims=True)
        for e in range(local_experts)
    ]
    unit = lax.broadcasted_iota(jnp.int32, (half, 1), 0)
    scale = scales[0]
    for e in range(1, local_experts):
        scale = jnp.where(unit >= e * (half // local_experts), scales[e], scale)
    for side in range(2):
        at = slice(side * half, (side + 1) * half)
        gate = dot(weights[3 * side][...], rows[0], PLAIN)
        up = dot(weights[3 * side + 1][...], rows[0], PLAIN)
        back = dot(weights[3 * side + 2][...], rows[1], PLAIN) * scale
        sig = 1.0 / (1.0 + jnp.exp(-gate))
        swish = gate * sig
        results = (
            back * up * sig * (1.0 + gate * (1.0 - sig)),
            back * swish,
            swish * up * scale,
        )
        for kind, result in enumerate(results):
            result = result.astype(BF16)
            saved[kind][at, :] = result
            left[kind, :, at] = result.T

    def column(start):
        at, later = span(start), span(width + start)
        right = [
            jnp.concatenate([weights[kind][:, at], weights[3 + kind][:, at]], axis=0)
            for kind in range(3)
        ]
        output = dot(left[2], right[2], PLAIN).astype(BF16)
        grad = (dot(left[0], right[0], PLAIN) + dot(left[1], right[1], PLAIN)).astype(BF16)
        for i, out in enumerate(outs):
            out[:, at] = output[i * tokens : (i + 1) * tokens]
            out[:, later] = grad[i * tokens : (i + 1) * tokens]

    columns_of(width, column)


def expert_call(blocks, weights, experts, local_experts):
    count, tokens = len(blocks), blocks[0].shape[0]
    half, width = weights[0].shape
    units, rows = 2 * half, count * tokens
    results = pl.pallas_call(
        functools.partial(expert_kernel, count, experts, local_experts),
        out_shape=[jax.ShapeDtypeStruct((tokens, 2 * width), BF16)] * count
        + [jax.ShapeDtypeStruct((units, rows), BF16)] * 3,
        in_specs=[whole()] * (count + 6),
        out_specs=[whole()] * (count + 3),
        scratch_shapes=[
            pltpu.VMEM((2, width, rows), BF16),
            pltpu.VMEM((3, rows, units), BF16),
        ],
        compiler_params=pltpu.CompilerParams(vmem_limit_bytes=vmem(experts // local_experts)),
        cost_estimate=pl.CostEstimate(
            flops=6 * 2 * rows * units * width,
            bytes_accessed=6 * units * width + 8 * rows * width,
            transcendentals=rows * units,
        ),
        name="expert_rows",
    )(*blocks, *weights)
    return results[:count], results[count:]


def weight_kernel(groups, count, *refs):
    blocks = refs[:count]
    kept = [refs[count + g * 3 : count + g * 3 + 3] for g in range(groups)]
    outs, across = refs[-7:-1], refs[-1]
    half, width = outs[0].shape
    for kind in range(3):
        start = 0
        for group in kept:
            size = group[kind].shape[1]
            across[kind, :, start : start + size] = group[kind][...]
            start += size

    def column(start):
        at, later = span(start), span(width + start)
        right = [
            jnp.concatenate([b[:, at] for b in blocks], axis=0),
            jnp.concatenate([b[:, later] for b in blocks], axis=0),
        ]
        for kind in range(3):
            total = dot(across[kind], right[kind // 2], PLAIN).astype(BF16)
            outs[kind][:, at] = total[:half]
            outs[3 + kind][:, at] = total[half:]

    columns_of(width, column)


def weight_call(blocks, kept, width, peers):
    count = len(blocks)
    units = kept[0][0].shape[0]
    half, total = units // 2, count * blocks[0].shape[0]
    results = pl.pallas_call(
        functools.partial(weight_kernel, len(kept), count),
        out_shape=[jax.ShapeDtypeStruct((half, width), BF16)] * 6,
        in_specs=[whole()] * (count + 3 * len(kept)),
        out_specs=[whole()] * 6,
        scratch_shapes=[pltpu.VMEM((3, units, total), BF16)],
        compiler_params=pltpu.CompilerParams(vmem_limit_bytes=vmem(peers)),
        cost_estimate=pl.CostEstimate(
            flops=3 * 2 * total * units * width,
            bytes_accessed=4 * total * width + 12 * half * width,
            transcendentals=0,
        ),
        name="weight_grads",
    )(*blocks, *[k for group in kept for k in group])
    return results[:3], results[3:]


def add(a, b):
    return (a.astype(F32) + b.astype(F32)).astype(BF16)


def shards(
    row_codes, block_exponents, routes, route_weight, out_grad, gate_weight, up_weight, down_weight
):
    tokens, width = row_codes.shape[1:]
    local_experts, half_units = gate_weight.shape[1:3]
    half = local_experts * half_units
    peers = lax.axis_size("exp")
    experts = peers * local_experts
    lanes = -(-3 * experts // 128) * 128
    shards_of = [w.reshape(half, width) for w in (gate_weight, up_weight, down_weight)]
    other = [from_behind(w, "rep", 1) for w in shards_of]
    home = pl.pallas_call(
        functools.partial(pack_kernel, experts),
        out_shape=jax.ShapeDtypeStruct((tokens, 2 * width + lanes), BF16),
        in_specs=[whole()] * 5,
        out_specs=whole(),
        compiler_params=pltpu.CompilerParams(vmem_limit_bytes=60 * 2**20),
        name="pack_rows",
    )(row_codes[0], block_exponents[0].T, routes[0].T, route_weight[0].T, out_grad[0])

    tie = lax.optimization_barrier
    shards_of = tie((home, shards_of))[1]
    own = load_call(shards_of[:1]) + load_call(shards_of[1:])
    weights = list(own) + other
    ahead, behind = peers // 2, peers // 2 - 1
    names = [("near", 0)]
    for k in range(1, ahead + 1):
        names += [("near", k), ("far", k)]
    names = names[: 2 * ahead]
    groups = [names[i : i + 4] for i in range(0, len(names) - 4, 4)]
    groups.append([name for name in names[-4:] if name[0] == "far"])
    groups.append([name for name in names[-4:] if name[0] == "near"])
    held = {("near", 0): home, ("far", 0): tie((home, own))[0]}
    partial, kept = {}, []

    def work(group):
        outs, saved = expert_call(
            [held[name] for name in group], weights, experts, local_experts
        )
        partial.update(zip(group, outs))
        kept.append(saved)

    for k in range(1, ahead + 1):
        held["near", k] = ring_shift(held["near", k - 1], 1)
        if k <= behind:
            held["far", k] = ring_shift(held["far", k - 1], -1)
        if k == 1:
            held["near", 1], own = tie((held["near", 1], own))
            weights[:3] = own
        if k % 2 == 1 and k > 1:
            work(groups[(k - 3) // 2])
            held["near", k], kept[-1] = tie((held["near", k], kept[-1]))
    work(groups[-2])
    far_sum = ring_shift(partial["far", behind], 1)
    held["near", ahead], kept[-1] = tie((held["near", ahead], kept[-1]))
    work(groups[-1])
    both = (slice(0, width), slice(width, 2 * width))
    near_sum = partial["near", ahead]
    own_total = received = None
    blocks = [held[name] for group in groups for name in group]
    steps = (1, -1)
    finals = []
    here, near_sum = tie((partial["near", 0], near_sum))
    for part, step in zip(both, steps):
        kept_here = add(home[:, part], here[:, part])
        finals.append([from_behind(kept_here, "section", step)])
    for k in range(ahead, 1, -1):
        near_sum = ring_shift(near_sum, -1)
        left = k - 2
        if left > 1:
            far_done = far_sum
            far_sum = ring_shift(add(far_sum, partial["far", left]), 1)
            near_sum, _ = tie((near_sum, far_done))
        if k == 3:
            own_total, other_total = weight_call(blocks, kept, width, peers)
            here = [final[0] for final in finals]
            near_sum, own_total, other_total, _ = tie((near_sum, own_total, other_total, here))
            lasts = [add(far_sum[:, part], partial["far", 1][:, part]) for part in both]
            for final, last, step in zip(finals, lasts, steps):
                final.append(ring_shift(last, 1, step))
            near_sum, _ = tie((near_sum, lasts))
            near_sum = add(near_sum, partial["near", 2])
        elif k == 2:
            here = [final[1] for final in finals]
            near_sum, other_total, _ = tie((near_sum, other_total, here))
            received = [from_behind(g, "rep", 1) for g in other_total]
        elif k > 2:
            near_sum = add(near_sum, partial["near", k - 1])
    lasts = [add(near_sum[:, part], partial["near", 1][:, part]) for part in both]
    for final, last, step in zip(finals, lasts, steps):
        final.append(ring_shift(last, -1, step))
    totals = [add(a, b) for a, b in zip(own_total, received)]
    finals, totals = tie((finals, totals))
    results = [sum(f.astype(F32) for f in final).astype(BF16)[None] for final in finals]
    shape = (1, local_experts, half_units, width)
    return tuple(results) + tuple(t.reshape(shape) for t in totals)


def solution(mesh):
    tokens = P("section", ("rep", "exp"), None)
    weights = P("section", "exp", "rep", None)
    return jax.shard_map(
        shards,
        mesh=mesh,
        in_specs=(tokens,) * 5 + (weights,) * 3,
        out_specs=(tokens,) * 2 + (weights,) * 3,
        check_vma=False,
    )
```

```python
import functools
import jax
import jax.numpy as jnp
from jax import lax
from jax.experimental import pallas as pl
from jax.experimental.pallas import tpu as pltpu
from jax.sharding import PartitionSpec as P

F32 = jnp.float32
BF16 = jnp.bfloat16


def vmem(peers):
    return (24 if peers <= 8 else 60) * 2**20


def ring_order(peers):
    width = 1
    while 8 * width * width <= peers:
        width *= 2
    depth = peers // width
    if width == 1 or depth % 2:
        return list(range(peers))
    order = [z * width for z in range(depth)]
    for back, z in enumerate(reversed(range(depth))):
        columns = list(range(1, width))
        order += [z * width + x for x in (columns if back % 2 == 0 else reversed(columns))]
    return order


def ring_shift(value, by, sections=0):
    peers, layers = lax.axis_size("exp"), lax.axis_size("section")
    order = ring_order(peers)
    pairs = []
    for rep in range(lax.axis_size("rep")):
        step = by if rep % 2 == 0 else -by
        for layer in range(layers):
            source = (rep * layers + layer) * peers
            target = (rep * layers + (layer + sections) % layers) * peers
            for spot in range(peers):
                pairs.append((source + order[spot], target + order[(spot + step) % peers]))
    return lax.ppermute(value, ("rep", "section", "exp"), pairs)


def from_behind(value, axis, by):
    peers = lax.axis_size(axis)
    return lax.ppermute(value, axis, [(i, (i + by) % peers) for i in range(peers)])


def dot(a, b, dims):
    return lax.dot_general(a, b, (dims, ((), ())), preferred_element_type=F32)


def whole():
    return pl.BlockSpec(memory_space=pltpu.VMEM)


def turned(value):
    rows, columns = value.shape
    wide = jnp.concatenate([value, jnp.zeros((rows, 128 - columns), F32)], axis=1)
    return wide.T[:columns]


def pack_kernel(experts, codes_ref, exps_ref, routes_ref, weight_ref, grad_ref, out_ref):
    tokens, width = codes_ref.shape
    blocks = exps_ref.shape[0]
    scales = jnp.exp2(exps_ref[...].astype(F32))
    scales = turned(jnp.concatenate([scales, jnp.zeros((128 - blocks, tokens), F32)], axis=0))
    per = width // blocks
    for b in range(blocks):
        cols = slice(b * per, (b + 1) * per)
        out_ref[:, cols] = (codes_ref[:, cols].astype(F32) * scales[:, b : b + 1]).astype(BF16)
    expert = lax.broadcasted_iota(jnp.int32, (experts, tokens), 0)
    table = jnp.zeros((experts, tokens), F32)
    for k in range(routes_ref.shape[0]):
        table += jnp.where(routes_ref[k : k + 1, :] == expert, weight_ref[k : k + 1, :], 0.0)
    high = table.astype(BF16).astype(F32)
    middle = (table - high).astype(BF16).astype(F32)
    low = table - high - middle
    out_ref[:, width : 2 * width] = grad_ref[...]
    extra = out_ref.shape[1] - 2 * width
    parts = [high, middle, low]
    if extra > 3 * experts:
        parts.append(jnp.zeros((extra - 3 * experts, tokens), F32))
    out_ref[:, 2 * width :] = turned(jnp.concatenate(parts, axis=0)).astype(BF16)


LAST = ((1,), (1,))
PLAIN = ((1,), (0,))
TILE = 256


def columns_of(width, body):
    def step(n, carry):
        body(n * TILE)
        return carry

    lax.fori_loop(0, width // TILE, step, 0, unroll=2)


def span(start):
    return pl.ds(pl.multiple_of(start, TILE), TILE)


def load_kernel(*refs):
    count = len(refs) // 2
    copies = [
        pltpu.make_async_copy(refs[i], refs[count + i], refs[-1].at[i]) for i in range(count)
    ]
    for copy in copies:
        copy.start()
    for copy in copies:
        copy.wait()


def load_call(weights):
    return pl.pallas_call(
        load_kernel,
        out_shape=[jax.ShapeDtypeStruct(w.shape, w.dtype) for w in weights],
        in_specs=[pl.BlockSpec(memory_space=pl.ANY)] * len(weights),
        out_specs=[whole()] * len(weights),
        scratch_shapes=[pltpu.SemaphoreType.DMA((len(weights),))],
        compiler_params=pltpu.CompilerParams(vmem_limit_bytes=8 * 2**20),
        cost_estimate=pl.CostEstimate(
            flops=0, bytes_accessed=sum(4 * w.size for w in weights), transcendentals=0
        ),
        name="load_weights",
    )(*weights)


def expert_kernel(count, experts, local_experts, *refs):
    blocks = refs[:count]
    weights = refs[count : count + 6]
    outs = refs[count + 6 : 2 * count + 6]
    saved = refs[2 * count + 6 : 2 * count + 9]
    rows, left = refs[2 * count + 9 :]
    half, width = weights[0].shape
    tokens = blocks[0].shape[0]
    tables = []
    for i, block in enumerate(blocks):
        rows[0, i * tokens : (i + 1) * tokens] = block[:, :width]
        rows[1, i * tokens : (i + 1) * tokens] = block[:, width : 2 * width]
        tables.append(block[:, 2 * width :].astype(F32))
    table = jnp.concatenate(tables, axis=0).T
    expert_of = lax.rem(lax.broadcasted_iota(jnp.int32, table.shape, 0), experts)
    first = lax.axis_index("exp") * local_experts
    scales = [
        jnp.sum(jnp.where(expert_of == first + e, table, 0.0), axis=0, keepdims=True)
        for e in range(local_experts)
    ]
    unit = lax.broadcasted_iota(jnp.int32, (half, 1), 0)
    scale = scales[0]
    for e in range(1, local_experts):
        scale = jnp.where(unit >= e * (half // local_experts), scales[e], scale)
    for side in range(2):
        at = slice(side * half, (side + 1) * half)
        gate = dot(weights[3 * side][...], rows[0], LAST)
        up = dot(weights[3 * side + 1][...], rows[0], LAST)
        back = dot(weights[3 * side + 2][...], rows[1], LAST) * scale
        sig = 1.0 / (1.0 + jnp.exp(-gate))
        swish = gate * sig
        results = (
            back * up * sig * (1.0 + gate * (1.0 - sig)),
            back * swish,
            swish * up * scale,
        )
        for kind, result in enumerate(results):
            result = result.astype(BF16)
            saved[kind][at, :] = result
            left[kind, :, at] = result.T

    def column(start):
        at, later = span(start), span(width + start)
        right = [
            jnp.concatenate([weights[kind][:, at], weights[3 + kind][:, at]], axis=0)
            for kind in range(3)
        ]
        output = dot(left[2], right[2], PLAIN).astype(BF16)
        grad = (dot(left[0], right[0], PLAIN) + dot(left[1], right[1], PLAIN)).astype(BF16)
        for i, out in enumerate(outs):
            out[:, at] = output[i * tokens : (i + 1) * tokens]
            out[:, later] = grad[i * tokens : (i + 1) * tokens]

    columns_of(width, column)


def expert_call(blocks, weights, experts, local_experts):
    count, tokens = len(blocks), blocks[0].shape[0]
    half, width = weights[0].shape
    units, rows = 2 * half, count * tokens
    results = pl.pallas_call(
        functools.partial(expert_kernel, count, experts, local_experts),
        out_shape=[jax.ShapeDtypeStruct((tokens, 2 * width), BF16)] * count
        + [jax.ShapeDtypeStruct((units, rows), BF16)] * 3,
        in_specs=[whole()] * (count + 6),
        out_specs=[whole()] * (count + 3),
        scratch_shapes=[
            pltpu.VMEM((2, rows, width), BF16),
            pltpu.VMEM((3, rows, units), BF16),
        ],
        compiler_params=pltpu.CompilerParams(vmem_limit_bytes=vmem(experts // local_experts)),
        cost_estimate=pl.CostEstimate(
            flops=6 * 2 * rows * units * width,
            bytes_accessed=6 * units * width + 8 * rows * width,
            transcendentals=rows * units,
        ),
        name="expert_rows",
    )(*blocks, *weights)
    return results[:count], results[count:]


def weight_kernel(groups, count, *refs):
    blocks = refs[:count]
    kept = [refs[count + g * 3 : count + g * 3 + 3] for g in range(groups)]
    outs, across = refs[-7:-1], refs[-1]
    half, width = outs[0].shape
    for kind in range(3):
        start = 0
        for group in kept:
            size = group[kind].shape[1]
            across[kind, :, start : start + size] = group[kind][...]
            start += size

    def column(start):
        at, later = span(start), span(width + start)
        right = [
            jnp.concatenate([b[:, at] for b in blocks], axis=0),
            jnp.concatenate([b[:, later] for b in blocks], axis=0),
        ]
        for kind in range(3):
            total = dot(across[kind], right[kind // 2], PLAIN).astype(BF16)
            outs[kind][:, at] = total[:half]
            outs[3 + kind][:, at] = total[half:]

    columns_of(width, column)


def weight_call(blocks, kept, width, peers):
    count = len(blocks)
    units = kept[0][0].shape[0]
    half, total = units // 2, count * blocks[0].shape[0]
    results = pl.pallas_call(
        functools.partial(weight_kernel, len(kept), count),
        out_shape=[jax.ShapeDtypeStruct((half, width), BF16)] * 6,
        in_specs=[whole()] * (count + 3 * len(kept)),
        out_specs=[whole()] * 6,
        scratch_shapes=[pltpu.VMEM((3, units, total), BF16)],
        compiler_params=pltpu.CompilerParams(vmem_limit_bytes=vmem(peers)),
        cost_estimate=pl.CostEstimate(
            flops=3 * 2 * total * units * width,
            bytes_accessed=4 * total * width + 12 * half * width,
            transcendentals=0,
        ),
        name="weight_grads",
    )(*blocks, *[k for group in kept for k in group])
    return results[:3], results[3:]


def add(a, b):
    return (a.astype(F32) + b.astype(F32)).astype(BF16)


def shards(
    row_codes, block_exponents, routes, route_weight, out_grad, gate_weight, up_weight, down_weight
):
    tokens, width = row_codes.shape[1:]
    local_experts, half_units = gate_weight.shape[1:3]
    half = local_experts * half_units
    peers = lax.axis_size("exp")
    experts = peers * local_experts
    lanes = -(-3 * experts // 128) * 128
    shards_of = [w.reshape(half, width) for w in (gate_weight, up_weight, down_weight)]
    other = [from_behind(w, "rep", 1) for w in shards_of]
    home = pl.pallas_call(
        functools.partial(pack_kernel, experts),
        out_shape=jax.ShapeDtypeStruct((tokens, 2 * width + lanes), BF16),
        in_specs=[whole()] * 5,
        out_specs=whole(),
        compiler_params=pltpu.CompilerParams(vmem_limit_bytes=60 * 2**20),
        name="pack_rows",
    )(row_codes[0], block_exponents[0].T, routes[0].T, route_weight[0].T, out_grad[0])

    tie = lax.optimization_barrier
    shards_of = tie((home, shards_of))[1]
    own = load_call(shards_of[:1]) + load_call(shards_of[1:])
    weights = list(own) + other
    ahead, behind = peers // 2, peers // 2 - 1
    names = [("near", 0)]
    for k in range(1, ahead + 1):
        names += [("near", k), ("far", k)]
    names = names[: 2 * ahead]
    groups = [names[i : i + 4] for i in range(0, len(names) - 4, 4)]
    groups += [names[-4:-2], names[-2:]]
    held = {("near", 0): home, ("far", 0): tie((home, own))[0]}
    partial, kept = {}, []

    def work(group):
        outs, saved = expert_call(
            [held[name] for name in group], weights, experts, local_experts
        )
        partial.update(zip(group, outs))
        kept.append(saved)

    for k in range(1, ahead + 1):
        held["near", k] = ring_shift(held["near", k - 1], 1)
        if k == 1:
            held["near", 1], own = tie((held["near", 1], own))
            weights[:3] = own
        if k % 2 == 1 and k > 1:
            work(groups[(k - 3) // 2])
            held["far", k - 1], kept[-1] = tie((held["far", k - 1], kept[-1]))
        if k <= behind:
            held["far", k] = ring_shift(held["far", k - 1], -1)
    work(groups[-2])
    outs, back = slice(0, width), slice(width, 2 * width)
    early_far = from_behind(partial["far", 1][:, back], "section", -1)
    arrived = [held[name] for name in groups[-1]]
    arrived, kept[-1], early_far = tie((arrived, kept[-1], early_far))
    held.update(zip(groups[-1], arrived))
    work(groups[-1])
    blocks = [held[name] for group in groups for name in group]

    near_sum = partial["near", ahead]
    far_sum = ring_shift(partial["far", behind], 1)
    for k in range(ahead, 4, -1):
        near_sum, far_sum = tie((ring_shift(near_sum, -1), far_sum))
        near_sum = add(near_sum, partial["near", k - 1])
        far_sum = ring_shift(add(far_sum, partial["far", k - 2]), 1)

    near_sum = ring_shift(near_sum, -1)
    here = partial["near", 0]
    early_near = from_behind(partial["near", 1][:, back], "section", -1)
    home_back = from_behind(add(home[:, back], here[:, back]), "section", -1)
    own_total, other_total = weight_call(blocks, kept, width, peers)
    near_sum, far_sum, early_near, home_back, own_total, other_total, here = tie(
        (near_sum, far_sum, early_near, home_back, own_total, other_total, here)
    )

    near_sum = ring_shift(add(near_sum, partial["near", 3]), -1)
    far_outs = ring_shift(add(far_sum[:, outs], partial["far", 2][:, outs]), 1)
    far_back = ring_shift(add(far_sum[:, back], partial["far", 2][:, back]), 1, -1)
    home_outs = from_behind(add(home[:, outs], here[:, outs]), "section", 1)
    near_sum, far_outs, far_back, home_outs = tie((near_sum, far_outs, far_back, home_outs))

    near_outs = add(near_sum[:, outs], partial["near", 2][:, outs])
    near_back = add(near_sum[:, back], partial["near", 2][:, back])
    far_outs = add(far_outs, partial["far", 1][:, outs])
    far_back = add(far_back, early_far)
    near_outs, near_back, other_total = tie((near_outs, near_back, other_total))
    received = [from_behind(g, "rep", 1) for g in other_total]
    near_outs, near_back = ring_shift(near_outs, -1), ring_shift(near_back, -1, -1)
    far_outs, far_back = ring_shift(far_outs, 1, 1), ring_shift(far_back, 1)
    near_outs, near_back, far_outs, far_back = tie((near_outs, near_back, far_outs, far_back))

    near_outs = ring_shift(add(near_outs, partial["near", 1][:, outs]), -1, 1)
    near_back = ring_shift(add(near_back, early_near), -1)
    totals = [add(a, b) for a, b in zip(own_total, received)]
    near_outs, near_back, totals = tie((near_outs, near_back, totals))
    results = [
        sum(f.astype(F32) for f in final).astype(BF16)[None]
        for final in ((home_outs, near_outs, far_outs), (home_back, near_back, far_back))
    ]
    shape = (1, local_experts, half_units, width)
    return tuple(results) + tuple(t.reshape(shape) for t in totals)


def solution(mesh):
    tokens = P("section", ("rep", "exp"), None)
    weights = P("section", "exp", "rep", None)
    return jax.shard_map(
        shards,
        mesh=mesh,
        in_specs=(tokens,) * 5 + (weights,) * 3,
        out_specs=(tokens,) * 2 + (weights,) * 3,
        check_vma=False,
    )
```

```python
import functools
import jax
import jax.numpy as jnp
from jax import lax
from jax.experimental import pallas as pl
from jax.experimental.pallas import tpu as pltpu
from jax.sharding import PartitionSpec as P

F32 = jnp.float32
BF16 = jnp.bfloat16


def vmem(peers):
    return (24 if peers <= 8 else 60) * 2**20


def ring_order(peers):
    width = 1
    while 8 * width * width <= peers:
        width *= 2
    depth = peers // width
    if width == 1 or depth % 2:
        return list(range(peers))
    order = [z * width for z in range(depth)]
    for back, z in enumerate(reversed(range(depth))):
        columns = list(range(1, width))
        order += [z * width + x for x in (columns if back % 2 == 0 else reversed(columns))]
    return order


def ring_shift(value, by, sections=0):
    peers, layers = lax.axis_size("exp"), lax.axis_size("section")
    order = ring_order(peers)
    pairs = []
    for rep in range(lax.axis_size("rep")):
        step = by if rep % 2 == 0 else -by
        for layer in range(layers):
            source = (rep * layers + layer) * peers
            target = (rep * layers + (layer + sections) % layers) * peers
            for spot in range(peers):
                pairs.append((source + order[spot], target + order[(spot + step) % peers]))
    return lax.ppermute(value, ("rep", "section", "exp"), pairs)


def from_behind(value, axis, by):
    peers = lax.axis_size(axis)
    return lax.ppermute(value, axis, [(i, (i + by) % peers) for i in range(peers)])


def dot(a, b, dims):
    return lax.dot_general(a, b, (dims, ((), ())), preferred_element_type=F32)


def whole():
    return pl.BlockSpec(memory_space=pltpu.VMEM)


def turned(value):
    rows, columns = value.shape
    wide = jnp.concatenate([value, jnp.zeros((rows, 128 - columns), F32)], axis=1)
    return wide.T[:columns]


def pack_kernel(experts, codes_ref, exps_ref, routes_ref, weight_ref, grad_ref, out_ref):
    tokens, width = codes_ref.shape
    blocks = exps_ref.shape[0]
    scales = jnp.exp2(exps_ref[...].astype(F32))
    scales = turned(jnp.concatenate([scales, jnp.zeros((128 - blocks, tokens), F32)], axis=0))
    per = width // blocks
    for b in range(blocks):
        cols = slice(b * per, (b + 1) * per)
        out_ref[:, cols] = (codes_ref[:, cols].astype(F32) * scales[:, b : b + 1]).astype(BF16)
    expert = lax.broadcasted_iota(jnp.int32, (experts, tokens), 0)
    table = jnp.zeros((experts, tokens), F32)
    for k in range(routes_ref.shape[0]):
        table += jnp.where(routes_ref[k : k + 1, :] == expert, weight_ref[k : k + 1, :], 0.0)
    high = table.astype(BF16).astype(F32)
    middle = (table - high).astype(BF16).astype(F32)
    low = table - high - middle
    out_ref[:, width : 2 * width] = grad_ref[...]
    extra = out_ref.shape[1] - 2 * width
    parts = [high, middle, low]
    if extra > 3 * experts:
        parts.append(jnp.zeros((extra - 3 * experts, tokens), F32))
    out_ref[:, 2 * width :] = turned(jnp.concatenate(parts, axis=0)).astype(BF16)


LAST = ((1,), (1,))
PLAIN = ((1,), (0,))
TILE = 256


def columns_of(width, body):
    def step(n, carry):
        body(n * TILE)
        return carry

    lax.fori_loop(0, width // TILE, step, 0, unroll=2)


def span(start):
    return pl.ds(pl.multiple_of(start, TILE), TILE)


def load_kernel(*refs):
    count = len(refs) // 2
    copies = [
        pltpu.make_async_copy(refs[i], refs[count + i], refs[-1].at[i]) for i in range(count)
    ]
    for copy in copies:
        copy.start()
    for copy in copies:
        copy.wait()


def load_call(weights):
    return pl.pallas_call(
        load_kernel,
        out_shape=[jax.ShapeDtypeStruct(w.shape, w.dtype) for w in weights],
        in_specs=[pl.BlockSpec(memory_space=pl.ANY)] * len(weights),
        out_specs=[whole()] * len(weights),
        scratch_shapes=[pltpu.SemaphoreType.DMA((len(weights),))],
        compiler_params=pltpu.CompilerParams(vmem_limit_bytes=8 * 2**20),
        cost_estimate=pl.CostEstimate(
            flops=0, bytes_accessed=sum(4 * w.size for w in weights), transcendentals=0
        ),
        name="load_weights",
    )(*weights)


def expert_kernel(count, experts, local_experts, *refs):
    blocks = refs[:count]
    weights = refs[count : count + 6]
    outs = refs[count + 6 : 2 * count + 6]
    saved = refs[2 * count + 6 : 2 * count + 9]
    rows, left = refs[2 * count + 9 :]
    half, width = weights[0].shape
    tokens = blocks[0].shape[0]
    tables = []
    for i, block in enumerate(blocks):
        rows[0, i * tokens : (i + 1) * tokens] = block[:, :width]
        rows[1, i * tokens : (i + 1) * tokens] = block[:, width : 2 * width]
        tables.append(block[:, 2 * width :].astype(F32))
    table = jnp.concatenate(tables, axis=0).T
    expert_of = lax.rem(lax.broadcasted_iota(jnp.int32, table.shape, 0), experts)
    first = lax.axis_index("exp") * local_experts
    scales = [
        jnp.sum(jnp.where(expert_of == first + e, table, 0.0), axis=0, keepdims=True)
        for e in range(local_experts)
    ]
    unit = lax.broadcasted_iota(jnp.int32, (half, 1), 0)
    scale = scales[0]
    for e in range(1, local_experts):
        scale = jnp.where(unit >= e * (half // local_experts), scales[e], scale)
    for side in range(2):
        at = slice(side * half, (side + 1) * half)
        gate = dot(weights[3 * side][...], rows[0], LAST)
        up = dot(weights[3 * side + 1][...], rows[0], LAST)
        back = dot(weights[3 * side + 2][...], rows[1], LAST) * scale
        sig = 1.0 / (1.0 + jnp.exp(-gate))
        swish = gate * sig
        results = (
            back * up * sig * (1.0 + gate * (1.0 - sig)),
            back * swish,
            swish * up * scale,
        )
        for kind, result in enumerate(results):
            result = result.astype(BF16)
            saved[kind][at, :] = result
            left[kind, :, at] = result.T

    def column(start):
        at, later = span(start), span(width + start)
        right = [
            jnp.concatenate([weights[kind][:, at], weights[3 + kind][:, at]], axis=0)
            for kind in range(3)
        ]
        output = dot(left[2], right[2], PLAIN).astype(BF16)
        grad = (dot(left[0], right[0], PLAIN) + dot(left[1], right[1], PLAIN)).astype(BF16)
        for i, out in enumerate(outs):
            out[:, at] = output[i * tokens : (i + 1) * tokens]
            out[:, later] = grad[i * tokens : (i + 1) * tokens]

    columns_of(width, column)


def expert_call(blocks, weights, experts, local_experts):
    count, tokens = len(blocks), blocks[0].shape[0]
    half, width = weights[0].shape
    units, rows = 2 * half, count * tokens
    results = pl.pallas_call(
        functools.partial(expert_kernel, count, experts, local_experts),
        out_shape=[jax.ShapeDtypeStruct((tokens, 2 * width), BF16)] * count
        + [jax.ShapeDtypeStruct((units, rows), BF16)] * 3,
        in_specs=[whole()] * (count + 6),
        out_specs=[whole()] * (count + 3),
        scratch_shapes=[
            pltpu.VMEM((2, rows, width), BF16),
            pltpu.VMEM((3, rows, units), BF16),
        ],
        compiler_params=pltpu.CompilerParams(vmem_limit_bytes=vmem(experts // local_experts)),
        cost_estimate=pl.CostEstimate(
            flops=6 * 2 * rows * units * width,
            bytes_accessed=6 * units * width + 8 * rows * width,
            transcendentals=rows * units,
        ),
        name="expert_rows",
    )(*blocks, *weights)
    return results[:count], results[count:]


def weight_kernel(groups, count, *refs):
    blocks = refs[:count]
    kept = [refs[count + g * 3 : count + g * 3 + 3] for g in range(groups)]
    outs, across = refs[-7:-1], refs[-1]
    half, width = outs[0].shape
    for kind in range(3):
        start = 0
        for group in kept:
            size = group[kind].shape[1]
            across[kind, :, start : start + size] = group[kind][...]
            start += size

    def column(start):
        at, later = span(start), span(width + start)
        right = [
            jnp.concatenate([b[:, at] for b in blocks], axis=0),
            jnp.concatenate([b[:, later] for b in blocks], axis=0),
        ]
        for kind in range(3):
            total = dot(across[kind], right[kind // 2], PLAIN).astype(BF16)
            outs[kind][:, at] = total[:half]
            outs[3 + kind][:, at] = total[half:]

    columns_of(width, column)


def weight_call(blocks, kept, width, peers):
    count = len(blocks)
    units = kept[0][0].shape[0]
    half, total = units // 2, count * blocks[0].shape[0]
    results = pl.pallas_call(
        functools.partial(weight_kernel, len(kept), count),
        out_shape=[jax.ShapeDtypeStruct((half, width), BF16)] * 6,
        in_specs=[whole()] * (count + 3 * len(kept)),
        out_specs=[whole()] * 6,
        scratch_shapes=[pltpu.VMEM((3, units, total), BF16)],
        compiler_params=pltpu.CompilerParams(vmem_limit_bytes=vmem(peers)),
        cost_estimate=pl.CostEstimate(
            flops=3 * 2 * total * units * width,
            bytes_accessed=4 * total * width + 12 * half * width,
            transcendentals=0,
        ),
        name="weight_grads",
    )(*blocks, *[k for group in kept for k in group])
    return results[:3], results[3:]


def add(a, b):
    return (a.astype(F32) + b.astype(F32)).astype(BF16)


def shards(
    row_codes, block_exponents, routes, route_weight, out_grad, gate_weight, up_weight, down_weight
):
    tokens, width = row_codes.shape[1:]
    local_experts, half_units = gate_weight.shape[1:3]
    half = local_experts * half_units
    peers = lax.axis_size("exp")
    experts = peers * local_experts
    lanes = -(-3 * experts // 128) * 128
    shards_of = [w.reshape(half, width) for w in (gate_weight, up_weight, down_weight)]
    other = [from_behind(w, "rep", 1) for w in shards_of]
    home = pl.pallas_call(
        functools.partial(pack_kernel, experts),
        out_shape=jax.ShapeDtypeStruct((tokens, 2 * width + lanes), BF16),
        in_specs=[whole()] * 5,
        out_specs=whole(),
        compiler_params=pltpu.CompilerParams(vmem_limit_bytes=60 * 2**20),
        name="pack_rows",
    )(row_codes[0], block_exponents[0].T, routes[0].T, route_weight[0].T, out_grad[0])

    tie = lax.optimization_barrier
    shards_of = tie((home, shards_of))[1]
    own = load_call(shards_of[:1]) + load_call(shards_of[1:])
    weights = list(own) + other
    ahead, behind = peers // 2, peers // 2 - 1
    names = [("near", 0)]
    for k in range(1, ahead + 1):
        names += [("near", k), ("far", k)]
    names = names[: 2 * ahead]
    groups = [names[i : i + 2] for i in range(0, len(names) - 4, 2)]
    groups.append([name for name in names[-4:] if name[0] == "far"])
    groups.append([name for name in names[-4:] if name[0] == "near"])
    held = {("near", 0): home, ("far", 0): tie((home, own))[0]}
    partial, kept = {}, []

    def work(group):
        outs, saved = expert_call(
            [held[name] for name in group], weights, experts, local_experts
        )
        partial.update(zip(group, outs))
        kept.append(saved)

    for k in range(1, ahead + 1):
        held["near", k] = ring_shift(held["near", k - 1], 1)
        if k == 1:
            held["near", 1], own = tie((held["near", 1], own))
            weights[:3] = own
        elif k <= behind:
            work(groups[k - 2])
            held["far", k - 1], kept[-1] = tie((held["far", k - 1], kept[-1]))
        if k <= behind:
            held["far", k] = ring_shift(held["far", k - 1], -1)
    work(groups[-2])
    far_sum = ring_shift(partial["far", behind], 1)
    held["near", ahead], kept[-1] = tie((held["near", ahead], kept[-1]))
    work(groups[-1])
    both = (slice(0, width), slice(width, 2 * width))
    near_sum, far_sum = tie((partial["near", ahead], far_sum))
    own_total = received = None
    blocks = [held[name] for group in groups for name in group]
    steps = (1, -1)
    finals = []
    here, near_sum = tie((partial["near", 0], near_sum))
    for part, step in zip(both, steps):
        kept_here = add(home[:, part], here[:, part])
        finals.append([from_behind(kept_here, "section", step)])
    for k in range(ahead, 1, -1):
        near_sum = ring_shift(near_sum, -1)
        left = k - 2
        if left > 1:
            far_done, far_next = far_sum, add(far_sum, partial["far", left])
            far_sum = ring_shift(far_next, 1)
            near_sum, _ = tie((near_sum, far_done))
        if k == 4:
            kept[-1], _ = tie((kept[-1], far_next))
            own_total, other_total = weight_call(blocks, kept, width, peers)
            near_sum, own_total, other_total = tie((near_sum, own_total, other_total))
        if k == 3:
            lasts = [add(far_sum[:, part], partial["far", 1][:, part]) for part in both]
            for final, last, step in zip(finals, lasts, steps):
                final.append(ring_shift(last, 1, step))
            here = [final[0] for final in finals] + finals[0][1:]
            near_sum, _ = tie((near_sum, here))
            near_sum = add(near_sum, partial["near", 2])
        elif k == 2:
            here = [final[1] for final in finals]
            near_sum, other_total, _ = tie((near_sum, other_total, here))
            received = [from_behind(g, "rep", 1) for g in other_total]
        elif k > 2:
            near_sum = add(near_sum, partial["near", k - 1])
    lasts = [add(near_sum[:, part], partial["near", 1][:, part]) for part in both]
    for final, last, step in zip(finals, lasts, steps):
        final.append(ring_shift(last, -1, step))
    totals = [add(a, b) for a, b in zip(own_total, received)]
    finals, totals = tie((finals, totals))
    results = [sum(f.astype(F32) for f in final).astype(BF16)[None] for final in finals]
    shape = (1, local_experts, half_units, width)
    return tuple(results) + tuple(t.reshape(shape) for t in totals)


def solution(mesh):
    tokens = P("section", ("rep", "exp"), None)
    weights = P("section", "exp", "rep", None)
    return jax.shard_map(
        shards,
        mesh=mesh,
        in_specs=(tokens,) * 5 + (weights,) * 3,
        out_specs=(tokens,) * 2 + (weights,) * 3,
        check_vma=False,
    )
```

```python
import functools
import jax
import jax.numpy as jnp
from jax import lax
from jax.experimental import pallas as pl
from jax.experimental.pallas import tpu as pltpu
from jax.sharding import PartitionSpec as P

F32 = jnp.float32
BF16 = jnp.bfloat16


def vmem(peers):
    return (24 if peers <= 8 else 60) * 2**20


def ring_order(peers):
    width = 1
    while 8 * width * width <= peers:
        width *= 2
    depth = peers // width
    if width == 1 or depth % 2:
        return list(range(peers))
    order = [z * width for z in range(depth)]
    for back, z in enumerate(reversed(range(depth))):
        columns = list(range(1, width))
        order += [z * width + x for x in (columns if back % 2 == 0 else reversed(columns))]
    return order


def ring_shift(value, by, sections=0):
    peers, layers = lax.axis_size("exp"), lax.axis_size("section")
    order = ring_order(peers)
    pairs = []
    for rep in range(lax.axis_size("rep")):
        step = by if rep % 2 == 0 else -by
        for layer in range(layers):
            source = (rep * layers + layer) * peers
            target = (rep * layers + (layer + sections) % layers) * peers
            for spot in range(peers):
                pairs.append((source + order[spot], target + order[(spot + step) % peers]))
    return lax.ppermute(value, ("rep", "section", "exp"), pairs)


def from_behind(value, axis, by):
    peers = lax.axis_size(axis)
    return lax.ppermute(value, axis, [(i, (i + by) % peers) for i in range(peers)])


def dot(a, b, dims):
    return lax.dot_general(a, b, (dims, ((), ())), preferred_element_type=F32)


def whole():
    return pl.BlockSpec(memory_space=pltpu.VMEM)


def turned(value):
    rows, columns = value.shape
    wide = jnp.concatenate([value, jnp.zeros((rows, 128 - columns), F32)], axis=1)
    return wide.T[:columns]


def pack_kernel(experts, codes_ref, exps_ref, routes_ref, weight_ref, grad_ref, out_ref):
    tokens, width = codes_ref.shape
    blocks = exps_ref.shape[0]
    scales = jnp.exp2(exps_ref[...].astype(F32))
    scales = turned(jnp.concatenate([scales, jnp.zeros((128 - blocks, tokens), F32)], axis=0))
    per = width // blocks
    for b in range(blocks):
        cols = slice(b * per, (b + 1) * per)
        out_ref[:, cols] = (codes_ref[:, cols].astype(F32) * scales[:, b : b + 1]).astype(BF16)
    expert = lax.broadcasted_iota(jnp.int32, (experts, tokens), 0)
    table = jnp.zeros((experts, tokens), F32)
    for k in range(routes_ref.shape[0]):
        table += jnp.where(routes_ref[k : k + 1, :] == expert, weight_ref[k : k + 1, :], 0.0)
    high = table.astype(BF16).astype(F32)
    middle = (table - high).astype(BF16).astype(F32)
    low = table - high - middle
    out_ref[:, width : 2 * width] = grad_ref[...]
    extra = out_ref.shape[1] - 2 * width
    parts = [high, middle, low]
    if extra > 3 * experts:
        parts.append(jnp.zeros((extra - 3 * experts, tokens), F32))
    out_ref[:, 2 * width :] = turned(jnp.concatenate(parts, axis=0)).astype(BF16)


LAST = ((1,), (1,))
PLAIN = ((1,), (0,))
TILE = 256


def columns_of(width, body):
    def step(n, carry):
        body(n * TILE)
        return carry

    lax.fori_loop(0, width // TILE, step, 0, unroll=2)


def span(start):
    return pl.ds(pl.multiple_of(start, TILE), TILE)


def load_kernel(*refs):
    count = len(refs) // 2
    copies = [
        pltpu.make_async_copy(refs[i], refs[count + i], refs[-1].at[i]) for i in range(count)
    ]
    for copy in copies:
        copy.start()
    for copy in copies:
        copy.wait()


def load_call(weights):
    return pl.pallas_call(
        load_kernel,
        out_shape=[jax.ShapeDtypeStruct(w.shape, w.dtype) for w in weights],
        in_specs=[pl.BlockSpec(memory_space=pl.ANY)] * len(weights),
        out_specs=[whole()] * len(weights),
        scratch_shapes=[pltpu.SemaphoreType.DMA((len(weights),))],
        compiler_params=pltpu.CompilerParams(vmem_limit_bytes=8 * 2**20),
        cost_estimate=pl.CostEstimate(
            flops=0, bytes_accessed=sum(4 * w.size for w in weights), transcendentals=0
        ),
        name="load_weights",
    )(*weights)


def expert_kernel(count, experts, local_experts, *refs):
    blocks = refs[:count]
    weights = refs[count : count + 6]
    outs = refs[count + 6 : 2 * count + 6]
    saved = refs[2 * count + 6 : 2 * count + 9]
    rows, left = refs[2 * count + 9 :]
    half, width = weights[0].shape
    tokens = blocks[0].shape[0]
    tables = []
    for i, block in enumerate(blocks):
        rows[0, i * tokens : (i + 1) * tokens] = block[:, :width]
        rows[1, i * tokens : (i + 1) * tokens] = block[:, width : 2 * width]
        tables.append(block[:, 2 * width :].astype(F32))
    table = jnp.concatenate(tables, axis=0).T
    expert_of = lax.rem(lax.broadcasted_iota(jnp.int32, table.shape, 0), experts)
    first = lax.axis_index("exp") * local_experts
    scales = [
        jnp.sum(jnp.where(expert_of == first + e, table, 0.0), axis=0, keepdims=True)
        for e in range(local_experts)
    ]
    unit = lax.broadcasted_iota(jnp.int32, (half, 1), 0)
    scale = scales[0]
    for e in range(1, local_experts):
        scale = jnp.where(unit >= e * (half // local_experts), scales[e], scale)
    for side in range(2):
        at = slice(side * half, (side + 1) * half)
        gate = dot(weights[3 * side][...], rows[0], LAST)
        up = dot(weights[3 * side + 1][...], rows[0], LAST)
        back = dot(weights[3 * side + 2][...], rows[1], LAST) * scale
        sig = 1.0 / (1.0 + jnp.exp(-gate))
        swish = gate * sig
        results = (
            back * up * sig * (1.0 + gate * (1.0 - sig)),
            back * swish,
            swish * up * scale,
        )
        for kind, result in enumerate(results):
            result = result.astype(BF16)
            saved[kind][at, :] = result
            left[kind, :, at] = result.T

    def column(start):
        at, later = span(start), span(width + start)
        right = [
            jnp.concatenate([weights[kind][:, at], weights[3 + kind][:, at]], axis=0)
            for kind in range(3)
        ]
        output = dot(left[2], right[2], PLAIN).astype(BF16)
        grad = (dot(left[0], right[0], PLAIN) + dot(left[1], right[1], PLAIN)).astype(BF16)
        for i, out in enumerate(outs):
            out[:, at] = output[i * tokens : (i + 1) * tokens]
            out[:, later] = grad[i * tokens : (i + 1) * tokens]

    columns_of(width, column)


def expert_call(blocks, weights, experts, local_experts):
    count, tokens = len(blocks), blocks[0].shape[0]
    half, width = weights[0].shape
    units, rows = 2 * half, count * tokens
    results = pl.pallas_call(
        functools.partial(expert_kernel, count, experts, local_experts),
        out_shape=[jax.ShapeDtypeStruct((tokens, 2 * width), BF16)] * count
        + [jax.ShapeDtypeStruct((units, rows), BF16)] * 3,
        in_specs=[whole()] * (count + 6),
        out_specs=[whole()] * (count + 3),
        scratch_shapes=[
            pltpu.VMEM((2, rows, width), BF16),
            pltpu.VMEM((3, rows, units), BF16),
        ],
        compiler_params=pltpu.CompilerParams(vmem_limit_bytes=vmem(experts // local_experts)),
        cost_estimate=pl.CostEstimate(
            flops=6 * 2 * rows * units * width,
            bytes_accessed=6 * units * width + 8 * rows * width,
            transcendentals=rows * units,
        ),
        name="expert_rows",
    )(*blocks, *weights)
    return results[:count], results[count:]


def weight_kernel(groups, count, *refs):
    blocks = refs[:count]
    kept = [refs[count + g * 3 : count + g * 3 + 3] for g in range(groups)]
    outs, across = refs[-7:-1], refs[-1]
    half, width = outs[0].shape
    for kind in range(3):
        start = 0
        for group in kept:
            size = group[kind].shape[1]
            across[kind, :, start : start + size] = group[kind][...]
            start += size

    def column(start):
        at, later = span(start), span(width + start)
        right = [
            jnp.concatenate([b[:, at] for b in blocks], axis=0),
            jnp.concatenate([b[:, later] for b in blocks], axis=0),
        ]
        for kind in range(3):
            total = dot(across[kind], right[kind // 2], PLAIN).astype(BF16)
            outs[kind][:, at] = total[:half]
            outs[3 + kind][:, at] = total[half:]

    columns_of(width, column)


def weight_call(blocks, kept, width, peers):
    count = len(blocks)
    units = kept[0][0].shape[0]
    half, total = units // 2, count * blocks[0].shape[0]
    results = pl.pallas_call(
        functools.partial(weight_kernel, len(kept), count),
        out_shape=[jax.ShapeDtypeStruct((half, width), BF16)] * 6,
        in_specs=[whole()] * (count + 3 * len(kept)),
        out_specs=[whole()] * 6,
        scratch_shapes=[pltpu.VMEM((3, units, total), BF16)],
        compiler_params=pltpu.CompilerParams(vmem_limit_bytes=vmem(peers)),
        cost_estimate=pl.CostEstimate(
            flops=3 * 2 * total * units * width,
            bytes_accessed=4 * total * width + 12 * half * width,
            transcendentals=0,
        ),
        name="weight_grads",
    )(*blocks, *[k for group in kept for k in group])
    return results[:3], results[3:]


def add(a, b):
    return (a.astype(F32) + b.astype(F32)).astype(BF16)


def shards(
    row_codes, block_exponents, routes, route_weight, out_grad, gate_weight, up_weight, down_weight
):
    tokens, width = row_codes.shape[1:]
    local_experts, half_units = gate_weight.shape[1:3]
    half = local_experts * half_units
    peers = lax.axis_size("exp")
    experts = peers * local_experts
    lanes = -(-3 * experts // 128) * 128
    shards_of = [w.reshape(half, width) for w in (gate_weight, up_weight, down_weight)]
    other = [from_behind(w, "rep", 1) for w in shards_of]
    home = pl.pallas_call(
        functools.partial(pack_kernel, experts),
        out_shape=jax.ShapeDtypeStruct((tokens, 2 * width + lanes), BF16),
        in_specs=[whole()] * 5,
        out_specs=whole(),
        compiler_params=pltpu.CompilerParams(vmem_limit_bytes=60 * 2**20),
        name="pack_rows",
    )(row_codes[0], block_exponents[0].T, routes[0].T, route_weight[0].T, out_grad[0])

    tie = lax.optimization_barrier
    shards_of = tie((home, shards_of))[1]
    own = load_call(shards_of[:1]) + load_call(shards_of[1:])
    weights = list(own) + other
    ahead, behind = peers // 2, peers // 2 - 1
    names = [("near", 0)]
    for k in range(1, ahead + 1):
        names += [("near", k), ("far", k)]
    names = names[: 2 * ahead]
    groups = [names[i : i + 4] for i in range(0, len(names) - 4, 4)]
    groups.append([name for name in names[-4:] if name[0] == "far"])
    groups.append([name for name in names[-4:] if name[0] == "near"])
    held = {("near", 0): home, ("far", 0): tie((home, own))[0]}
    partial, kept = {}, []

    def work(group):
        outs, saved = expert_call(
            [held[name] for name in group], weights, experts, local_experts
        )
        partial.update(zip(group, outs))
        kept.append(saved)

    for k in range(1, ahead + 1):
        held["near", k] = ring_shift(held["near", k - 1], 1)
        if k <= behind:
            held["far", k] = ring_shift(held["far", k - 1], -1)
        if k == 1:
            held["near", 1], own = tie((held["near", 1], own))
            weights[:3] = own
        if k % 2 == 1 and k > 1:
            work(groups[(k - 3) // 2])
            held["near", k], kept[-1] = tie((held["near", k], kept[-1]))
    work(groups[-2])
    far_sum = ring_shift(partial["far", behind], 1)
    held["near", ahead], kept[-1] = tie((held["near", ahead], kept[-1]))
    work(groups[-1])
    both = (slice(0, width), slice(width, 2 * width))
    near_sum = partial["near", ahead]
    own_total = received = None
    blocks = [held[name] for group in groups for name in group]
    steps = (1, -1)
    finals = []
    for part, step in zip(both, steps):
        kept_here = add(home[:, part], partial["near", 0][:, part])
        finals.append([from_behind(kept_here, "section", step)])
    for k in range(ahead, 1, -1):
        near_sum = ring_shift(near_sum, -1)
        left = k - 2
        if left > 1:
            far_done = far_sum
            far_sum = ring_shift(add(far_sum, partial["far", left]), 1)
            near_sum, _ = tie((near_sum, far_done))
        if k == 3:
            own_total, other_total = weight_call(blocks, kept, width, peers)
            here = [final[0] for final in finals]
            near_sum, own_total, other_total, _ = tie((near_sum, own_total, other_total, here))
            lasts = [add(far_sum[:, part], partial["far", 1][:, part]) for part in both]
            for final, last, step in zip(finals, lasts, steps):
                final.append(ring_shift(last, 1, step))
            near_sum, _ = tie((near_sum, lasts))
            near_sum = add(near_sum, partial["near", 2])
            near_sum, other_total = tie((near_sum, other_total))
            received = [from_behind(g, "rep", 1) for g in other_total]
        elif k == 2:
            here = [final[1] for final in finals]
            near_sum, _ = tie((near_sum, here))
        elif k > 2:
            near_sum = add(near_sum, partial["near", k - 1])
    lasts = [add(near_sum[:, part], partial["near", 1][:, part]) for part in both]
    for final, last, step in zip(finals, lasts, steps):
        final.append(ring_shift(last, -1, step))
    totals = [add(a, b) for a, b in zip(own_total, received)]
    finals, totals = tie((finals, totals))
    results = [sum(f.astype(F32) for f in final).astype(BF16)[None] for final in finals]
    shape = (1, local_experts, half_units, width)
    return tuple(results) + tuple(t.reshape(shape) for t in totals)


def solution(mesh):
    tokens = P("section", ("rep", "exp"), None)
    weights = P("section", "exp", "rep", None)
    return jax.shard_map(
        shards,
        mesh=mesh,
        in_specs=(tokens,) * 5 + (weights,) * 3,
        out_specs=(tokens,) * 2 + (weights,) * 3,
        check_vma=False,
    )
```

```python
import functools
import jax
import jax.numpy as jnp
from jax import lax
from jax.experimental import pallas as pl
from jax.experimental.pallas import tpu as pltpu
from jax.sharding import PartitionSpec as P

F32 = jnp.float32
BF16 = jnp.bfloat16


def vmem(peers):
    return (24 if peers <= 8 else 60) * 2**20


def ring_order(peers):
    width = 1
    while 8 * width * width <= peers:
        width *= 2
    depth = peers // width
    if width == 1 or depth % 2:
        return list(range(peers))
    order = [z * width for z in range(depth)]
    for back, z in enumerate(reversed(range(depth))):
        columns = list(range(1, width))
        order += [z * width + x for x in (columns if back % 2 == 0 else reversed(columns))]
    return order


def ring_shift(value, by, sections=0):
    peers, layers = lax.axis_size("exp"), lax.axis_size("section")
    order = ring_order(peers)
    pairs = []
    for rep in range(lax.axis_size("rep")):
        step = by if rep % 2 == 0 else -by
        for layer in range(layers):
            source = (rep * layers + layer) * peers
            target = (rep * layers + (layer + sections) % layers) * peers
            for spot in range(peers):
                pairs.append((source + order[spot], target + order[(spot + step) % peers]))
    return lax.ppermute(value, ("rep", "section", "exp"), pairs)


def from_behind(value, axis, by):
    peers = lax.axis_size(axis)
    return lax.ppermute(value, axis, [(i, (i + by) % peers) for i in range(peers)])


def dot(a, b, dims):
    return lax.dot_general(a, b, (dims, ((), ())), preferred_element_type=F32)


def whole():
    return pl.BlockSpec(memory_space=pltpu.VMEM)


def turned(value):
    rows, columns = value.shape
    wide = jnp.concatenate([value, jnp.zeros((rows, 128 - columns), F32)], axis=1)
    return wide.T[:columns]


def pack_kernel(experts, codes_ref, exps_ref, routes_ref, weight_ref, grad_ref, out_ref):
    tokens, width = codes_ref.shape
    blocks = exps_ref.shape[0]
    scales = jnp.exp2(exps_ref[...].astype(F32))
    scales = turned(jnp.concatenate([scales, jnp.zeros((128 - blocks, tokens), F32)], axis=0))
    per = width // blocks
    for b in range(blocks):
        cols = slice(b * per, (b + 1) * per)
        out_ref[:, cols] = (codes_ref[:, cols].astype(F32) * scales[:, b : b + 1]).astype(BF16)
    expert = lax.broadcasted_iota(jnp.int32, (experts, tokens), 0)
    table = jnp.zeros((experts, tokens), F32)
    for k in range(routes_ref.shape[0]):
        table += jnp.where(routes_ref[k : k + 1, :] == expert, weight_ref[k : k + 1, :], 0.0)
    high = table.astype(BF16).astype(F32)
    middle = (table - high).astype(BF16).astype(F32)
    low = table - high - middle
    out_ref[:, width : 2 * width] = grad_ref[...]
    extra = out_ref.shape[1] - 2 * width
    parts = [high, middle, low]
    if extra > 3 * experts:
        parts.append(jnp.zeros((extra - 3 * experts, tokens), F32))
    out_ref[:, 2 * width :] = turned(jnp.concatenate(parts, axis=0)).astype(BF16)


LAST = ((1,), (1,))
PLAIN = ((1,), (0,))
TILE = 256


def columns_of(width, body):
    def step(n, carry):
        body(n * TILE)
        return carry

    lax.fori_loop(0, width // TILE, step, 0, unroll=2)


def span(start):
    return pl.ds(pl.multiple_of(start, TILE), TILE)


def load_kernel(*refs):
    count = len(refs) // 2
    copies = [
        pltpu.make_async_copy(refs[i], refs[count + i], refs[-1].at[i]) for i in range(count)
    ]
    for copy in copies:
        copy.start()
    for copy in copies:
        copy.wait()


def load_call(weights):
    return pl.pallas_call(
        load_kernel,
        out_shape=[jax.ShapeDtypeStruct(w.shape, w.dtype) for w in weights],
        in_specs=[pl.BlockSpec(memory_space=pl.ANY)] * len(weights),
        out_specs=[whole()] * len(weights),
        scratch_shapes=[pltpu.SemaphoreType.DMA((len(weights),))],
        compiler_params=pltpu.CompilerParams(vmem_limit_bytes=8 * 2**20),
        cost_estimate=pl.CostEstimate(
            flops=0, bytes_accessed=sum(4 * w.size for w in weights), transcendentals=0
        ),
        name="load_weights",
    )(*weights)


def expert_kernel(count, experts, local_experts, *refs):
    blocks = refs[:count]
    weights = refs[count : count + 6]
    outs = refs[count + 6 : 2 * count + 6]
    saved = refs[2 * count + 6 : 2 * count + 9]
    rows, left = refs[2 * count + 9 :]
    half, width = weights[0].shape
    tokens = blocks[0].shape[0]
    tables = []
    for i, block in enumerate(blocks):
        rows[0, i * tokens : (i + 1) * tokens] = block[:, :width]
        rows[1, i * tokens : (i + 1) * tokens] = block[:, width : 2 * width]
        tables.append(block[:, 2 * width :].astype(F32))
    table = jnp.concatenate(tables, axis=0).T
    expert_of = lax.rem(lax.broadcasted_iota(jnp.int32, table.shape, 0), experts)
    first = lax.axis_index("exp") * local_experts
    scales = [
        jnp.sum(jnp.where(expert_of == first + e, table, 0.0), axis=0, keepdims=True)
        for e in range(local_experts)
    ]
    unit = lax.broadcasted_iota(jnp.int32, (half, 1), 0)
    scale = scales[0]
    for e in range(1, local_experts):
        scale = jnp.where(unit >= e * (half // local_experts), scales[e], scale)
    for side in range(2):
        at = slice(side * half, (side + 1) * half)
        gate = dot(weights[3 * side][...], rows[0], LAST)
        up = dot(weights[3 * side + 1][...], rows[0], LAST)
        back = dot(weights[3 * side + 2][...], rows[1], LAST) * scale
        sig = 1.0 / (1.0 + jnp.exp(-gate))
        swish = gate * sig
        results = (
            back * up * sig * (1.0 + gate * (1.0 - sig)),
            back * swish,
            swish * up * scale,
        )
        for kind, result in enumerate(results):
            result = result.astype(BF16)
            saved[kind][at, :] = result
            left[kind, :, at] = result.T

    def column(start):
        at, later = span(start), span(width + start)
        right = [
            jnp.concatenate([weights[kind][:, at], weights[3 + kind][:, at]], axis=0)
            for kind in range(3)
        ]
        output = dot(left[2], right[2], PLAIN).astype(BF16)
        grad = (dot(left[0], right[0], PLAIN) + dot(left[1], right[1], PLAIN)).astype(BF16)
        for i, out in enumerate(outs):
            out[:, at] = output[i * tokens : (i + 1) * tokens]
            out[:, later] = grad[i * tokens : (i + 1) * tokens]

    columns_of(width, column)


def expert_call(blocks, weights, experts, local_experts):
    count, tokens = len(blocks), blocks[0].shape[0]
    half, width = weights[0].shape
    units, rows = 2 * half, count * tokens
    results = pl.pallas_call(
        functools.partial(expert_kernel, count, experts, local_experts),
        out_shape=[jax.ShapeDtypeStruct((tokens, 2 * width), BF16)] * count
        + [jax.ShapeDtypeStruct((units, rows), BF16)] * 3,
        in_specs=[whole()] * (count + 6),
        out_specs=[whole()] * (count + 3),
        scratch_shapes=[
            pltpu.VMEM((2, rows, width), BF16),
            pltpu.VMEM((3, rows, units), BF16),
        ],
        compiler_params=pltpu.CompilerParams(vmem_limit_bytes=vmem(experts // local_experts)),
        cost_estimate=pl.CostEstimate(
            flops=6 * 2 * rows * units * width,
            bytes_accessed=6 * units * width + 8 * rows * width,
            transcendentals=rows * units,
        ),
        name="expert_rows",
    )(*blocks, *weights)
    return results[:count], results[count:]


def weight_kernel(groups, count, *refs):
    blocks = refs[:count]
    kept = [refs[count + g * 3 : count + g * 3 + 3] for g in range(groups)]
    outs, other, across = refs[-5:-2], refs[-2], refs[-1]
    half, width = outs[0].shape
    for kind in range(3):
        start = 0
        for group in kept:
            size = group[kind].shape[1]
            across[kind, :, start : start + size] = group[kind][...]
            start += size

    def column(start):
        at, later = span(start), span(width + start)
        right = [
            jnp.concatenate([b[:, at] for b in blocks], axis=0),
            jnp.concatenate([b[:, later] for b in blocks], axis=0),
        ]
        for kind in range(3):
            total = dot(across[kind], right[kind // 2], PLAIN).astype(BF16)
            outs[kind][:, at] = total[:half]
            other[kind, :, at] = total[half:]

    columns_of(width, column)


def weight_call(blocks, kept, width, peers):
    count = len(blocks)
    units = kept[0][0].shape[0]
    half, total = units // 2, count * blocks[0].shape[0]
    results = pl.pallas_call(
        functools.partial(weight_kernel, len(kept), count),
        out_shape=[jax.ShapeDtypeStruct((half, width), BF16)] * 3
        + [jax.ShapeDtypeStruct((3, half, width), BF16)],
        in_specs=[whole()] * (count + 3 * len(kept)),
        out_specs=[whole()] * 4,
        scratch_shapes=[pltpu.VMEM((3, units, total), BF16)],
        compiler_params=pltpu.CompilerParams(vmem_limit_bytes=vmem(peers)),
        cost_estimate=pl.CostEstimate(
            flops=3 * 2 * total * units * width,
            bytes_accessed=4 * total * width + 12 * half * width,
            transcendentals=0,
        ),
        name="weight_grads",
    )(*blocks, *[k for group in kept for k in group])
    return results[:3], results[3]


def add(a, b):
    return (a.astype(F32) + b.astype(F32)).astype(BF16)


def shards(
    row_codes, block_exponents, routes, route_weight, out_grad, gate_weight, up_weight, down_weight
):
    tokens, width = row_codes.shape[1:]
    local_experts, half_units = gate_weight.shape[1:3]
    half = local_experts * half_units
    peers = lax.axis_size("exp")
    experts = peers * local_experts
    lanes = -(-3 * experts // 128) * 128
    shards_of = [w.reshape(half, width) for w in (gate_weight, up_weight, down_weight)]
    other = [from_behind(w, "rep", 1) for w in shards_of]
    home = pl.pallas_call(
        functools.partial(pack_kernel, experts),
        out_shape=jax.ShapeDtypeStruct((tokens, 2 * width + lanes), BF16),
        in_specs=[whole()] * 5,
        out_specs=whole(),
        compiler_params=pltpu.CompilerParams(vmem_limit_bytes=60 * 2**20),
        name="pack_rows",
    )(row_codes[0], block_exponents[0].T, routes[0].T, route_weight[0].T, out_grad[0])

    tie = lax.optimization_barrier
    shards_of = tie((home, shards_of))[1]
    own = load_call(shards_of[:1]) + load_call(shards_of[1:])
    weights = list(own) + other
    ahead, behind = peers // 2, peers // 2 - 1
    names = [("near", 0)]
    for k in range(1, ahead + 1):
        names += [("near", k), ("far", k)]
    names = names[: 2 * ahead]
    groups = [names[i : i + 4] for i in range(0, len(names) - 4, 4)]
    groups += [names[-4:-2], names[-2:]]
    held = {("near", 0): home, ("far", 0): tie((home, own))[0]}
    partial, kept = {}, []

    def work(group):
        outs, saved = expert_call(
            [held[name] for name in group], weights, experts, local_experts
        )
        partial.update(zip(group, outs))
        kept.append(saved)

    for k in range(1, ahead + 1):
        held["near", k] = ring_shift(held["near", k - 1], 1)
        if k == 1:
            held["near", 1], own = tie((held["near", 1], own))
            weights[:3] = own
        if k % 2 == 1 and k > 1:
            work(groups[(k - 3) // 2])
            held["far", k - 1], kept[-1] = tie((held["far", k - 1], kept[-1]))
        if k <= behind:
            held["far", k] = ring_shift(held["far", k - 1], -1)
    work(groups[-2])
    arrived = [held[name] for name in groups[-1]]
    arrived, kept[-1] = tie((arrived, kept[-1]))
    held.update(zip(groups[-1], arrived))
    work(groups[-1])
    far_sum = ring_shift(partial["far", behind], 1)
    both, steps = (slice(0, width), slice(width, 2 * width)), (1, -1)
    if lax.axis_size("section") == 2:
        both, steps = (slice(0, 2 * width),), (1,)
    near_sum = partial["near", ahead]
    own_total = received = None
    blocks = [held[name] for group in groups for name in group]
    finals = []
    for part, step in zip(both, steps):
        kept_here = add(home[:, part], partial["near", 0][:, part])
        finals.append([from_behind(kept_here, "section", step)])
    here = [final[0] for final in finals]
    for k in range(ahead, 1, -1):
        near_sum = ring_shift(near_sum, -1)
        near_sum, far_sum = tie((near_sum, far_sum))
        if k == 4:
            near_sum, far_sum, _ = tie((near_sum, far_sum, here))
        if k == 3:
            own_total, other_total = weight_call(blocks, kept, width, peers)
            near_sum, far_sum, own_total, other_total = tie(
                (near_sum, far_sum, own_total, other_total)
            )
        if k > 2:
            near_sum = add(near_sum, partial["near", k - 1])
        if k > 3:
            far_sum = ring_shift(add(far_sum, partial["far", k - 2]), 1)
        elif k == 3:
            lasts = [add(far_sum[:, part], partial["far", 1][:, part]) for part in both]
            near_sum, lasts, other_total = tie((near_sum, lasts, other_total))
            for final, last, step in zip(finals, lasts, steps):
                final.append(ring_shift(last, 1, step))
            far_sum = [final[1] for final in finals]
            received = from_behind(other_total, "rep", 1)
    lasts = [add(near_sum[:, part], partial["near", 1][:, part]) for part in both]
    for final, last, step in zip(finals, lasts, steps):
        final.append(ring_shift(last, -1, step))
    totals = [add(a, b) for a, b in zip(own_total, received)]
    finals, totals = tie((finals, totals))
    results = [sum(f.astype(F32) for f in final).astype(BF16)[None] for final in finals]
    if len(results) == 1:
        results = [results[0][:, :, :width], results[0][:, :, width:]]
    shape = (1, local_experts, half_units, width)
    return tuple(results) + tuple(t.reshape(shape) for t in totals)


def solution(mesh):
    tokens = P("section", ("rep", "exp"), None)
    weights = P("section", "exp", "rep", None)
    return jax.shard_map(
        shards,
        mesh=mesh,
        in_specs=(tokens,) * 5 + (weights,) * 3,
        out_specs=(tokens,) * 2 + (weights,) * 3,
        check_vma=False,
    )
```

```python
import functools
import jax
import jax.numpy as jnp
from jax import lax
from jax.experimental import pallas as pl
from jax.experimental.pallas import tpu as pltpu
from jax.sharding import PartitionSpec as P

F32 = jnp.float32
BF16 = jnp.bfloat16


def vmem(peers):
    return (24 if peers <= 8 else 60) * 2**20


def ring_order(peers):
    width = 1
    while 8 * width * width <= peers:
        width *= 2
    depth = peers // width
    if width == 1 or depth % 2:
        return list(range(peers))
    order = [z * width for z in range(depth)]
    for back, z in enumerate(reversed(range(depth))):
        columns = list(range(1, width))
        order += [z * width + x for x in (columns if back % 2 == 0 else reversed(columns))]
    return order


def ring_shift(value, by, sections=0):
    peers, layers = lax.axis_size("exp"), lax.axis_size("section")
    order = ring_order(peers)
    pairs = []
    for rep in range(lax.axis_size("rep")):
        step = by if rep % 2 == 0 else -by
        for layer in range(layers):
            source = (rep * layers + layer) * peers
            target = (rep * layers + (layer + sections) % layers) * peers
            for spot in range(peers):
                pairs.append((source + order[spot], target + order[(spot + step) % peers]))
    return lax.ppermute(value, ("rep", "section", "exp"), pairs)


def from_behind(value, axis, by):
    peers = lax.axis_size(axis)
    return lax.ppermute(value, axis, [(i, (i + by) % peers) for i in range(peers)])


def dot(a, b, dims):
    return lax.dot_general(a, b, (dims, ((), ())), preferred_element_type=F32)


def whole():
    return pl.BlockSpec(memory_space=pltpu.VMEM)


def turned(value):
    rows, columns = value.shape
    wide = jnp.concatenate([value, jnp.zeros((rows, 128 - columns), F32)], axis=1)
    return wide.T[:columns]


def pack_kernel(experts, codes_ref, exps_ref, routes_ref, weight_ref, grad_ref, out_ref):
    tokens, width = codes_ref.shape
    blocks = exps_ref.shape[0]
    scales = jnp.exp2(exps_ref[...].astype(F32))
    scales = turned(jnp.concatenate([scales, jnp.zeros((128 - blocks, tokens), F32)], axis=0))
    per = width // blocks
    for b in range(blocks):
        cols = slice(b * per, (b + 1) * per)
        out_ref[:, cols] = (codes_ref[:, cols].astype(F32) * scales[:, b : b + 1]).astype(BF16)
    expert = lax.broadcasted_iota(jnp.int32, (experts, tokens), 0)
    table = jnp.zeros((experts, tokens), F32)
    for k in range(routes_ref.shape[0]):
        table += jnp.where(routes_ref[k : k + 1, :] == expert, weight_ref[k : k + 1, :], 0.0)
    high = table.astype(BF16).astype(F32)
    middle = (table - high).astype(BF16).astype(F32)
    low = table - high - middle
    out_ref[:, width : 2 * width] = grad_ref[...]
    extra = out_ref.shape[1] - 2 * width
    parts = [high, middle, low]
    if extra > 3 * experts:
        parts.append(jnp.zeros((extra - 3 * experts, tokens), F32))
    out_ref[:, 2 * width :] = turned(jnp.concatenate(parts, axis=0)).astype(BF16)


LAST = ((1,), (1,))
PLAIN = ((1,), (0,))
TILE = 256


def columns_of(width, body):
    def step(n, carry):
        body(n * TILE)
        return carry

    lax.fori_loop(0, width // TILE, step, 0, unroll=2)


def span(start):
    return pl.ds(pl.multiple_of(start, TILE), TILE)


def load_kernel(*refs):
    count = len(refs) // 2
    copies = [
        pltpu.make_async_copy(refs[i], refs[count + i], refs[-1].at[i]) for i in range(count)
    ]
    for copy in copies:
        copy.start()
    for copy in copies:
        copy.wait()


def load_call(weights):
    return pl.pallas_call(
        load_kernel,
        out_shape=[jax.ShapeDtypeStruct(w.shape, w.dtype) for w in weights],
        in_specs=[pl.BlockSpec(memory_space=pl.ANY)] * len(weights),
        out_specs=[whole()] * len(weights),
        scratch_shapes=[pltpu.SemaphoreType.DMA((len(weights),))],
        compiler_params=pltpu.CompilerParams(vmem_limit_bytes=8 * 2**20),
        cost_estimate=pl.CostEstimate(
            flops=0, bytes_accessed=sum(4 * w.size for w in weights), transcendentals=0
        ),
        name="load_weights",
    )(*weights)


def expert_kernel(count, experts, local_experts, *refs):
    blocks = refs[:count]
    weights = refs[count : count + 6]
    outs = refs[count + 6 : 2 * count + 6]
    saved = refs[2 * count + 6 : 2 * count + 9]
    rows, left = refs[2 * count + 9 :]
    half, width = weights[0].shape
    tokens = blocks[0].shape[0]
    tables = []
    for i, block in enumerate(blocks):
        rows[0, i * tokens : (i + 1) * tokens] = block[:, :width]
        rows[1, i * tokens : (i + 1) * tokens] = block[:, width : 2 * width]
        tables.append(block[:, 2 * width :].astype(F32))
    table = jnp.concatenate(tables, axis=0).T
    expert_of = lax.rem(lax.broadcasted_iota(jnp.int32, table.shape, 0), experts)
    first = lax.axis_index("exp") * local_experts
    scales = [
        jnp.sum(jnp.where(expert_of == first + e, table, 0.0), axis=0, keepdims=True)
        for e in range(local_experts)
    ]
    unit = lax.broadcasted_iota(jnp.int32, (half, 1), 0)
    scale = scales[0]
    for e in range(1, local_experts):
        scale = jnp.where(unit >= e * (half // local_experts), scales[e], scale)
    for side in range(2):
        at = slice(side * half, (side + 1) * half)
        gate = dot(weights[3 * side][...], rows[0], LAST)
        up = dot(weights[3 * side + 1][...], rows[0], LAST)
        back = dot(weights[3 * side + 2][...], rows[1], LAST) * scale
        sig = 1.0 / (1.0 + jnp.exp(-gate))
        swish = gate * sig
        results = (
            back * up * sig * (1.0 + gate * (1.0 - sig)),
            back * swish,
            swish * up * scale,
        )
        for kind, result in enumerate(results):
            result = result.astype(BF16)
            saved[kind][at, :] = result
            left[kind, :, at] = result.T

    def column(start):
        at, later = span(start), span(width + start)
        right = [
            jnp.concatenate([weights[kind][:, at], weights[3 + kind][:, at]], axis=0)
            for kind in range(3)
        ]
        output = dot(left[2], right[2], PLAIN).astype(BF16)
        grad = (dot(left[0], right[0], PLAIN) + dot(left[1], right[1], PLAIN)).astype(BF16)
        for i, out in enumerate(outs):
            out[:, at] = output[i * tokens : (i + 1) * tokens]
            out[:, later] = grad[i * tokens : (i + 1) * tokens]

    columns_of(width, column)


def expert_call(blocks, weights, experts, local_experts):
    count, tokens = len(blocks), blocks[0].shape[0]
    half, width = weights[0].shape
    units, rows = 2 * half, count * tokens
    results = pl.pallas_call(
        functools.partial(expert_kernel, count, experts, local_experts),
        out_shape=[jax.ShapeDtypeStruct((tokens, 2 * width), BF16)] * count
        + [jax.ShapeDtypeStruct((units, rows), BF16)] * 3,
        in_specs=[whole()] * (count + 6),
        out_specs=[whole()] * (count + 3),
        scratch_shapes=[
            pltpu.VMEM((2, rows, width), BF16),
            pltpu.VMEM((3, rows, units), BF16),
        ],
        compiler_params=pltpu.CompilerParams(vmem_limit_bytes=vmem(experts // local_experts)),
        cost_estimate=pl.CostEstimate(
            flops=6 * 2 * rows * units * width,
            bytes_accessed=6 * units * width + 8 * rows * width,
            transcendentals=rows * units,
        ),
        name="expert_rows",
    )(*blocks, *weights)
    return results[:count], results[count:]


def weight_kernel(groups, count, *refs):
    blocks = refs[:count]
    kept = [refs[count + g * 3 : count + g * 3 + 3] for g in range(groups)]
    outs, other, across = refs[-5:-2], refs[-2], refs[-1]
    half, width = outs[0].shape
    for kind in range(3):
        start = 0
        for group in kept:
            size = group[kind].shape[1]
            across[kind, :, start : start + size] = group[kind][...]
            start += size

    def column(start):
        at, later = span(start), span(width + start)
        right = [
            jnp.concatenate([b[:, at] for b in blocks], axis=0),
            jnp.concatenate([b[:, later] for b in blocks], axis=0),
        ]
        for kind in range(3):
            total = dot(across[kind], right[kind // 2], PLAIN).astype(BF16)
            outs[kind][:, at] = total[:half]
            other[kind, :, at] = total[half:]

    columns_of(width, column)


def weight_call(blocks, kept, width, peers):
    count = len(blocks)
    units = kept[0][0].shape[0]
    half, total = units // 2, count * blocks[0].shape[0]
    results = pl.pallas_call(
        functools.partial(weight_kernel, len(kept), count),
        out_shape=[jax.ShapeDtypeStruct((half, width), BF16)] * 3
        + [jax.ShapeDtypeStruct((3, half, width), BF16)],
        in_specs=[whole()] * (count + 3 * len(kept)),
        out_specs=[whole()] * 4,
        scratch_shapes=[pltpu.VMEM((3, units, total), BF16)],
        compiler_params=pltpu.CompilerParams(vmem_limit_bytes=vmem(peers)),
        cost_estimate=pl.CostEstimate(
            flops=3 * 2 * total * units * width,
            bytes_accessed=4 * total * width + 12 * half * width,
            transcendentals=0,
        ),
        name="weight_grads",
    )(*blocks, *[k for group in kept for k in group])
    return results[:3], results[3]


def add(a, b):
    return (a.astype(F32) + b.astype(F32)).astype(BF16)


def shards(
    row_codes, block_exponents, routes, route_weight, out_grad, gate_weight, up_weight, down_weight
):
    tokens, width = row_codes.shape[1:]
    local_experts, half_units = gate_weight.shape[1:3]
    half = local_experts * half_units
    peers = lax.axis_size("exp")
    experts = peers * local_experts
    lanes = -(-3 * experts // 128) * 128
    shards_of = [w.reshape(half, width) for w in (gate_weight, up_weight, down_weight)]
    home = pl.pallas_call(
        functools.partial(pack_kernel, experts),
        out_shape=jax.ShapeDtypeStruct((tokens, 2 * width + lanes), BF16),
        in_specs=[whole()] * 5,
        out_specs=whole(),
        compiler_params=pltpu.CompilerParams(vmem_limit_bytes=60 * 2**20),
        name="pack_rows",
    )(row_codes[0], block_exponents[0].T, routes[0].T, route_weight[0].T, out_grad[0])

    tie = lax.optimization_barrier
    other = [from_behind(w, "rep", 1) for w in shards_of]
    shards_of = tie((home, shards_of))[1]
    own = load_call(shards_of[:1]) + load_call(shards_of[1:])
    weights = list(own) + other
    ahead, behind = peers // 2, peers // 2 - 1
    names = [("near", 0)]
    for k in range(1, ahead + 1):
        names += [("near", k), ("far", k)]
    names = names[: 2 * ahead]
    groups = [names[i : i + 4] for i in range(0, len(names) - 4, 4)]
    groups.append([name for name in names[-4:] if name[0] == "far"])
    groups.append([name for name in names[-4:] if name[0] == "near"])
    held = {("near", 0): home, ("far", 0): tie((home, own))[0]}
    partial, kept = {}, []

    def work(group):
        outs, saved = expert_call(
            [held[name] for name in group], weights, experts, local_experts
        )
        partial.update(zip(group, outs))
        kept.append(saved)

    for k in range(1, ahead + 1):
        held["near", k] = ring_shift(held["near", k - 1], 1)
        if k <= behind:
            held["far", k] = ring_shift(held["far", k - 1], -1)
        if k == 1:
            held["near", 1], own = tie((held["near", 1], own))
            weights[:3] = own
        if k % 2 == 1 and k > 1:
            work(groups[(k - 3) // 2])
            held["near", k], kept[-1] = tie((held["near", k], kept[-1]))
    work(groups[-2])
    far_sum = ring_shift(partial["far", behind], 1)
    held["near", ahead], kept[-1] = tie((held["near", ahead], kept[-1]))
    work(groups[-1])
    both = (slice(0, width), slice(width, 2 * width))
    near_sum = partial["near", ahead]
    own_total = received = None
    blocks = [held[name] for group in groups for name in group]
    steps = (1, -1)
    home_terms = [
        from_behind(add(home[:, part], partial["near", 0][:, part]), "section", step)
        for part, step in zip(both, steps)
    ]
    joined = [slice(0, 2 * width)] if lax.axis_size("section") == 2 else both

    def crossing(value, by):
        return [ring_shift(value[:, part], by, step) for part, step in zip(joined, steps)]

    def part_of(sent, i):
        return sent[i] if len(sent) == 2 else sent[0][:, both[i]]

    for k in range(ahead, 1, -1):
        near_sum = ring_shift(near_sum, -1)
        left = k - 2
        if left > 1:
            far_done = far_sum
            far_sum = ring_shift(add(far_sum, partial["far", left]), 1)
            near_sum, _ = tie((near_sum, far_done))
        if k == 3:
            own_total, other_total = weight_call(blocks, kept, width, peers)
            near_sum, own_total, other_total, home_terms = tie(
                (near_sum, own_total, other_total, home_terms)
            )
            last = add(far_sum, partial["far", 1])
            far_last = crossing(last, 1)
            near_sum, _ = tie((near_sum, last))
            near_sum = add(near_sum, partial["near", 2])
            near_sum, other_total = tie((near_sum, other_total))
            received = from_behind(other_total, "rep", 1)
        elif k == 2:
            near_sum, far_last = tie((near_sum, far_last))
        elif k > 2:
            near_sum = add(near_sum, partial["near", k - 1])
    near_last = crossing(add(near_sum, partial["near", 1]), -1)
    totals = [add(a, b) for a, b in zip(own_total, received)]
    near_last, totals = tie((near_last, totals))
    results = []
    for i in range(2):
        total = home_terms[i].astype(F32) + part_of(far_last, i).astype(F32)
        total = total + part_of(near_last, i).astype(F32)
        results.append(total.astype(BF16)[None])
    shape = (1, local_experts, half_units, width)
    return tuple(results) + tuple(t.reshape(shape) for t in totals)


def solution(mesh):
    tokens = P("section", ("rep", "exp"), None)
    weights = P("section", "exp", "rep", None)
    return jax.shard_map(
        shards,
        mesh=mesh,
        in_specs=(tokens,) * 5 + (weights,) * 3,
        out_specs=(tokens,) * 2 + (weights,) * 3,
        check_vma=False,
    )
```

```python
import functools
import jax
import jax.numpy as jnp
from jax import lax
from jax.experimental import pallas as pl
from jax.experimental.pallas import tpu as pltpu
from jax.sharding import PartitionSpec as P

F32 = jnp.float32
BF16 = jnp.bfloat16


def vmem(peers):
    return (24 if peers <= 8 else 60) * 2**20


def ring_order(peers):
    width = 1
    while 8 * width * width <= peers:
        width *= 2
    depth = peers // width
    if width == 1 or depth % 2:
        return list(range(peers))
    order = [z * width for z in range(depth)]
    for back, z in enumerate(reversed(range(depth))):
        columns = list(range(1, width))
        order += [z * width + x for x in (columns if back % 2 == 0 else reversed(columns))]
    return order


def ring_shift(value, by, sections=0):
    peers, layers = lax.axis_size("exp"), lax.axis_size("section")
    order = ring_order(peers)
    pairs = []
    for rep in range(lax.axis_size("rep")):
        step = by if rep % 2 == 0 else -by
        for layer in range(layers):
            source = (rep * layers + layer) * peers
            target = (rep * layers + (layer + sections) % layers) * peers
            for spot in range(peers):
                pairs.append((source + order[spot], target + order[(spot + step) % peers]))
    return lax.ppermute(value, ("rep", "section", "exp"), pairs)


def from_behind(value, axis, by):
    peers = lax.axis_size(axis)
    return lax.ppermute(value, axis, [(i, (i + by) % peers) for i in range(peers)])


def dot(a, b, dims):
    return lax.dot_general(a, b, (dims, ((), ())), preferred_element_type=F32)


def whole():
    return pl.BlockSpec(memory_space=pltpu.VMEM)


def turned(value):
    rows, columns = value.shape
    wide = jnp.concatenate([value, jnp.zeros((rows, 128 - columns), F32)], axis=1)
    return wide.T[:columns]


def pack_kernel(experts, codes_ref, exps_ref, routes_ref, weight_ref, grad_ref, out_ref):
    tokens, width = codes_ref.shape
    blocks = exps_ref.shape[0]
    scales = jnp.exp2(exps_ref[...].astype(F32))
    scales = turned(jnp.concatenate([scales, jnp.zeros((128 - blocks, tokens), F32)], axis=0))
    per = width // blocks
    for b in range(blocks):
        cols = slice(b * per, (b + 1) * per)
        out_ref[:, cols] = (codes_ref[:, cols].astype(F32) * scales[:, b : b + 1]).astype(BF16)
    expert = lax.broadcasted_iota(jnp.int32, (experts, tokens), 0)
    table = jnp.zeros((experts, tokens), F32)
    for k in range(routes_ref.shape[0]):
        table += jnp.where(routes_ref[k : k + 1, :] == expert, weight_ref[k : k + 1, :], 0.0)
    high = table.astype(BF16).astype(F32)
    middle = (table - high).astype(BF16).astype(F32)
    low = table - high - middle
    out_ref[:, width : 2 * width] = grad_ref[...]
    extra = out_ref.shape[1] - 2 * width
    parts = [high, middle, low]
    if extra > 3 * experts:
        parts.append(jnp.zeros((extra - 3 * experts, tokens), F32))
    out_ref[:, 2 * width :] = turned(jnp.concatenate(parts, axis=0)).astype(BF16)


LAST = ((1,), (1,))
PLAIN = ((1,), (0,))
TILE = 256


def columns_of(width, body):
    def step(n, carry):
        body(n * TILE)
        return carry

    lax.fori_loop(0, width // TILE, step, 0, unroll=2)


def span(start):
    return pl.ds(pl.multiple_of(start, TILE), TILE)


def load_kernel(*refs):
    count = len(refs) // 2
    copies = [
        pltpu.make_async_copy(refs[i], refs[count + i], refs[-1].at[i]) for i in range(count)
    ]
    for copy in copies:
        copy.start()
    for copy in copies:
        copy.wait()


def load_call(weights):
    return pl.pallas_call(
        load_kernel,
        out_shape=[jax.ShapeDtypeStruct(w.shape, w.dtype) for w in weights],
        in_specs=[pl.BlockSpec(memory_space=pl.ANY)] * len(weights),
        out_specs=[whole()] * len(weights),
        scratch_shapes=[pltpu.SemaphoreType.DMA((len(weights),))],
        compiler_params=pltpu.CompilerParams(vmem_limit_bytes=8 * 2**20),
        cost_estimate=pl.CostEstimate(
            flops=0, bytes_accessed=sum(4 * w.size for w in weights), transcendentals=0
        ),
        name="load_weights",
    )(*weights)


def expert_kernel(count, experts, local_experts, *refs):
    blocks = refs[:count]
    weights = refs[count : count + 6]
    outs = refs[count + 6 : 2 * count + 6]
    saved = refs[2 * count + 6 : 2 * count + 9]
    rows, left = refs[2 * count + 9 :]
    half, width = weights[0].shape
    tokens = blocks[0].shape[0]
    tables = []
    for i, block in enumerate(blocks):
        rows[0, i * tokens : (i + 1) * tokens] = block[:, :width]
        rows[1, i * tokens : (i + 1) * tokens] = block[:, width : 2 * width]
        tables.append(block[:, 2 * width :].astype(F32))
    table = jnp.concatenate(tables, axis=0).T
    expert_of = lax.rem(lax.broadcasted_iota(jnp.int32, table.shape, 0), experts)
    first = lax.axis_index("exp") * local_experts
    scales = [
        jnp.sum(jnp.where(expert_of == first + e, table, 0.0), axis=0, keepdims=True)
        for e in range(local_experts)
    ]
    unit = lax.broadcasted_iota(jnp.int32, (half, 1), 0)
    scale = scales[0]
    for e in range(1, local_experts):
        scale = jnp.where(unit >= e * (half // local_experts), scales[e], scale)
    for side in range(2):
        at = slice(side * half, (side + 1) * half)
        gate = dot(weights[3 * side][...], rows[0], LAST)
        up = dot(weights[3 * side + 1][...], rows[0], LAST)
        back = dot(weights[3 * side + 2][...], rows[1], LAST) * scale
        sig = 1.0 / (1.0 + jnp.exp(-gate))
        swish = gate * sig
        results = (
            back * up * sig * (1.0 + gate * (1.0 - sig)),
            back * swish,
            swish * up * scale,
        )
        for kind, result in enumerate(results):
            result = result.astype(BF16)
            saved[kind][at, :] = result
            left[kind, :, at] = result.T

    def column(start):
        at, later = span(start), span(width + start)
        right = [
            jnp.concatenate([weights[kind][:, at], weights[3 + kind][:, at]], axis=0)
            for kind in range(3)
        ]
        output = dot(left[2], right[2], PLAIN).astype(BF16)
        grad = (dot(left[0], right[0], PLAIN) + dot(left[1], right[1], PLAIN)).astype(BF16)
        for i, out in enumerate(outs):
            out[:, at] = output[i * tokens : (i + 1) * tokens]
            out[:, later] = grad[i * tokens : (i + 1) * tokens]

    columns_of(width, column)


def expert_call(blocks, weights, experts, local_experts):
    count, tokens = len(blocks), blocks[0].shape[0]
    half, width = weights[0].shape
    units, rows = 2 * half, count * tokens
    results = pl.pallas_call(
        functools.partial(expert_kernel, count, experts, local_experts),
        out_shape=[jax.ShapeDtypeStruct((tokens, 2 * width), BF16)] * count
        + [jax.ShapeDtypeStruct((units, rows), BF16)] * 3,
        in_specs=[whole()] * (count + 6),
        out_specs=[whole()] * (count + 3),
        scratch_shapes=[
            pltpu.VMEM((2, rows, width), BF16),
            pltpu.VMEM((3, rows, units), BF16),
        ],
        compiler_params=pltpu.CompilerParams(vmem_limit_bytes=vmem(experts // local_experts)),
        cost_estimate=pl.CostEstimate(
            flops=6 * 2 * rows * units * width,
            bytes_accessed=6 * units * width + 8 * rows * width,
            transcendentals=rows * units,
        ),
        name="expert_rows",
    )(*blocks, *weights)
    return results[:count], results[count:]


def weight_kernel(groups, count, *refs):
    blocks = refs[:count]
    kept = [refs[count + g * 3 : count + g * 3 + 3] for g in range(groups)]
    outs, other, across = refs[-5:-2], refs[-2], refs[-1]
    half, width = outs[0].shape
    for kind in range(3):
        start = 0
        for group in kept:
            size = group[kind].shape[1]
            across[kind, :, start : start + size] = group[kind][...]
            start += size

    def column(start):
        at, later = span(start), span(width + start)
        right = [
            jnp.concatenate([b[:, at] for b in blocks], axis=0),
            jnp.concatenate([b[:, later] for b in blocks], axis=0),
        ]
        for kind in range(3):
            total = dot(across[kind], right[kind // 2], PLAIN).astype(BF16)
            outs[kind][:, at] = total[:half]
            other[kind, :, at] = total[half:]

    columns_of(width, column)


def weight_call(blocks, kept, width, peers):
    count = len(blocks)
    units = kept[0][0].shape[0]
    half, total = units // 2, count * blocks[0].shape[0]
    results = pl.pallas_call(
        functools.partial(weight_kernel, len(kept), count),
        out_shape=[jax.ShapeDtypeStruct((half, width), BF16)] * 3
        + [jax.ShapeDtypeStruct((3, half, width), BF16)],
        in_specs=[whole()] * (count + 3 * len(kept)),
        out_specs=[whole()] * 4,
        scratch_shapes=[pltpu.VMEM((3, units, total), BF16)],
        compiler_params=pltpu.CompilerParams(vmem_limit_bytes=vmem(peers)),
        cost_estimate=pl.CostEstimate(
            flops=3 * 2 * total * units * width,
            bytes_accessed=4 * total * width + 12 * half * width,
            transcendentals=0,
        ),
        name="weight_grads",
    )(*blocks, *[k for group in kept for k in group])
    return results[:3], results[3]


def add(a, b):
    return (a.astype(F32) + b.astype(F32)).astype(BF16)


def shards(
    row_codes, block_exponents, routes, route_weight, out_grad, gate_weight, up_weight, down_weight
):
    tokens, width = row_codes.shape[1:]
    local_experts, half_units = gate_weight.shape[1:3]
    half = local_experts * half_units
    peers = lax.axis_size("exp")
    experts = peers * local_experts
    lanes = -(-3 * experts // 128) * 128
    shards_of = [w.reshape(half, width) for w in (gate_weight, up_weight, down_weight)]
    home = pl.pallas_call(
        functools.partial(pack_kernel, experts),
        out_shape=jax.ShapeDtypeStruct((tokens, 2 * width + lanes), BF16),
        in_specs=[whole()] * 5,
        out_specs=whole(),
        compiler_params=pltpu.CompilerParams(vmem_limit_bytes=60 * 2**20),
        name="pack_rows",
    )(row_codes[0], block_exponents[0].T, routes[0].T, route_weight[0].T, out_grad[0])

    tie = lax.optimization_barrier
    other = [from_behind(w, "rep", 1) for w in shards_of]
    shards_of = tie((home, shards_of))[1]
    own = load_call(shards_of[:1]) + load_call(shards_of[1:])
    weights = list(own) + other
    ahead, behind = peers // 2, peers // 2 - 1
    names = [("near", 0)]
    for k in range(1, ahead + 1):
        names += [("near", k), ("far", k)]
    names = names[: 2 * ahead]
    groups = [names[i : i + 4] for i in range(0, len(names) - 4, 4)]
    groups.append([name for name in names[-4:] if name[0] == "far"])
    groups.append([name for name in names[-4:] if name[0] == "near"])
    held = {("near", 0): home, ("far", 0): tie((home, own))[0]}
    partial, kept = {}, []

    def work(group):
        outs, saved = expert_call(
            [held[name] for name in group], weights, experts, local_experts
        )
        partial.update(zip(group, outs))
        kept.append(saved)

    for k in range(1, ahead + 1):
        held["near", k] = ring_shift(held["near", k - 1], 1)
        if k <= behind:
            held["far", k] = ring_shift(held["far", k - 1], -1)
        if k == 1:
            held["near", 1], own = tie((held["near", 1], own))
            weights[:3] = own
        if k % 2 == 1 and k > 1:
            work(groups[(k - 3) // 2])
            held["near", k], kept[-1] = tie((held["near", k], kept[-1]))
    work(groups[-2])
    far_sum = ring_shift(partial["far", behind], 1)
    held["near", ahead], kept[-1] = tie((held["near", ahead], kept[-1]))
    work(groups[-1])
    both = (slice(0, width), slice(width, 2 * width))
    near_sum = partial["near", ahead]
    own_total = received = None
    blocks = [held[name] for group in groups for name in group]
    outs, back = both
    home_outs = from_behind(add(home[:, outs], partial["near", 0][:, outs]), "section", 1)

    def last_sums(value, term):
        return add(value[:, back], term[:, back]), add(value[:, outs], term[:, outs])

    def last_step(sums, by):
        return ring_shift(sums[0], by), ring_shift(sums[1], by, 1)

    for k in range(ahead, 1, -1):
        near_sum = ring_shift(near_sum, -1)
        left = k - 2
        if left > 1:
            far_done = far_sum
            far_sum = ring_shift(add(far_sum, partial["far", left]), 1)
            near_sum, _ = tie((near_sum, far_done))
        if k == 3:
            own_total, other_total = weight_call(blocks, kept, width, peers)
            near_sum, own_total, other_total, home_outs = tie(
                (near_sum, own_total, other_total, home_outs)
            )
            sums = last_sums(far_sum, partial["far", 1])
            far_last = last_step(sums, 1)
            near_sum, _ = tie((near_sum, sums))
            near_sum = add(near_sum, partial["near", 2])
            near_sum, other_total = tie((near_sum, other_total))
            received = from_behind(other_total, "rep", 1)
        elif k == 2:
            near_sum, far_last = tie((near_sum, far_last))
        elif k > 2:
            near_sum = add(near_sum, partial["near", k - 1])
    near_back, near_outs = last_step(last_sums(near_sum, partial["near", 1]), -1)
    totals = [add(a, b) for a, b in zip(own_total, received)]
    near_back, totals = tie((near_back, totals))

    def total(*terms):
        return sum(term.astype(F32) for term in terms).astype(BF16)[None]

    back_sum = total(home[:, back], partial["near", 0][:, back], far_last[0], near_back)
    results = [
        total(home_outs, far_last[1], near_outs),
        from_behind(back_sum, "section", -1),
    ]
    shape = (1, local_experts, half_units, width)
    return tuple(results) + tuple(t.reshape(shape) for t in totals)


def solution(mesh):
    tokens = P("section", ("rep", "exp"), None)
    weights = P("section", "exp", "rep", None)
    return jax.shard_map(
        shards,
        mesh=mesh,
        in_specs=(tokens,) * 5 + (weights,) * 3,
        out_specs=(tokens,) * 2 + (weights,) * 3,
        check_vma=False,
    )
```

```python
import functools
import jax
import jax.numpy as jnp
from jax import lax
from jax.experimental import pallas as pl
from jax.experimental.pallas import tpu as pltpu
from jax.sharding import PartitionSpec as P

F32 = jnp.float32
BF16 = jnp.bfloat16


def vmem(peers):
    return (24 if peers <= 8 else 60) * 2**20


def ring_order(peers):
    width = 1
    while 8 * width * width <= peers:
        width *= 2
    depth = peers // width
    if width == 1 or depth % 2:
        return list(range(peers))
    order = [z * width for z in range(depth)]
    for back, z in enumerate(reversed(range(depth))):
        columns = list(range(1, width))
        order += [z * width + x for x in (columns if back % 2 == 0 else reversed(columns))]
    return order


def ring_shift(value, by, sections=0):
    peers, layers = lax.axis_size("exp"), lax.axis_size("section")
    order = ring_order(peers)
    pairs = []
    for rep in range(lax.axis_size("rep")):
        step = by if rep % 2 == 0 else -by
        for layer in range(layers):
            source = (rep * layers + layer) * peers
            target = (rep * layers + (layer + sections) % layers) * peers
            for spot in range(peers):
                pairs.append((source + order[spot], target + order[(spot + step) % peers]))
    return lax.ppermute(value, ("rep", "section", "exp"), pairs)


def from_behind(value, axis, by):
    peers = lax.axis_size(axis)
    return lax.ppermute(value, axis, [(i, (i + by) % peers) for i in range(peers)])


def dot(a, b, dims):
    return lax.dot_general(a, b, (dims, ((), ())), preferred_element_type=F32)


def whole():
    return pl.BlockSpec(memory_space=pltpu.VMEM)


def turned(value):
    rows, columns = value.shape
    wide = jnp.concatenate([value, jnp.zeros((rows, 128 - columns), F32)], axis=1)
    return wide.T[:columns]


def pack_kernel(experts, codes_ref, exps_ref, routes_ref, weight_ref, grad_ref, out_ref):
    tokens, width = codes_ref.shape
    blocks = exps_ref.shape[0]
    scales = jnp.exp2(exps_ref[...].astype(F32))
    scales = turned(jnp.concatenate([scales, jnp.zeros((128 - blocks, tokens), F32)], axis=0))
    per = width // blocks
    for b in range(blocks):
        cols = slice(b * per, (b + 1) * per)
        out_ref[:, cols] = (codes_ref[:, cols].astype(F32) * scales[:, b : b + 1]).astype(BF16)
    expert = lax.broadcasted_iota(jnp.int32, (experts, tokens), 0)
    table = jnp.zeros((experts, tokens), F32)
    for k in range(routes_ref.shape[0]):
        table += jnp.where(routes_ref[k : k + 1, :] == expert, weight_ref[k : k + 1, :], 0.0)
    high = table.astype(BF16).astype(F32)
    middle = (table - high).astype(BF16).astype(F32)
    low = table - high - middle
    out_ref[:, width : 2 * width] = grad_ref[...]
    extra = out_ref.shape[1] - 2 * width
    parts = [high, middle, low]
    if extra > 3 * experts:
        parts.append(jnp.zeros((extra - 3 * experts, tokens), F32))
    out_ref[:, 2 * width :] = turned(jnp.concatenate(parts, axis=0)).astype(BF16)


LAST = ((1,), (1,))
PLAIN = ((1,), (0,))
TILE = 256


def columns_of(width, body):
    def step(n, carry):
        body(n * TILE)
        return carry

    lax.fori_loop(0, width // TILE, step, 0, unroll=2)


def span(start):
    return pl.ds(pl.multiple_of(start, TILE), TILE)


def load_kernel(*refs):
    count = len(refs) // 2
    copies = [
        pltpu.make_async_copy(refs[i], refs[count + i], refs[-1].at[i]) for i in range(count)
    ]
    for copy in copies:
        copy.start()
    for copy in copies:
        copy.wait()


def load_call(weights):
    return pl.pallas_call(
        load_kernel,
        out_shape=[jax.ShapeDtypeStruct(w.shape, w.dtype) for w in weights],
        in_specs=[pl.BlockSpec(memory_space=pl.ANY)] * len(weights),
        out_specs=[whole()] * len(weights),
        scratch_shapes=[pltpu.SemaphoreType.DMA((len(weights),))],
        compiler_params=pltpu.CompilerParams(vmem_limit_bytes=8 * 2**20),
        cost_estimate=pl.CostEstimate(
            flops=0, bytes_accessed=sum(4 * w.size for w in weights), transcendentals=0
        ),
        name="load_weights",
    )(*weights)


def expert_kernel(count, experts, local_experts, *refs):
    blocks = refs[:count]
    weights = refs[count : count + 6]
    outs = refs[count + 6 : 2 * count + 6]
    saved = refs[2 * count + 6 : 2 * count + 9]
    rows, left = refs[2 * count + 9 :]
    half, width = weights[0].shape
    tokens = blocks[0].shape[0]
    tables = []
    for i, block in enumerate(blocks):
        rows[0, i * tokens : (i + 1) * tokens] = block[:, :width]
        rows[1, i * tokens : (i + 1) * tokens] = block[:, width : 2 * width]
        tables.append(block[:, 2 * width :].astype(F32))
    table = jnp.concatenate(tables, axis=0).T
    expert_of = lax.rem(lax.broadcasted_iota(jnp.int32, table.shape, 0), experts)
    first = lax.axis_index("exp") * local_experts
    scales = [
        jnp.sum(jnp.where(expert_of == first + e, table, 0.0), axis=0, keepdims=True)
        for e in range(local_experts)
    ]
    unit = lax.broadcasted_iota(jnp.int32, (half, 1), 0)
    scale = scales[0]
    for e in range(1, local_experts):
        scale = jnp.where(unit >= e * (half // local_experts), scales[e], scale)
    for side in range(2):
        at = slice(side * half, (side + 1) * half)
        gate = dot(weights[3 * side][...], rows[0], LAST)
        up = dot(weights[3 * side + 1][...], rows[0], LAST)
        back = dot(weights[3 * side + 2][...], rows[1], LAST) * scale
        sig = 1.0 / (1.0 + jnp.exp(-gate))
        swish = gate * sig
        results = (
            back * up * sig * (1.0 + gate * (1.0 - sig)),
            back * swish,
            swish * up * scale,
        )
        for kind, result in enumerate(results):
            result = result.astype(BF16)
            saved[kind][at, :] = result
            left[kind, :, at] = result.T

    def column(start):
        at, later = span(start), span(width + start)
        right = [
            jnp.concatenate([weights[kind][:, at], weights[3 + kind][:, at]], axis=0)
            for kind in range(3)
        ]
        output = dot(left[2], right[2], PLAIN).astype(BF16)
        grad = (dot(left[0], right[0], PLAIN) + dot(left[1], right[1], PLAIN)).astype(BF16)
        for i, out in enumerate(outs):
            out[:, at] = output[i * tokens : (i + 1) * tokens]
            out[:, later] = grad[i * tokens : (i + 1) * tokens]

    columns_of(width, column)


def expert_call(blocks, weights, experts, local_experts):
    count, tokens = len(blocks), blocks[0].shape[0]
    half, width = weights[0].shape
    units, rows = 2 * half, count * tokens
    results = pl.pallas_call(
        functools.partial(expert_kernel, count, experts, local_experts),
        out_shape=[jax.ShapeDtypeStruct((tokens, 2 * width), BF16)] * count
        + [jax.ShapeDtypeStruct((units, rows), BF16)] * 3,
        in_specs=[whole()] * (count + 6),
        out_specs=[whole()] * (count + 3),
        scratch_shapes=[
            pltpu.VMEM((2, rows, width), BF16),
            pltpu.VMEM((3, rows, units), BF16),
        ],
        compiler_params=pltpu.CompilerParams(vmem_limit_bytes=vmem(experts // local_experts)),
        cost_estimate=pl.CostEstimate(
            flops=6 * 2 * rows * units * width,
            bytes_accessed=6 * units * width + 8 * rows * width,
            transcendentals=rows * units,
        ),
        name="expert_rows",
    )(*blocks, *weights)
    return results[:count], results[count:]


def weight_kernel(groups, count, *refs):
    blocks = refs[:count]
    kept = [refs[count + g * 3 : count + g * 3 + 3] for g in range(groups)]
    outs, other, across = refs[-5:-2], refs[-2], refs[-1]
    half, width = outs[0].shape
    for kind in range(3):
        start = 0
        for group in kept:
            size = group[kind].shape[1]
            across[kind, :, start : start + size] = group[kind][...]
            start += size

    def column(start):
        at, later = span(start), span(width + start)
        right = [
            jnp.concatenate([b[:, at] for b in blocks], axis=0),
            jnp.concatenate([b[:, later] for b in blocks], axis=0),
        ]
        for kind in range(3):
            total = dot(across[kind], right[kind // 2], PLAIN).astype(BF16)
            outs[kind][:, at] = total[:half]
            other[kind, :, at] = total[half:]

    columns_of(width, column)


def weight_call(blocks, kept, width, peers):
    count = len(blocks)
    units = kept[0][0].shape[0]
    half, total = units // 2, count * blocks[0].shape[0]
    results = pl.pallas_call(
        functools.partial(weight_kernel, len(kept), count),
        out_shape=[jax.ShapeDtypeStruct((half, width), BF16)] * 3
        + [jax.ShapeDtypeStruct((3, half, width), BF16)],
        in_specs=[whole()] * (count + 3 * len(kept)),
        out_specs=[whole()] * 4,
        scratch_shapes=[pltpu.VMEM((3, units, total), BF16)],
        compiler_params=pltpu.CompilerParams(vmem_limit_bytes=vmem(peers)),
        cost_estimate=pl.CostEstimate(
            flops=3 * 2 * total * units * width,
            bytes_accessed=4 * total * width + 12 * half * width,
            transcendentals=0,
        ),
        name="weight_grads",
    )(*blocks, *[k for group in kept for k in group])
    return results[:3], results[3]


def add(a, b):
    return (a.astype(F32) + b.astype(F32)).astype(BF16)


def shards(
    row_codes, block_exponents, routes, route_weight, out_grad, gate_weight, up_weight, down_weight
):
    tokens, width = row_codes.shape[1:]
    local_experts, half_units = gate_weight.shape[1:3]
    half = local_experts * half_units
    peers = lax.axis_size("exp")
    experts = peers * local_experts
    lanes = -(-3 * experts // 128) * 128
    shards_of = [w.reshape(half, width) for w in (gate_weight, up_weight, down_weight)]
    other = [from_behind(w, "rep", 1) for w in shards_of]
    home = pl.pallas_call(
        functools.partial(pack_kernel, experts),
        out_shape=jax.ShapeDtypeStruct((tokens, 2 * width + lanes), BF16),
        in_specs=[whole()] * 5,
        out_specs=whole(),
        compiler_params=pltpu.CompilerParams(vmem_limit_bytes=60 * 2**20),
        name="pack_rows",
    )(row_codes[0], block_exponents[0].T, routes[0].T, route_weight[0].T, out_grad[0])

    tie = lax.optimization_barrier
    shards_of = tie((home, shards_of))[1]
    own = load_call(shards_of[:1]) + load_call(shards_of[1:])
    weights = list(own) + other
    ahead, behind = peers // 2, peers // 2 - 1
    names = [("near", 0)]
    for k in range(1, ahead + 1):
        names += [("near", k), ("far", k)]
    names = names[: 2 * ahead]
    groups = [names[i : i + 4] for i in range(0, len(names) - 4, 4)]
    groups.append([name for name in names[-4:] if name[0] == "far"])
    groups.append([name for name in names[-4:] if name[0] == "near"])
    held = {("near", 0): home, ("far", 0): tie((home, own))[0]}
    partial, kept = {}, []

    def work(group):
        outs, saved = expert_call(
            [held[name] for name in group], weights, experts, local_experts
        )
        partial.update(zip(group, outs))
        kept.append(saved)

    for k in range(1, ahead + 1):
        held["near", k] = ring_shift(held["near", k - 1], 1)
        if k <= behind:
            held["far", k] = ring_shift(held["far", k - 1], -1)
        if k == 1:
            held["near", 1], own = tie((held["near", 1], own))
            weights[:3] = own
        if k % 2 == 1 and k > 1:
            work(groups[(k - 3) // 2])
            held["near", k], kept[-1] = tie((held["near", k], kept[-1]))
    work(groups[-2])
    far_sum = ring_shift(partial["far", behind], 1)
    held["near", ahead], kept[-1] = tie((held["near", ahead], kept[-1]))
    work(groups[-1])
    both = (slice(0, width), slice(width, 2 * width))
    near_sum = partial["near", ahead]
    own_total = received = None
    blocks = [held[name] for group in groups for name in group]
    steps = (1, -1)
    finals = []
    here, near_sum = tie((partial["near", 0], near_sum))
    for part, step in zip(both, steps):
        kept_here = add(home[:, part], here[:, part])
        finals.append([from_behind(kept_here, "section", step)])
    for k in range(ahead, 1, -1):
        near_sum = ring_shift(near_sum, -1)
        left = k - 2
        if left > 1:
            far_done = far_sum
            far_sum = ring_shift(add(far_sum, partial["far", left]), 1)
            near_sum, _ = tie((near_sum, far_done))
        if k == 3:
            own_total, other_total = weight_call(blocks, kept, width, peers)
            here = [final[0] for final in finals]
            near_sum, own_total, other_total, _ = tie((near_sum, own_total, other_total, here))
            lasts = [add(far_sum[:, part], partial["far", 1][:, part]) for part in both]
            for final, last, step in zip(finals, lasts, steps):
                final.append(ring_shift(last, 1, step))
            near_sum, _ = tie((near_sum, lasts))
            near_sum = add(near_sum, partial["near", 2])
        elif k == 2:
            here = [final[1] for final in finals]
            near_sum, other_total, _ = tie((near_sum, other_total, here))
            received = from_behind(other_total, "rep", 1)
        elif k > 2:
            near_sum = add(near_sum, partial["near", k - 1])
    joined = [slice(0, 2 * width)] if lax.axis_size("section") == 2 else both
    near_last = [
        ring_shift(add(near_sum[:, part], partial["near", 1][:, part]), -1, step)
        for part, step in zip(joined, steps)
    ]
    totals = [add(a, b) for a, b in zip(own_total, received)]
    near_last, totals = tie((near_last, totals))
    if len(near_last) == 1:
        near_last = [near_last[0][:, part] for part in both]
    results = [
        sum(f.astype(F32) for f in final + [last]).astype(BF16)[None]
        for final, last in zip(finals, near_last)
    ]
    shape = (1, local_experts, half_units, width)
    return tuple(results) + tuple(t.reshape(shape) for t in totals)


def solution(mesh):
    tokens = P("section", ("rep", "exp"), None)
    weights = P("section", "exp", "rep", None)
    return jax.shard_map(
        shards,
        mesh=mesh,
        in_specs=(tokens,) * 5 + (weights,) * 3,
        out_specs=(tokens,) * 2 + (weights,) * 3,
        check_vma=False,
    )
```

```python
import functools
import jax
import jax.numpy as jnp
from jax import lax
from jax.experimental import pallas as pl
from jax.experimental.pallas import tpu as pltpu
from jax.sharding import PartitionSpec as P

F32 = jnp.float32
BF16 = jnp.bfloat16


def vmem(peers):
    return (24 if peers <= 8 else 60) * 2**20


def ring_order(peers):
    width = 1
    while 8 * width * width <= peers:
        width *= 2
    depth = peers // width
    if width == 1 or depth % 2:
        return list(range(peers))
    order = [z * width for z in range(depth)]
    for back, z in enumerate(reversed(range(depth))):
        columns = list(range(1, width))
        order += [z * width + x for x in (columns if back % 2 == 0 else reversed(columns))]
    return order


def ring_shift(value, by, sections=0):
    peers, layers = lax.axis_size("exp"), lax.axis_size("section")
    order = ring_order(peers)
    pairs = []
    for rep in range(lax.axis_size("rep")):
        step = by if rep % 2 == 0 else -by
        for layer in range(layers):
            source = (rep * layers + layer) * peers
            target = (rep * layers + (layer + sections) % layers) * peers
            for spot in range(peers):
                pairs.append((source + order[spot], target + order[(spot + step) % peers]))
    return lax.ppermute(value, ("rep", "section", "exp"), pairs)


def from_behind(value, axis, by):
    peers = lax.axis_size(axis)
    return lax.ppermute(value, axis, [(i, (i + by) % peers) for i in range(peers)])


def dot(a, b, dims):
    return lax.dot_general(a, b, (dims, ((), ())), preferred_element_type=F32)


def whole():
    return pl.BlockSpec(memory_space=pltpu.VMEM)


def turned(value):
    rows, columns = value.shape
    wide = jnp.concatenate([value, jnp.zeros((rows, 128 - columns), F32)], axis=1)
    return wide.T[:columns]


def pack_kernel(experts, codes_ref, exps_ref, routes_ref, weight_ref, grad_ref, out_ref):
    tokens, width = codes_ref.shape
    blocks = exps_ref.shape[0]
    scales = jnp.exp2(exps_ref[...].astype(F32))
    scales = turned(jnp.concatenate([scales, jnp.zeros((128 - blocks, tokens), F32)], axis=0))
    per = width // blocks
    for b in range(blocks):
        cols = slice(b * per, (b + 1) * per)
        out_ref[:, cols] = (codes_ref[:, cols].astype(F32) * scales[:, b : b + 1]).astype(BF16)
    expert = lax.broadcasted_iota(jnp.int32, (experts, tokens), 0)
    table = jnp.zeros((experts, tokens), F32)
    for k in range(routes_ref.shape[0]):
        table += jnp.where(routes_ref[k : k + 1, :] == expert, weight_ref[k : k + 1, :], 0.0)
    high = table.astype(BF16).astype(F32)
    middle = (table - high).astype(BF16).astype(F32)
    low = table - high - middle
    out_ref[:, width : 2 * width] = grad_ref[...]
    extra = out_ref.shape[1] - 2 * width
    parts = [high, middle, low]
    if extra > 3 * experts:
        parts.append(jnp.zeros((extra - 3 * experts, tokens), F32))
    out_ref[:, 2 * width :] = turned(jnp.concatenate(parts, axis=0)).astype(BF16)


LAST = ((1,), (1,))
PLAIN = ((1,), (0,))
TILE = 256


def columns_of(width, body):
    def step(n, carry):
        body(n * TILE)
        return carry

    lax.fori_loop(0, width // TILE, step, 0, unroll=2)


def span(start):
    return pl.ds(pl.multiple_of(start, TILE), TILE)


def load_kernel(*refs):
    count = len(refs) // 2
    copies = [
        pltpu.make_async_copy(refs[i], refs[count + i], refs[-1].at[i]) for i in range(count)
    ]
    for copy in copies:
        copy.start()
    for copy in copies:
        copy.wait()


def load_call(weights):
    return pl.pallas_call(
        load_kernel,
        out_shape=[jax.ShapeDtypeStruct(w.shape, w.dtype) for w in weights],
        in_specs=[pl.BlockSpec(memory_space=pl.ANY)] * len(weights),
        out_specs=[whole()] * len(weights),
        scratch_shapes=[pltpu.SemaphoreType.DMA((len(weights),))],
        compiler_params=pltpu.CompilerParams(vmem_limit_bytes=8 * 2**20),
        cost_estimate=pl.CostEstimate(
            flops=0, bytes_accessed=sum(4 * w.size for w in weights), transcendentals=0
        ),
        name="load_weights",
    )(*weights)


def expert_kernel(count, experts, local_experts, *refs):
    blocks = refs[:count]
    weights = refs[count : count + 6]
    outs = refs[count + 6 : 2 * count + 6]
    saved = refs[2 * count + 6 : 2 * count + 9]
    rows, left = refs[2 * count + 9 :]
    half, width = weights[0].shape
    tokens = blocks[0].shape[0]
    tables = []
    for i, block in enumerate(blocks):
        rows[0, i * tokens : (i + 1) * tokens] = block[:, :width]
        rows[1, i * tokens : (i + 1) * tokens] = block[:, width : 2 * width]
        tables.append(block[:, 2 * width :].astype(F32))
    table = jnp.concatenate(tables, axis=0).T
    expert_of = lax.rem(lax.broadcasted_iota(jnp.int32, table.shape, 0), experts)
    first = lax.axis_index("exp") * local_experts
    scales = [
        jnp.sum(jnp.where(expert_of == first + e, table, 0.0), axis=0, keepdims=True)
        for e in range(local_experts)
    ]
    unit = lax.broadcasted_iota(jnp.int32, (half, 1), 0)
    scale = scales[0]
    for e in range(1, local_experts):
        scale = jnp.where(unit >= e * (half // local_experts), scales[e], scale)
    for side in range(2):
        at = slice(side * half, (side + 1) * half)
        gate = dot(weights[3 * side][...], rows[0], LAST)
        up = dot(weights[3 * side + 1][...], rows[0], LAST)
        back = dot(weights[3 * side + 2][...], rows[1], LAST) * scale
        sig = 1.0 / (1.0 + jnp.exp(-gate))
        swish = gate * sig
        results = (
            back * up * sig * (1.0 + gate * (1.0 - sig)),
            back * swish,
            swish * up * scale,
        )
        for kind, result in enumerate(results):
            result = result.astype(BF16)
            saved[kind][at, :] = result
            left[kind, :, at] = result.T

    def column(start):
        at, later = span(start), span(width + start)
        right = [
            jnp.concatenate([weights[kind][:, at], weights[3 + kind][:, at]], axis=0)
            for kind in range(3)
        ]
        output = dot(left[2], right[2], PLAIN).astype(BF16)
        grad = (dot(left[0], right[0], PLAIN) + dot(left[1], right[1], PLAIN)).astype(BF16)
        for i, out in enumerate(outs):
            out[:, at] = output[i * tokens : (i + 1) * tokens]
            out[:, later] = grad[i * tokens : (i + 1) * tokens]

    columns_of(width, column)


def expert_call(blocks, weights, experts, local_experts):
    count, tokens = len(blocks), blocks[0].shape[0]
    half, width = weights[0].shape
    units, rows = 2 * half, count * tokens
    results = pl.pallas_call(
        functools.partial(expert_kernel, count, experts, local_experts),
        out_shape=[jax.ShapeDtypeStruct((tokens, 2 * width), BF16)] * count
        + [jax.ShapeDtypeStruct((units, rows), BF16)] * 3,
        in_specs=[whole()] * (count + 6),
        out_specs=[whole()] * (count + 3),
        scratch_shapes=[
            pltpu.VMEM((2, rows, width), BF16),
            pltpu.VMEM((3, rows, units), BF16),
        ],
        compiler_params=pltpu.CompilerParams(vmem_limit_bytes=vmem(experts // local_experts)),
        cost_estimate=pl.CostEstimate(
            flops=6 * 2 * rows * units * width,
            bytes_accessed=6 * units * width + 8 * rows * width,
            transcendentals=rows * units,
        ),
        name="expert_rows",
    )(*blocks, *weights)
    return results[:count], results[count:]


def weight_kernel(groups, count, *refs):
    blocks = refs[:count]
    kept = [refs[count + g * 3 : count + g * 3 + 3] for g in range(groups)]
    outs, other, across = refs[-5:-2], refs[-2], refs[-1]
    half, width = outs[0].shape
    for kind in range(3):
        start = 0
        for group in kept:
            size = group[kind].shape[1]
            across[kind, :, start : start + size] = group[kind][...]
            start += size

    def column(start):
        at, later = span(start), span(width + start)
        right = [
            jnp.concatenate([b[:, at] for b in blocks], axis=0),
            jnp.concatenate([b[:, later] for b in blocks], axis=0),
        ]
        for kind in range(3):
            total = dot(across[kind], right[kind // 2], PLAIN).astype(BF16)
            outs[kind][:, at] = total[:half]
            other[kind, :, at] = total[half:]

    columns_of(width, column)


def weight_call(blocks, kept, width, peers):
    count = len(blocks)
    units = kept[0][0].shape[0]
    half, total = units // 2, count * blocks[0].shape[0]
    results = pl.pallas_call(
        functools.partial(weight_kernel, len(kept), count),
        out_shape=[jax.ShapeDtypeStruct((half, width), BF16)] * 3
        + [jax.ShapeDtypeStruct((3, half, width), BF16)],
        in_specs=[whole()] * (count + 3 * len(kept)),
        out_specs=[whole()] * 4,
        scratch_shapes=[pltpu.VMEM((3, units, total), BF16)],
        compiler_params=pltpu.CompilerParams(vmem_limit_bytes=vmem(peers)),
        cost_estimate=pl.CostEstimate(
            flops=3 * 2 * total * units * width,
            bytes_accessed=4 * total * width + 12 * half * width,
            transcendentals=0,
        ),
        name="weight_grads",
    )(*blocks, *[k for group in kept for k in group])
    return results[:3], results[3]


def add(a, b):
    return (a.astype(F32) + b.astype(F32)).astype(BF16)


def shards(
    row_codes, block_exponents, routes, route_weight, out_grad, gate_weight, up_weight, down_weight
):
    tokens, width = row_codes.shape[1:]
    local_experts, half_units = gate_weight.shape[1:3]
    half = local_experts * half_units
    peers = lax.axis_size("exp")
    experts = peers * local_experts
    lanes = -(-3 * experts // 128) * 128
    shards_of = [w.reshape(half, width) for w in (gate_weight, up_weight, down_weight)]
    other = [from_behind(w, "rep", 1) for w in shards_of]
    home = pl.pallas_call(
        functools.partial(pack_kernel, experts),
        out_shape=jax.ShapeDtypeStruct((tokens, 2 * width + lanes), BF16),
        in_specs=[whole()] * 5,
        out_specs=whole(),
        compiler_params=pltpu.CompilerParams(vmem_limit_bytes=60 * 2**20),
        name="pack_rows",
    )(row_codes[0], block_exponents[0].T, routes[0].T, route_weight[0].T, out_grad[0])

    tie = lax.optimization_barrier
    shards_of = tie((home, shards_of))[1]
    own = load_call(shards_of[:1]) + load_call(shards_of[1:])
    weights = list(own) + other
    ahead, behind = peers // 2, peers // 2 - 1
    names = [("near", 0)]
    for k in range(1, ahead + 1):
        names += [("near", k), ("far", k)]
    names = names[: 2 * ahead]
    groups = [names[i : i + 4] for i in range(0, len(names) - 4, 4)]
    groups.append([name for name in names[-4:] if name[0] == "far"])
    groups.append([name for name in names[-4:] if name[0] == "near"])
    held = {("near", 0): home, ("far", 0): tie((home, own))[0]}
    partial, kept = {}, []

    def work(group):
        outs, saved = expert_call(
            [held[name] for name in group], weights, experts, local_experts
        )
        partial.update(zip(group, outs))
        kept.append(saved)

    for k in range(1, ahead + 1):
        held["near", k] = ring_shift(held["near", k - 1], 1)
        if k <= behind:
            held["far", k] = ring_shift(held["far", k - 1], -1)
        if k == 1:
            held["near", 1], own = tie((held["near", 1], own))
            weights[:3] = own
        if k % 2 == 1 and k > 1:
            work(groups[(k - 3) // 2])
            held["near", k], kept[-1] = tie((held["near", k], kept[-1]))
            if k <= behind:
                held["far", k], kept[-1] = tie((held["far", k], kept[-1]))
    work(groups[-2])
    far_sum = ring_shift(partial["far", behind], 1)
    held["near", ahead], kept[-1] = tie((held["near", ahead], kept[-1]))
    work(groups[-1])
    both = (slice(0, width), slice(width, 2 * width))
    near_sum = partial["near", ahead]
    far_sum, _ = tie((far_sum, near_sum))
    own_total = received = None
    blocks = [held[name] for group in groups for name in group]
    steps = (1, -1)
    joined = [slice(0, 2 * width)] if lax.axis_size("section") == 2 else both
    finals = []
    here, near_sum = tie((partial["near", 0], near_sum))
    for part, step in zip(both, steps):
        kept_here = add(home[:, part], here[:, part])
        finals.append([from_behind(kept_here, "section", step)])
    for k in range(ahead, 1, -1):
        near_sum = ring_shift(near_sum, -1)
        left = k - 2
        if left > 1:
            far_done = far_sum
            far_sum = ring_shift(add(far_sum, partial["far", left]), 1)
            near_sum, _ = tie((near_sum, far_done))
        if k == 3:
            own_total, other_total = weight_call(blocks, kept, width, peers)
            here = [final[0] for final in finals]
            near_sum, own_total, other_total, _ = tie((near_sum, own_total, other_total, here))
            lasts = [add(far_sum[:, part], partial["far", 1][:, part]) for part in joined]
            far_last = [ring_shift(last, 1, step) for last, step in zip(lasts, steps)]
            near_sum, _ = tie((near_sum, lasts))
            near_sum = add(near_sum, partial["near", 2])
        elif k == 2:
            near_sum, other_total, far_last = tie((near_sum, other_total, far_last))
            received = from_behind(other_total, "rep", 1)
        elif k > 2:
            near_sum = add(near_sum, partial["near", k - 1])
    near_last = [
        ring_shift(add(near_sum[:, part], partial["near", 1][:, part]), -1, step)
        for part, step in zip(joined, steps)
    ]
    totals = [add(a, b) for a, b in zip(own_total, received)]
    near_last, totals = tie((near_last, totals))
    if len(near_last) == 1:
        near_last = [near_last[0][:, part] for part in both]
        far_last = [far_last[0][:, part] for part in both]
    results = [
        sum(f.astype(F32) for f in (final[0], far, last)).astype(BF16)[None]
        for final, far, last in zip(finals, far_last, near_last)
    ]
    shape = (1, local_experts, half_units, width)
    return tuple(results) + tuple(t.reshape(shape) for t in totals)


def solution(mesh):
    tokens = P("section", ("rep", "exp"), None)
    weights = P("section", "exp", "rep", None)
    return jax.shard_map(
        shards,
        mesh=mesh,
        in_specs=(tokens,) * 5 + (weights,) * 3,
        out_specs=(tokens,) * 2 + (weights,) * 3,
        check_vma=False,
    )
```
